512 devices in a mesh: gx: 32 (over y, x), gy: 16 (over z, core).
Axes of the slice: x: 4, y: 8, z: 8, core: 2. Of those that a mesh axis runs over, the one named last changes fastest.
Arguments:
- material: int32 [4, 256, 2048], P(None, 'gx', 'gy'), may hold values from 0 to 3
- face_open: int32 [3, 4, 256, 2048], P(None, None, 'gx', 'gy'), may hold values from 1 to 64
Outputs:
- first_level: float32 [27, 2, 128, 1024], P(None, None, 'gx', 'gy')
- second_level: float32 [27, 1, 64, 512], P(None, None, 'gx', 'gy')
The draws below stay inside these ranges and needn't reach their ends.
All inputs are finite; a program needn't handle non-finite values.
Results may differ from the reference program's by a relative error of at most 0.0003.
Values sent between devices are 32-bit elements; how exact they have to be, the bound alone decides.
No kernel may reach another device: no remote copies, remote signals or barrier semaphores. Data moves between devices by JAX's collectives and lax.ppermute only.
A program may use at most 64 MiB of HBM per device.

```python
from functools import partial
import jax
import jax.numpy as jnp
from jax import lax

NZ = 4
NX = 256
NY = 2048


def set_ends(result, key, smallest, high):
    longest = result.shape.index(max(result.shape))
    spots = []
    for shift in (0, 1):
        where = [jax.random.randint(jax.random.fold_in(key, axis), (), 0, length) for axis, length in enumerate(result.shape)]
        where[longest] = (where[longest] + shift) % result.shape[longest]
        spots.append(tuple(where))
    return result.at[spots[0]].set(smallest).at[spots[1]].set(high)


def setup_inputs(seed: int = 0) -> dict:
    keys = jax.random.split(jax.random.key(seed), 3)
    material = set_ends(jax.random.randint(keys[0], (NZ, NX, NY), 0, 4), jax.random.fold_in(keys[0], 1), 0, 3).astype(jnp.int32)
    face_open = set_ends(jax.random.randint(keys[1], (3, NZ, NX, NY), 1, 65), jax.random.fold_in(keys[1], 1), 1, 64).astype(jnp.int32)
    return {"material": material, "face_open": face_open}


permit_levels = (1.0 / 80.0, 4.0 / 80.0, 20.0 / 80.0, 1.0)


def permittivity(material):
    values = jnp.zeros(material.shape, jnp.float32)
    for material_id in range(4):
        values = values + jnp.where(material == material_id, permit_levels[material_id], 0.0)
    return values


def neighbour(values, direction, offset):
    extent = values.shape[direction]
    edge_shape = list(values.shape)
    edge_shape[direction] = 1
    zeros_edge = jnp.zeros(edge_shape, values.dtype)
    if offset > 0:
        return jnp.concatenate([lax.slice_in_dim(values, 1, extent, axis=direction), zeros_edge], axis=direction)
    return jnp.concatenate([zeros_edge, lax.slice_in_dim(values, 0, extent - 1, axis=direction)], axis=direction)


def parity_masks(positions):
    return ((positions[0] % 2 == 1)[:, None, None], (positions[1] % 2 == 1)[None, :, None], (positions[2] % 2 == 1)[None, None, :])


def local_pairs(couplings, positions):
    parities = parity_masks(positions)
    weight_pairs = []
    for direction in range(3):
        current = couplings[direction]
        before = neighbour(current, direction, -1)
        fraction = before / (before + current)
        weight_pairs.append((jnp.where(parities[direction], fraction, 1.0), jnp.where(parities[direction], 1.0 - fraction, 0.0)))
    return weight_pairs


def weight_products(weight_pairs):
    return [weight_pairs[0][corner // 4] * weight_pairs[1][corner // 2 % 2] * weight_pairs[2][corner % 2] for corner in range(8)]


def indicator(extent, offset, limit, target):
    coarse = jnp.arange(extent, dtype=jnp.int32) // 2 + offset
    inside = (coarse >= 0) & (coarse < limit)
    return (inside & (jnp.mod(coarse, 3) == target)).astype(jnp.float32)


def prolong(products, probe_id):
    grid_shape = products[0].shape
    targets = (probe_id // 9, probe_id // 3 % 3, probe_id % 3)
    summed = None
    for corner in range(8):
        corner_sides = (corner // 4, corner // 2 % 2, corner % 2)
        factors = [indicator(grid_shape[direction], corner_sides[direction], grid_shape[direction] // 2, targets[direction]) for direction in range(3)]
        contribution = products[corner] * (factors[0][:, None, None] * factors[1][None, :, None] * factors[2][None, None, :])
        summed = contribution if summed is None else summed + contribution
    return summed


def pool_pairs(values, direction):
    grid_shape = values.shape
    split_shape = grid_shape[:direction] + (grid_shape[direction] // 2, 2) + grid_shape[direction + 1:]
    return jnp.sum(values.reshape(split_shape), axis=direction + 1)


def restrict(products, residual):
    summed = None
    for corner in range(8):
        corner_sides = (corner // 4, corner // 2 % 2, corner % 2)
        pooled = residual * products[corner]
        for direction in range(3):
            pooled = pool_pairs(pooled, direction)
        for direction in range(3):
            if corner_sides[direction] == 1:
                pooled = neighbour(pooled, direction, -1)
        summed = pooled if summed is None else summed + pooled
    return summed


def select_offsets(values, coords):
    entries = []
    for offset in (-1, 0, 1):
        colour = jnp.mod(coords + offset, 3)
        entries.append(values[0] * (colour == 0) + values[1] * (colour == 1) + values[2] * (colour == 2))
    return jnp.stack(entries)


def extract(results, positions):
    grid_shape = results.shape[1:]
    selected = results.reshape((3, 3, 3) + grid_shape)
    selected = select_offsets(selected, positions[0][:, None, None])
    selected = jnp.moveaxis(select_offsets(jnp.moveaxis(selected, 1, 0), positions[1][:, None]), 0, 1)
    selected = jnp.moveaxis(select_offsets(jnp.moveaxis(selected, 2, 0), positions[2]), 0, 2)
    return selected.reshape((27,) + grid_shape)


def apply_fine(couplings, values):
    summed = jnp.zeros(values.shape, jnp.float32)
    for direction in range(3):
        current = couplings[direction]
        before = neighbour(current, direction, -1)
        summed = summed + current * (values - neighbour(values, direction, 1)) + before * (values - neighbour(values, direction, -1))
    return summed


def apply_stencil(coefficients, values):
    summed = jnp.zeros(values.shape, jnp.float32)
    for offset_id in range(27):
        shifted = values
        for direction, offset in enumerate((offset_id // 9 - 1, offset_id // 3 % 3 - 1, offset_id % 3 - 1)):
            if offset != 0:
                shifted = neighbour(shifted, direction, offset)
        summed = summed + coefficients[offset_id] * shifted
    return summed


def series(couplings):
    anchor = couplings[:, 0::2, 0::2, 0::2]
    further = (couplings[0, 1::2, 0::2, 0::2], couplings[1, 0::2, 1::2, 0::2], couplings[2, 0::2, 0::2, 1::2])
    return jnp.stack([anchor[direction] * further[direction] / (anchor[direction] + further[direction]) for direction in range(3)])


def coarse_level(couplings, operator):
    grid_shape = couplings.shape[1:]
    positions = tuple(jnp.arange(extent, dtype=jnp.int32) for extent in grid_shape)
    products = weight_products(local_pairs(couplings, positions))

    def probe(probe_id):
        return restrict(products, operator(prolong(products, probe_id)))

    results = lax.map(probe, jnp.arange(27, dtype=jnp.int32))
    coarse_positions = tuple(jnp.arange(extent // 2, dtype=jnp.int32) for extent in grid_shape)
    return extract(results, coarse_positions)


def reference(material, face_open):
    couplings = face_open.astype(jnp.float32) / 64.0 * permittivity(material)[None]
    first_level = coarse_level(couplings, partial(apply_fine, couplings))
    second_level = coarse_level(series(couplings), partial(apply_stencil, first_level))
    return first_level, second_level
```

```python
import functools

import jax
import jax.numpy as jnp
from jax import lax
from jax.experimental import pallas as pl
from jax.experimental.pallas import tpu as pltpu
from jax.sharding import PartitionSpec as P

permit_levels = (1.0 / 80.0, 4.0 / 80.0, 20.0 / 80.0, 1.0)

ROWS, LANES = 8, 128


def permittivity(material):
    values = jnp.zeros(material.shape, jnp.float32)
    for material_id in range(4):
        values = values + jnp.where(material == material_id, permit_levels[material_id], 0.0)
    return values


def shifted(values, by_x, by_y):
    if by_x:
        values = pltpu.roll(values, (-by_x) % ROWS, 0)
    if by_y:
        values = pltpu.roll(values, (-by_y) % LANES, 1)
    return values


def pick_lanes(values, index):
    return jnp.take_along_axis(values, index, axis=1)


def times(a, b):
    if a is None:
        return b
    if b is None:
        return a
    return a * b


def minus(a, b):
    return (1.0 if a is None else a) - (1.0 if b is None else b)


def line_terms(lower, upper):
    total = lower + upper
    inverse = 1.0 / jnp.where(total > 0.0, total, 1.0)
    f = lower * inverse
    g = upper * inverse
    return f, g, lower * g, lower * f, upper * g


def first_operator(c, last_x, last_y, rows, lanes):
    lines = {}
    for z in range(4):
        for p in range(2):
            lines[1, z, p] = line_terms(c[1][z][0][p], c[1][z][1][p])
            lines[2, z, p] = line_terms(c[2][z][p][0], c[2][z][p][1])
    for zc in range(2):
        for px in range(2):
            for py in range(2):
                lines[0, zc, px, py] = line_terms(c[0][2 * zc][px][py], c[0][2 * zc + 1][px][py])

    rolled = {}

    def fraction(dim, zc, node, raised):
        pz, px, py = node
        if raised == 0:
            zc, raised = zc + 1, None
        if dim == 0:
            key = (0, zc, px, py)
        elif dim == 1:
            key = (1, 2 * zc + pz, py)
        else:
            key = (2, 2 * zc + pz, px)
        if raised is None:
            return lines[key][:2]
        if (key, raised) not in rolled:
            f = shifted(lines[key][0], int(raised == 1), int(raised == 2))
            rolled[key, raised] = (f, 1.0 - f)
        return rolled[key, raised]

    def transverse(d, zc, node, raised):
        dims = [dim for dim in range(3) if dim != d]
        entries = {(0, 0, 0): None}
        for dim in dims:
            if not node[dim]:
                continue
            pair = fraction(dim, zc, node, raised)
            fresh = {}
            for corner, weight in entries.items():
                for side in range(2):
                    moved = list(corner)
                    moved[dim] = side
                    if dim == 0 and side == 1 and zc == 1:
                        continue
                    fresh[tuple(moved)] = times(weight, pair[side])
            entries = fresh
        return entries

    sums = {}

    def put(zc, low, high, value):
        offset = tuple(b - a for a, b in zip(low, high))
        if offset < (0, 0, 0):
            low, high = high, low
            offset = tuple(-o for o in offset)
        if zc + low[0] > 1 or zc + high[0] > 1:
            return
        key = (offset, zc + low[0], low[1], low[2])
        sums[key] = sums[key] + value if key in sums else value

    for d in range(3):
        dims = [dim for dim in range(3) if dim != d]
        for zc in range(2):
            top = d == 0 and zc == 1
            for q1 in range(2):
                for q2 in range(2):
                    node = [0, 0, 0]
                    node[dims[0]], node[dims[1]] = q1, q2
                    odd = list(node)
                    odd[d] = 1
                    if d == 0:
                        key = (0, zc, node[1], node[2])
                    elif d == 1:
                        key = (1, 2 * zc + node[0], node[2])
                    else:
                        key = (2, 2 * zc + node[0], node[1])
                    _, _, s, h, k = lines[key]

                    def raised_corner(corner):
                        moved = list(corner)
                        moved[d] = 1
                        return tuple(moved)

                    zero = (0, 0, 0)
                    if not (q1 or q2):
                        put(zc, zero, zero, s)
                        if not top:
                            up = raised_corner(zero)
                            put(zc, up, up, s)
                            put(zc, zero, up, -s)
                        continue
                    alpha = transverse(d, zc, node, None)
                    beta = transverse(d, zc, odd, None)
                    corners = list(alpha)
                    delta = {t: minus(alpha[t], beta[t]) for t in corners}
                    for i, t in enumerate(corners):
                        s_alpha, h_delta = s * alpha[t], h * delta[t]
                        for u in corners[i:]:
                            put(zc, t, u, s_alpha * alpha[u] + h_delta * delta[u])
                    if top:
                        continue
                    gamma = transverse(d, zc, node, d)
                    epsilon = {t: minus(gamma[t], beta[t]) for t in corners}
                    for i, t in enumerate(corners):
                        s_gamma, k_epsilon = s * gamma[t], k * epsilon[t]
                        for u in corners[i:]:
                            put(zc, raised_corner(t), raised_corner(u), s_gamma * gamma[u] + k_epsilon * epsilon[u])
                    for t in corners:
                        s_delta, s_alpha = s * delta[t], s * alpha[t]
                        for u in corners:
                            put(zc, t, raised_corner(u), s_delta * epsilon[u] - s_alpha * gamma[u])

    drop_x = (rows == ROWS // 2 - 1) & last_x
    drop_y = (lanes == LANES // 2 - 1) & last_y

    def inside(values, offset):
        if offset[1] == 1 and offset[2] == 1:
            return jnp.where(drop_x | drop_y, 0.0, values)
        if offset[1] == 1:
            return jnp.where(drop_x, 0.0, values)
        if offset[2] == 1:
            return jnp.where(drop_y, 0.0, values)
        return values

    operator = {}
    keys = sorted({(offset, z) for offset, z, _, _ in sums})
    for offset, z in keys:
        total = None
        for ax in range(2):
            part = sums.get((offset, z, ax, 0))
            side = sums.get((offset, z, ax, 1))
            if side is not None:
                side = shifted(side, 0, -1)
                part = side if part is None else part + side
            if part is None:
                continue
            part = shifted(part, -ax, 0)
            total = part if total is None else total + part
        operator[offset, z] = inside(total, offset)
        if offset != (0, 0, 0):
            mirror = tuple(-o for o in offset)
            operator[mirror, z + offset[0]] = inside(shifted(total, -offset[1], -offset[2]), mirror)

    chain = [
        [lines[0, z, 0, 0][2] for z in range(2)],
        [lines[1, 2 * z, 0][2] for z in range(2)],
        [lines[2, 2 * z, 0][2] for z in range(2)],
    ]
    return operator, chain


def second_operator(operator, chain, last_x, last_y, rows, lanes):
    odd = {1: rows % 2 == 1, 2: lanes % 2 == 1}
    depth = line_terms(chain[0][0], chain[0][1])[0]
    down, up = {}, {}
    for d in (1, 2):
        for z in range(2):
            here = chain[d][z]
            before = shifted(here, -int(d == 1), -int(d == 2))
            f, g = line_terms(before, here)[:2]
            down[d, z] = jnp.where(odd[d], f, 1.0)
            up[d, z] = jnp.where(odd[d], g, 1.0)
    down_z = {0: down[1, 0], 1: down[1, 1] * depth}
    up_z = {0: up[1, 0], 1: up[1, 1] * depth}

    reaches = ((-1, -1), (0, -1), (0, 0), (0, 1), (1, 0), (1, 1))

    def factors(d, lower, upper):
        base = {}
        for j, o in reaches:
            source = lower if (j, o) in ((-1, -1), (0, 0), (0, 1)) else upper
            source = shifted(source, o if d == 1 else 0, o if d == 2 else 0)
            if (j, o) == (0, 1):
                source = jnp.where(odd[d], 0.0, source)
            if (j, o) == (1, 0):
                source = jnp.where(odd[d], source, 0.0)
            base[j, o] = source
        return {
            (j, o, across): shifted(base[j, o], 0 if d == 1 else across, across if d == 1 else 0)
            for j, o in reaches
            for across in (-1, 0, 1)
        }

    spread = {}
    for far in range(2):
        along_x = factors(1, down_z[far], up_z[far])
        along_y = factors(2, down[2, far], up[2, far])
        for jx, ox in reaches:
            for jy, oy in reaches:
                weight = along_x[jx, ox, oy] * along_y[jy, oy, ox]
                for z in range(2):
                    term = operator[(far - z, ox, oy), z] * weight
                    key = (z, jx, jy)
                    spread[key] = spread[key] + term if key in spread else term

    sides = {
        (z, d): {-1: up_z[z] if d == 1 else up[2, z], 0: depth if (d == 1 and z == 1) else None, 1: down_z[z] if d == 1 else down[2, z]}
        for z in range(2)
        for d in (1, 2)
    }
    own = {(z, mx, my): times(sides[z, 1][mx], sides[z, 2][my]) for z in range(2) for mx in (-1, 0, 1) for my in (-1, 0, 1)}

    def taken(offset):
        return [(m, offset + 1 if m == -1 else offset) for m in (-1, 0, 1) if m * offset != -1]

    drop_x = (rows == ROWS // 2 - 2) & last_x
    drop_y = (lanes == LANES // 2 - 2) & last_y
    results = {}
    for ox in (-1, 0, 1):
        for oy in (-1, 0, 1):
            total = None
            for my, jy in taken(oy):
                part = None
                for mx, jx in taken(ox):
                    term = times(own[0, mx, my], spread[0, jx, jy]) + times(own[1, mx, my], spread[1, jx, jy])
                    term = shifted(term, mx, 0)
                    part = term if part is None else part + term
                part = shifted(part, 0, my)
                total = part if total is None else total + part
            if ox == 1:
                total = jnp.where(drop_x, 0.0, total)
            if oy == 1:
                total = jnp.where(drop_y, 0.0, total)
            results[ox, oy] = total
    return results


def couplings_kernel(eps_ref, face_ref, own_ref, far_ref, near_ref):
    odd_x = lax.axis_index("gx") % 2 == 1
    for r in range(12):
        values = face_ref[r // 4, r % 4].astype(jnp.float32) / 64.0 * eps_ref[r % 4]
        own_ref[r] = values
        far_ref[r] = jnp.where(odd_x, values[4:8, :], values[0:4, :])
        near_ref[r] = jnp.where(odd_x, values[0:4, :], values[4:8, :])


def gather_kernel(own_ref, far_rows_ref, near_rows_ref, rows_ref, far_ref, near_ref, block):
    odd_x = lax.axis_index("gx") % 2 == 1
    odd_y = lax.axis_index("gy") % 2 == 1
    lanes = lax.broadcasted_iota(jnp.int32, (ROWS, LANES), 1)
    low = jnp.zeros((ROWS, LANES), jnp.float32)
    high = jnp.zeros((ROWS, LANES), jnp.float32)
    for r in range(12):
        block[r, 0:8, :] = own_ref[r]
        block[r, 8:12, :] = jnp.where(odd_x, far_rows_ref[r], near_rows_ref[r])
        block[r, 12:16, :] = jnp.where(odd_x, near_rows_ref[r], far_rows_ref[r])
        for px in range(2):
            k = 2 * r + px
            values = block[r, pl.ds(px, 8, stride=2), :]
            rows_ref[k] = values
            turned = pltpu.roll(values, (4 * k + 4) % LANES, 1)
            low = jnp.where((lanes >= 4 * k) & (lanes < 4 * k + 4), turned, low)
            high = jnp.where(lanes == 4 * k + 4, turned, high)
    far_ref[...] = jnp.where(odd_y, low, high)
    near_ref[...] = jnp.where(odd_y, high, low)


def operator_kernel(rows_ref, far_ref, near_ref, first_ref, second_ref):
    rows = lax.broadcasted_iota(jnp.int32, (ROWS, LANES), 0)
    lanes = lax.broadcasted_iota(jnp.int32, (ROWS, LANES), 1)
    last_x = lax.axis_index("gx") == lax.axis_size("gx") - 1
    last_y = lax.axis_index("gy") == lax.axis_size("gy") - 1

    odd_y = lax.axis_index("gy") % 2 == 1
    left = jnp.where(odd_y, near_ref[...], far_ref[...])
    right = jnp.where(odd_y, far_ref[...], near_ref[...])
    source = ((lanes + 2) % LANES // 2 * 4 + 2 * (lanes % 2)) % LANES
    above = pick_lanes(right, (2 * lanes + 4) % LANES)
    edge_even = jnp.where((lanes >= 64) & (lanes < 112), above, pick_lanes(left, source))
    edge_odd = pick_lanes(left, (source + 1) % LANES)
    at_even = (lanes >= 126) | (lanes == 64)
    at_odd = lanes >= 126
    even_lanes = (2 * lanes) % LANES
    odd_lanes = (2 * lanes + 1) % LANES

    c = [[[[None, None], [None, None]] for _ in range(4)] for _ in range(3)]
    for d in range(3):
        for z in range(4):
            for px in range(2):
                k = (d * 4 + z) * 2 + px
                values = rows_ref[k]
                c[d][z][px][0] = jnp.where(at_even, shifted(edge_even, 0, 2 * k), pick_lanes(values, even_lanes))
                c[d][z][px][1] = jnp.where(at_odd, shifted(edge_odd, 0, 2 * k), pick_lanes(values, odd_lanes))

    operator, chain = first_operator(c, last_x, last_y, rows, lanes)
    empty = jnp.zeros((ROWS, LANES), jnp.float32)
    full = {}
    for o in range(27):
        offset = (o // 9 - 1, o // 3 % 3 - 1, o % 3 - 1)
        for z in range(2):
            values = operator.get((offset, z), empty)
            full[offset, z] = values
            first_ref[o, z] = values[0:4, 0:64]

    results = second_operator(full, chain, last_x, last_y, rows, lanes)
    second_ref[...] = jnp.zeros(second_ref.shape, jnp.float32)
    for (ox, oy), values in results.items():
        o = 9 + (ox + 1) * 3 + oy + 1
        compact = pick_lanes(values, even_lanes)
        second_ref[o, 0, 0:1, :] = compact[0:1, 0:32]
        second_ref[o, 0, 1:2, :] = compact[2:3, 0:32]


def swapped(values, axis, first):
    pairs = [(i, i + 1) for i in range(first, lax.axis_size(axis) - 1, 2)]
    return lax.ppermute(values, axis, pairs + [(b, a) for a, b in pairs])


def body(material, face_open):
    whole = pl.BlockSpec(memory_space=pltpu.VMEM)
    page = jax.ShapeDtypeStruct((ROWS, LANES), jnp.float32)
    edge = jax.ShapeDtypeStruct((12, 4, LANES), jnp.float32)
    small = pltpu.CompilerParams(vmem_limit_bytes=1 << 20)
    own, far, near = pl.pallas_call(
        couplings_kernel,
        out_shape=(jax.ShapeDtypeStruct((12, ROWS, LANES), jnp.float32), edge, edge),
        in_specs=[whole] * 2,
        out_specs=(whole,) * 3,
        compiler_params=small,
        name="couplings",
    )(permittivity(material), face_open)
    far_rows = swapped(far, "gx", 1)
    near_rows = swapped(near, "gx", 0)
    rows, far, near = pl.pallas_call(
        gather_kernel,
        out_shape=(jax.ShapeDtypeStruct((24, ROWS, LANES), jnp.float32), page, page),
        in_specs=[whole] * 3,
        out_specs=(whole,) * 3,
        scratch_shapes=[pltpu.VMEM((12, 16, LANES), jnp.float32)],
        compiler_params=small,
        name="gather_rows",
    )(own, far_rows, near_rows)
    far_columns = swapped(far, "gy", 1)
    near_columns = swapped(near, "gy", 0)
    return pl.pallas_call(
        operator_kernel,
        out_shape=(
            jax.ShapeDtypeStruct((27, 2, 4, 64), jnp.float32),
            jax.ShapeDtypeStruct((27, 1, 2, 32), jnp.float32),
        ),
        in_specs=[whole] * 3,
        out_specs=(whole,) * 2,
        compiler_params=pltpu.CompilerParams(vmem_limit_bytes=2 << 20),
        name="operators",
    )(rows, far_columns, near_columns)


def solution(mesh):
    placed = (P(None, "gx", "gy"), P(None, None, "gx", "gy"))
    return jax.shard_map(
        body,
        mesh=mesh,
        in_specs=placed,
        out_specs=(P(None, None, "gx", "gy"), P(None, None, "gx", "gy")),
        check_vma=False,
    )
```

```python
import functools

import jax
import jax.numpy as jnp
from jax import lax
from jax.experimental import pallas as pl
from jax.experimental.pallas import tpu as pltpu
from jax.sharding import PartitionSpec as P

permit_levels = (1.0 / 80.0, 4.0 / 80.0, 20.0 / 80.0, 1.0)

ROWS, LANES = 8, 128


def permittivity(material):
    values = jnp.zeros(material.shape, jnp.float32)
    for material_id in range(4):
        values = values + jnp.where(material == material_id, permit_levels[material_id], 0.0)
    return values


def shifted(values, by_x, by_y):
    if by_x:
        values = pltpu.roll(values, (-by_x) % ROWS, 0)
    if by_y:
        values = pltpu.roll(values, (-by_y) % LANES, 1)
    return values


def pick_lanes(values, index):
    return jnp.take_along_axis(values, index, axis=1)


def times(a, b):
    if a is None:
        return b
    if b is None:
        return a
    return a * b


def minus(a, b):
    return (1.0 if a is None else a) - (1.0 if b is None else b)


def line_terms(lower, upper):
    total = lower + upper
    inverse = 1.0 / jnp.where(total > 0.0, total, 1.0)
    f = lower * inverse
    g = upper * inverse
    return f, g, lower * g, lower * f, upper * g


def first_operator(c, last_x, last_y, rows, lanes):
    lines = {}
    for z in range(4):
        for p in range(2):
            lines[1, z, p] = line_terms(c[1][z][0][p], c[1][z][1][p])
            lines[2, z, p] = line_terms(c[2][z][p][0], c[2][z][p][1])
    for zc in range(2):
        for px in range(2):
            for py in range(2):
                lines[0, zc, px, py] = line_terms(c[0][2 * zc][px][py], c[0][2 * zc + 1][px][py])

    rolled = {}

    def fraction(dim, zc, node, raised):
        pz, px, py = node
        if raised == 0:
            zc, raised = zc + 1, None
        if dim == 0:
            key = (0, zc, px, py)
        elif dim == 1:
            key = (1, 2 * zc + pz, py)
        else:
            key = (2, 2 * zc + pz, px)
        if raised is None:
            return lines[key][:2]
        if (key, raised) not in rolled:
            f = shifted(lines[key][0], int(raised == 1), int(raised == 2))
            rolled[key, raised] = (f, 1.0 - f)
        return rolled[key, raised]

    def transverse(d, zc, node, raised):
        dims = [dim for dim in range(3) if dim != d]
        entries = {(0, 0, 0): None}
        for dim in dims:
            if not node[dim]:
                continue
            pair = fraction(dim, zc, node, raised)
            fresh = {}
            for corner, weight in entries.items():
                for side in range(2):
                    moved = list(corner)
                    moved[dim] = side
                    if dim == 0 and side == 1 and zc == 1:
                        continue
                    fresh[tuple(moved)] = times(weight, pair[side])
            entries = fresh
        return entries

    sums = {}

    def put(zc, low, high, value):
        offset = tuple(b - a for a, b in zip(low, high))
        if offset < (0, 0, 0):
            low, high = high, low
            offset = tuple(-o for o in offset)
        if zc + low[0] > 1 or zc + high[0] > 1:
            return
        key = (offset, zc + low[0], low[1], low[2])
        sums[key] = sums[key] + value if key in sums else value

    for d in range(3):
        dims = [dim for dim in range(3) if dim != d]
        for zc in range(2):
            top = d == 0 and zc == 1
            for q1 in range(2):
                for q2 in range(2):
                    node = [0, 0, 0]
                    node[dims[0]], node[dims[1]] = q1, q2
                    odd = list(node)
                    odd[d] = 1
                    if d == 0:
                        key = (0, zc, node[1], node[2])
                    elif d == 1:
                        key = (1, 2 * zc + node[0], node[2])
                    else:
                        key = (2, 2 * zc + node[0], node[1])
                    _, _, s, h, k = lines[key]

                    def raised_corner(corner):
                        moved = list(corner)
                        moved[d] = 1
                        return tuple(moved)

                    zero = (0, 0, 0)
                    if not (q1 or q2):
                        put(zc, zero, zero, s)
                        if not top:
                            up = raised_corner(zero)
                            put(zc, up, up, s)
                            put(zc, zero, up, -s)
                        continue
                    alpha = transverse(d, zc, node, None)
                    beta = transverse(d, zc, odd, None)
                    corners = list(alpha)
                    delta = {t: minus(alpha[t], beta[t]) for t in corners}
                    for i, t in enumerate(corners):
                        s_alpha, h_delta = s * alpha[t], h * delta[t]
                        for u in corners[i:]:
                            put(zc, t, u, s_alpha * alpha[u] + h_delta * delta[u])
                    if top:
                        continue
                    gamma = transverse(d, zc, node, d)
                    epsilon = {t: minus(gamma[t], beta[t]) for t in corners}
                    for i, t in enumerate(corners):
                        s_gamma, k_epsilon = s * gamma[t], k * epsilon[t]
                        for u in corners[i:]:
                            put(zc, raised_corner(t), raised_corner(u), s_gamma * gamma[u] + k_epsilon * epsilon[u])
                    for t in corners:
                        s_delta, s_alpha = s * delta[t], s * alpha[t]
                        for u in corners:
                            put(zc, t, raised_corner(u), s_delta * epsilon[u] - s_alpha * gamma[u])

    drop_x = (rows == ROWS // 2 - 1) & last_x
    drop_y = (lanes == LANES // 2 - 1) & last_y

    def inside(values, offset):
        if offset[1] == 1 and offset[2] == 1:
            return jnp.where(drop_x | drop_y, 0.0, values)
        if offset[1] == 1:
            return jnp.where(drop_x, 0.0, values)
        if offset[2] == 1:
            return jnp.where(drop_y, 0.0, values)
        return values

    operator = {}
    keys = sorted({(offset, z) for offset, z, _, _ in sums})
    for offset, z in keys:
        total = None
        for ax in range(2):
            part = sums.get((offset, z, ax, 0))
            side = sums.get((offset, z, ax, 1))
            if side is not None:
                side = shifted(side, 0, -1)
                part = side if part is None else part + side
            if part is None:
                continue
            part = shifted(part, -ax, 0)
            total = part if total is None else total + part
        operator[offset, z] = inside(total, offset)
        if offset != (0, 0, 0):
            mirror = tuple(-o for o in offset)
            operator[mirror, z + offset[0]] = inside(shifted(total, -offset[1], -offset[2]), mirror)

    chain = [
        [lines[0, z, 0, 0][2] for z in range(2)],
        [lines[1, 2 * z, 0][2] for z in range(2)],
        [lines[2, 2 * z, 0][2] for z in range(2)],
    ]
    return operator, chain


def second_operator(operator, chain, last_x, last_y, rows, lanes):
    odd = {1: rows % 2 == 1, 2: lanes % 2 == 1}
    depth = line_terms(chain[0][0], chain[0][1])[0]
    down, up = {}, {}
    for d in (1, 2):
        for z in range(2):
            here = chain[d][z]
            before = shifted(here, -int(d == 1), -int(d == 2))
            f, g = line_terms(before, here)[:2]
            down[d, z] = jnp.where(odd[d], f, 1.0)
            up[d, z] = jnp.where(odd[d], g, 1.0)
    down_z = {0: down[1, 0], 1: down[1, 1] * depth}
    up_z = {0: up[1, 0], 1: up[1, 1] * depth}

    reaches = ((-1, -1), (0, -1), (0, 0), (0, 1), (1, 0), (1, 1))

    def factors(d, lower, upper):
        base = {}
        for j, o in reaches:
            source = lower if (j, o) in ((-1, -1), (0, 0), (0, 1)) else upper
            source = shifted(source, o if d == 1 else 0, o if d == 2 else 0)
            if (j, o) == (0, 1):
                source = jnp.where(odd[d], 0.0, source)
            if (j, o) == (1, 0):
                source = jnp.where(odd[d], source, 0.0)
            base[j, o] = source
        return {
            (j, o, across): shifted(base[j, o], 0 if d == 1 else across, across if d == 1 else 0)
            for j, o in reaches
            for across in (-1, 0, 1)
        }

    spread = {}
    for far in range(2):
        along_x = factors(1, down_z[far], up_z[far])
        along_y = factors(2, down[2, far], up[2, far])
        for jx, ox in reaches:
            for jy, oy in reaches:
                weight = along_x[jx, ox, oy] * along_y[jy, oy, ox]
                for z in range(2):
                    term = operator[(far - z, ox, oy), z] * weight
                    key = (z, jx, jy)
                    spread[key] = spread[key] + term if key in spread else term

    sides = {
        (z, d): {-1: up_z[z] if d == 1 else up[2, z], 0: depth if (d == 1 and z == 1) else None, 1: down_z[z] if d == 1 else down[2, z]}
        for z in range(2)
        for d in (1, 2)
    }
    own = {(z, mx, my): times(sides[z, 1][mx], sides[z, 2][my]) for z in range(2) for mx in (-1, 0, 1) for my in (-1, 0, 1)}

    def taken(offset):
        return [(m, offset + 1 if m == -1 else offset) for m in (-1, 0, 1) if m * offset != -1]

    drop_x = (rows == ROWS // 2 - 2) & last_x
    drop_y = (lanes == LANES // 2 - 2) & last_y
    results = {}
    for ox in (-1, 0, 1):
        for oy in (-1, 0, 1):
            total = None
            for my, jy in taken(oy):
                part = None
                for mx, jx in taken(ox):
                    term = times(own[0, mx, my], spread[0, jx, jy]) + times(own[1, mx, my], spread[1, jx, jy])
                    term = shifted(term, mx, 0)
                    part = term if part is None else part + term
                part = shifted(part, 0, my)
                total = part if total is None else total + part
            if ox == 1:
                total = jnp.where(drop_x, 0.0, total)
            if oy == 1:
                total = jnp.where(drop_y, 0.0, total)
            results[ox, oy] = total
    return results


def couplings_kernel(inputs_ref, own_ref, far_ref, near_ref):
    odd_x = lax.axis_index("gx") % 2 == 1
    eps = [permittivity(inputs_ref[0, z] & 3) for z in range(4)]
    for r in range(12):
        values = (inputs_ref[r // 4, r % 4] >> 2).astype(jnp.float32) / 64.0 * eps[r % 4]
        own_ref[r] = values
        far_ref[r] = jnp.where(odd_x, values[4:8, :], values[0:4, :])
        near_ref[r] = jnp.where(odd_x, values[0:4, :], values[4:8, :])


def gather_kernel(own_ref, far_rows_ref, near_rows_ref, rows_ref, far_ref, near_ref, block):
    odd_x = lax.axis_index("gx") % 2 == 1
    odd_y = lax.axis_index("gy") % 2 == 1
    lanes = lax.broadcasted_iota(jnp.int32, (ROWS, LANES), 1)
    low = jnp.zeros((ROWS, LANES), jnp.float32)
    high = jnp.zeros((ROWS, LANES), jnp.float32)
    for r in range(12):
        block[r, 0:8, :] = own_ref[r]
        block[r, 8:12, :] = jnp.where(odd_x, far_rows_ref[r], near_rows_ref[r])
        block[r, 12:16, :] = jnp.where(odd_x, near_rows_ref[r], far_rows_ref[r])
        for px in range(2):
            k = 2 * r + px
            values = block[r, pl.ds(px, 8, stride=2), :]
            rows_ref[k] = values
            turned = pltpu.roll(values, (4 * k + 4) % LANES, 1)
            low = jnp.where((lanes >= 4 * k) & (lanes < 4 * k + 4), turned, low)
            high = jnp.where(lanes == 4 * k + 4, turned, high)
    far_ref[...] = jnp.where(odd_y, low, high)
    near_ref[...] = jnp.where(odd_y, high, low)


def operator_kernel(rows_ref, far_ref, near_ref, first_ref, second_ref):
    rows = lax.broadcasted_iota(jnp.int32, (ROWS, LANES), 0)
    lanes = lax.broadcasted_iota(jnp.int32, (ROWS, LANES), 1)
    last_x = lax.axis_index("gx") == lax.axis_size("gx") - 1
    last_y = lax.axis_index("gy") == lax.axis_size("gy") - 1

    odd_y = lax.axis_index("gy") % 2 == 1
    left = jnp.where(odd_y, near_ref[...], far_ref[...])
    right = jnp.where(odd_y, far_ref[...], near_ref[...])
    source = ((lanes + 2) % LANES // 2 * 4 + 2 * (lanes % 2)) % LANES
    above = pick_lanes(right, (2 * lanes + 4) % LANES)
    edge_even = jnp.where((lanes >= 64) & (lanes < 112), above, pick_lanes(left, source))
    edge_odd = pick_lanes(left, (source + 1) % LANES)
    at_even = (lanes >= 126) | (lanes == 64)
    at_odd = lanes >= 126
    even_lanes = (2 * lanes) % LANES
    odd_lanes = (2 * lanes + 1) % LANES

    c = [[[[None, None], [None, None]] for _ in range(4)] for _ in range(3)]
    for d in range(3):
        for z in range(4):
            for px in range(2):
                k = (d * 4 + z) * 2 + px
                values = rows_ref[k]
                c[d][z][px][0] = jnp.where(at_even, shifted(edge_even, 0, 2 * k), pick_lanes(values, even_lanes))
                c[d][z][px][1] = jnp.where(at_odd, shifted(edge_odd, 0, 2 * k), pick_lanes(values, odd_lanes))

    operator, chain = first_operator(c, last_x, last_y, rows, lanes)
    empty = jnp.zeros((ROWS, LANES), jnp.float32)
    full = {}
    for o in range(27):
        offset = (o // 9 - 1, o // 3 % 3 - 1, o % 3 - 1)
        for z in range(2):
            values = operator.get((offset, z), empty)
            full[offset, z] = values
            first_ref[o, z] = values[0:4, 0:64]

    results = second_operator(full, chain, last_x, last_y, rows, lanes)
    second_ref[...] = jnp.zeros(second_ref.shape, jnp.float32)
    for (ox, oy), values in results.items():
        o = 9 + (ox + 1) * 3 + oy + 1
        compact = pick_lanes(values, even_lanes)
        second_ref[o, 0, 0:1, :] = compact[0:1, 0:32]
        second_ref[o, 0, 1:2, :] = compact[2:3, 0:32]


def swapped(values, axis, first):
    pairs = [(i, i + 1) for i in range(first, lax.axis_size(axis) - 1, 2)]
    return lax.ppermute(values, axis, pairs + [(b, a) for a, b in pairs])


def body(material, face_open):
    whole = pl.BlockSpec(memory_space=pltpu.VMEM)
    page = jax.ShapeDtypeStruct((ROWS, LANES), jnp.float32)
    edge = jax.ShapeDtypeStruct((12, 4, LANES), jnp.float32)
    small = pltpu.CompilerParams(vmem_limit_bytes=1 << 20)
    own, far, near = pl.pallas_call(
        couplings_kernel,
        out_shape=(jax.ShapeDtypeStruct((12, ROWS, LANES), jnp.float32), edge, edge),
        in_specs=[whole],
        out_specs=(whole,) * 3,
        compiler_params=small,
        name="couplings",
    )(face_open * 4 + material[None])
    far_rows = swapped(far, "gx", 1)
    near_rows = swapped(near, "gx", 0)
    rows, far, near = pl.pallas_call(
        gather_kernel,
        out_shape=(jax.ShapeDtypeStruct((24, ROWS, LANES), jnp.float32), page, page),
        in_specs=[whole] * 3,
        out_specs=(whole,) * 3,
        scratch_shapes=[pltpu.VMEM((12, 16, LANES), jnp.float32)],
        compiler_params=small,
        name="gather_rows",
    )(own, far_rows, near_rows)
    far_columns = swapped(far, "gy", 1)
    near_columns = swapped(near, "gy", 0)
    return pl.pallas_call(
        operator_kernel,
        out_shape=(
            jax.ShapeDtypeStruct((27, 2, 4, 64), jnp.float32),
            jax.ShapeDtypeStruct((27, 1, 2, 32), jnp.float32),
        ),
        in_specs=[whole] * 3,
        out_specs=(whole,) * 2,
        compiler_params=pltpu.CompilerParams(vmem_limit_bytes=2 << 20),
        name="operators",
    )(rows, far_columns, near_columns)


def solution(mesh):
    placed = (P(None, "gx", "gy"), P(None, None, "gx", "gy"))
    return jax.shard_map(
        body,
        mesh=mesh,
        in_specs=placed,
        out_specs=(P(None, None, "gx", "gy"), P(None, None, "gx", "gy")),
        check_vma=False,
    )
```

```python
import functools

import jax
import jax.numpy as jnp
from jax import lax
from jax.experimental import pallas as pl
from jax.experimental.pallas import tpu as pltpu
from jax.sharding import PartitionSpec as P

permit_levels = (1.0 / 80.0, 4.0 / 80.0, 20.0 / 80.0, 1.0)

ROWS, LANES = 8, 128


def permittivity(material):
    values = jnp.zeros(material.shape, jnp.float32)
    for material_id in range(4):
        values = values + jnp.where(material == material_id, permit_levels[material_id], 0.0)
    return values


def shifted(values, by_x, by_y):
    if by_x:
        values = pltpu.roll(values, (-by_x) % ROWS, 0)
    if by_y:
        values = pltpu.roll(values, (-by_y) % LANES, 1)
    return values


def pick_lanes(values, index):
    return jnp.take_along_axis(values, index, axis=1)


def times(a, b):
    if a is None:
        return b
    if b is None:
        return a
    return a * b


def minus(a, b):
    return (1.0 if a is None else a) - (1.0 if b is None else b)


def line_terms(lower, upper):
    total = lower + upper
    inverse = 1.0 / jnp.where(total > 0.0, total, 1.0)
    f = lower * inverse
    g = upper * inverse
    return f, g, lower * g, lower * f, upper * g


def first_operator(c, last_x, last_y, rows, lanes):
    lines = {}
    for z in range(4):
        for p in range(2):
            lines[1, z, p] = line_terms(c[1][z][0][p], c[1][z][1][p])
            lines[2, z, p] = line_terms(c[2][z][p][0], c[2][z][p][1])
    for zc in range(2):
        for px in range(2):
            for py in range(2):
                lines[0, zc, px, py] = line_terms(c[0][2 * zc][px][py], c[0][2 * zc + 1][px][py])

    rolled = {}

    def fraction(dim, zc, node, raised):
        pz, px, py = node
        if raised == 0:
            zc, raised = zc + 1, None
        if dim == 0:
            key = (0, zc, px, py)
        elif dim == 1:
            key = (1, 2 * zc + pz, py)
        else:
            key = (2, 2 * zc + pz, px)
        if raised is None:
            return lines[key][:2]
        if (key, raised) not in rolled:
            f = shifted(lines[key][0], int(raised == 1), int(raised == 2))
            rolled[key, raised] = (f, 1.0 - f)
        return rolled[key, raised]

    def transverse(d, zc, node, raised):
        dims = [dim for dim in range(3) if dim != d]
        entries = {(0, 0, 0): None}
        for dim in dims:
            if not node[dim]:
                continue
            pair = fraction(dim, zc, node, raised)
            fresh = {}
            for corner, weight in entries.items():
                for side in range(2):
                    moved = list(corner)
                    moved[dim] = side
                    if dim == 0 and side == 1 and zc == 1:
                        continue
                    fresh[tuple(moved)] = times(weight, pair[side])
            entries = fresh
        return entries

    sums = {}

    def put(zc, low, high, value):
        offset = tuple(b - a for a, b in zip(low, high))
        if offset < (0, 0, 0):
            low, high = high, low
            offset = tuple(-o for o in offset)
        if zc + low[0] > 1 or zc + high[0] > 1:
            return
        key = (offset, zc + low[0], low[1], low[2])
        sums[key] = sums[key] + value if key in sums else value

    for d in range(3):
        dims = [dim for dim in range(3) if dim != d]
        for zc in range(2):
            top = d == 0 and zc == 1
            for q1 in range(2):
                for q2 in range(2):
                    node = [0, 0, 0]
                    node[dims[0]], node[dims[1]] = q1, q2
                    odd = list(node)
                    odd[d] = 1
                    if d == 0:
                        key = (0, zc, node[1], node[2])
                    elif d == 1:
                        key = (1, 2 * zc + node[0], node[2])
                    else:
                        key = (2, 2 * zc + node[0], node[1])
                    _, _, s, h, k = lines[key]

                    def raised_corner(corner):
                        moved = list(corner)
                        moved[d] = 1
                        return tuple(moved)

                    zero = (0, 0, 0)
                    if not (q1 or q2):
                        put(zc, zero, zero, s)
                        if not top:
                            up = raised_corner(zero)
                            put(zc, up, up, s)
                            put(zc, zero, up, -s)
                        continue
                    alpha = transverse(d, zc, node, None)
                    beta = transverse(d, zc, odd, None)
                    corners = list(alpha)
                    delta = {t: minus(alpha[t], beta[t]) for t in corners}
                    for i, t in enumerate(corners):
                        s_alpha, h_delta = s * alpha[t], h * delta[t]
                        for u in corners[i:]:
                            put(zc, t, u, s_alpha * alpha[u] + h_delta * delta[u])
                    if top:
                        continue
                    gamma = transverse(d, zc, node, d)
                    epsilon = {t: minus(gamma[t], beta[t]) for t in corners}
                    for i, t in enumerate(corners):
                        s_gamma, k_epsilon = s * gamma[t], k * epsilon[t]
                        for u in corners[i:]:
                            put(zc, raised_corner(t), raised_corner(u), s_gamma * gamma[u] + k_epsilon * epsilon[u])
                    for t in corners:
                        s_delta, s_alpha = s * delta[t], s * alpha[t]
                        for u in corners:
                            put(zc, t, raised_corner(u), s_delta * epsilon[u] - s_alpha * gamma[u])

    drop_x = (rows == ROWS // 2 - 1) & last_x
    drop_y = (lanes == LANES // 2 - 1) & last_y

    def inside(values, offset):
        if offset[1] == 1 and offset[2] == 1:
            return jnp.where(drop_x | drop_y, 0.0, values)
        if offset[1] == 1:
            return jnp.where(drop_x, 0.0, values)
        if offset[2] == 1:
            return jnp.where(drop_y, 0.0, values)
        return values

    operator = {}
    keys = sorted({(offset, z) for offset, z, _, _ in sums})
    for offset, z in keys:
        total = None
        for ax in range(2):
            part = sums.get((offset, z, ax, 0))
            side = sums.get((offset, z, ax, 1))
            if side is not None:
                side = shifted(side, 0, -1)
                part = side if part is None else part + side
            if part is None:
                continue
            part = shifted(part, -ax, 0)
            total = part if total is None else total + part
        operator[offset, z] = inside(total, offset)
        if offset != (0, 0, 0):
            mirror = tuple(-o for o in offset)
            operator[mirror, z + offset[0]] = inside(shifted(total, -offset[1], -offset[2]), mirror)

    chain = [
        [lines[0, z, 0, 0][2] for z in range(2)],
        [lines[1, 2 * z, 0][2] for z in range(2)],
        [lines[2, 2 * z, 0][2] for z in range(2)],
    ]
    return operator, chain


def second_operator(operator, chain, last_x, last_y, rows, lanes):
    odd = {1: rows % 2 == 1, 2: lanes % 2 == 1}
    depth = line_terms(chain[0][0], chain[0][1])[0]
    down, up = {}, {}
    for d in (1, 2):
        for z in range(2):
            here = chain[d][z]
            before = shifted(here, -int(d == 1), -int(d == 2))
            f, g = line_terms(before, here)[:2]
            down[d, z] = jnp.where(odd[d], f, 1.0)
            up[d, z] = jnp.where(odd[d], g, 1.0)
    down_z = {0: down[1, 0], 1: down[1, 1] * depth}
    up_z = {0: up[1, 0], 1: up[1, 1] * depth}

    reaches = ((-1, -1), (0, -1), (0, 0), (0, 1), (1, 0), (1, 1))

    def factors(d, lower, upper):
        base = {}
        for j, o in reaches:
            source = lower if (j, o) in ((-1, -1), (0, 0), (0, 1)) else upper
            source = shifted(source, o if d == 1 else 0, o if d == 2 else 0)
            if (j, o) == (0, 1):
                source = jnp.where(odd[d], 0.0, source)
            if (j, o) == (1, 0):
                source = jnp.where(odd[d], source, 0.0)
            base[j, o] = source
        return {
            (j, o, across): shifted(base[j, o], 0 if d == 1 else across, across if d == 1 else 0)
            for j, o in reaches
            for across in (-1, 0, 1)
        }

    spread = {}
    for far in range(2):
        along_x = factors(1, down_z[far], up_z[far])
        along_y = factors(2, down[2, far], up[2, far])
        for jx, ox in reaches:
            for jy, oy in reaches:
                weight = along_x[jx, ox, oy] * along_y[jy, oy, ox]
                for z in range(2):
                    term = operator[(far - z, ox, oy), z] * weight
                    key = (z, jx, jy)
                    spread[key] = spread[key] + term if key in spread else term

    sides = {
        (z, d): {-1: up_z[z] if d == 1 else up[2, z], 0: depth if (d == 1 and z == 1) else None, 1: down_z[z] if d == 1 else down[2, z]}
        for z in range(2)
        for d in (1, 2)
    }
    own = {(z, mx, my): times(sides[z, 1][mx], sides[z, 2][my]) for z in range(2) for mx in (-1, 0, 1) for my in (-1, 0, 1)}

    def taken(offset):
        return [(m, offset + 1 if m == -1 else offset) for m in (-1, 0, 1) if m * offset != -1]

    drop_x = (rows == ROWS // 2 - 2) & last_x
    drop_y = (lanes == LANES // 2 - 2) & last_y
    results = {}
    for ox in (-1, 0, 1):
        for oy in (-1, 0, 1):
            total = None
            for my, jy in taken(oy):
                part = None
                for mx, jx in taken(ox):
                    term = times(own[0, mx, my], spread[0, jx, jy]) + times(own[1, mx, my], spread[1, jx, jy])
                    term = shifted(term, mx, 0)
                    part = term if part is None else part + term
                part = shifted(part, 0, my)
                total = part if total is None else total + part
            if ox == 1:
                total = jnp.where(drop_x, 0.0, total)
            if oy == 1:
                total = jnp.where(drop_y, 0.0, total)
            results[ox, oy] = total
    return results


def couplings_kernel(inputs_ref, own_ref, far_ref, near_ref):
    odd_y = lax.axis_index("gy") % 2 == 1
    lanes = lax.broadcasted_iota(jnp.int32, (ROWS, LANES), 1)
    low = jnp.zeros((ROWS, LANES), jnp.float32)
    high = jnp.zeros((ROWS, LANES), jnp.float32)
    eps = [permittivity(inputs_ref[0, z] & 3) for z in range(4)]
    for r in range(12):
        values = (inputs_ref[r // 4, r % 4] >> 2).astype(jnp.float32) / 64.0 * eps[r % 4]
        own_ref[r] = values
        turned = pltpu.roll(values, 4 * r + 4, 1)
        low = jnp.where((lanes >= 4 * r) & (lanes < 4 * r + 4), turned, low)
        high = jnp.where(lanes == 4 * r + 4, turned, high)
    far_ref[...] = jnp.where(odd_y, low, high)
    near_ref[...] = jnp.where(odd_y, high, low)


def beside(far_ref, near_ref):
    odd_y = lax.axis_index("gy") % 2 == 1
    far, near = far_ref[...], near_ref[...]
    return jnp.where(odd_y, near, far), jnp.where(odd_y, far, near)


def edges_kernel(own_ref, far_columns_ref, near_columns_ref, far_ref, near_ref):
    odd_x = lax.axis_index("gx") % 2 == 1
    tiles = [own_ref[r] for r in range(12)] + list(beside(far_columns_ref, near_columns_ref))
    for r, values in enumerate(tiles):
        far_ref[r] = jnp.where(odd_x, values[4:8, :], values[0:4, :])
        near_ref[r] = jnp.where(odd_x, values[0:4, :], values[4:8, :])


def operator_kernel(own_ref, far_columns_ref, near_columns_ref, far_ref, near_ref, first_ref, second_ref, block):
    rows = lax.broadcasted_iota(jnp.int32, (ROWS, LANES), 0)
    lanes = lax.broadcasted_iota(jnp.int32, (ROWS, LANES), 1)
    odd_x = lax.axis_index("gx") % 2 == 1
    last_x = lax.axis_index("gx") == lax.axis_size("gx") - 1
    last_y = lax.axis_index("gy") == lax.axis_size("gy") - 1

    tiles = [own_ref[r] for r in range(12)] + list(beside(far_columns_ref, near_columns_ref))
    for r, values in enumerate(tiles):
        block[r, 0:8, :] = values
        block[r, 8:12, :] = jnp.where(odd_x, far_ref[r], near_ref[r])
        block[r, 12:16, :] = jnp.where(odd_x, near_ref[r], far_ref[r])

    source = ((lanes + 2) % LANES // 2 * 4 + 2 * (lanes % 2)) % LANES
    at_even = (lanes >= 126) | (lanes == 64)
    at_odd = lanes >= 126
    even_lanes = (2 * lanes) % LANES
    odd_lanes = (2 * lanes + 1) % LANES

    c = [[[[None, None], [None, None]] for _ in range(4)] for _ in range(3)]
    for px in range(2):
        left = block[12, pl.ds(px, 8, stride=2), :]
        right = block[13, pl.ds(px, 8, stride=2), :]
        above = pick_lanes(right, (2 * lanes + 4) % LANES)
        edge_even = jnp.where((lanes >= 64) & (lanes < 112), above, pick_lanes(left, source))
        edge_odd = pick_lanes(left, (source + 1) % LANES)
        for r in range(12):
            values = block[r, pl.ds(px, 8, stride=2), :]
            planes = c[r // 4][r % 4][px]
            planes[0] = jnp.where(at_even, shifted(edge_even, 0, 2 * r), pick_lanes(values, even_lanes))
            planes[1] = jnp.where(at_odd, shifted(edge_odd, 0, 2 * r), pick_lanes(values, odd_lanes))

    operator, chain = first_operator(c, last_x, last_y, rows, lanes)
    empty = jnp.zeros((ROWS, LANES), jnp.float32)
    full = {}
    for o in range(27):
        offset = (o // 9 - 1, o // 3 % 3 - 1, o % 3 - 1)
        for z in range(2):
            values = operator.get((offset, z), empty)
            full[offset, z] = values
            first_ref[o, z] = values[0:4, 0:64]

    results = second_operator(full, chain, last_x, last_y, rows, lanes)
    second_ref[...] = jnp.zeros(second_ref.shape, jnp.float32)
    for (ox, oy), values in results.items():
        o = 9 + (ox + 1) * 3 + oy + 1
        compact = pick_lanes(values, even_lanes)
        second_ref[o, 0, 0:1, :] = compact[0:1, 0:32]
        second_ref[o, 0, 1:2, :] = compact[2:3, 0:32]


def swapped(values, axis, first):
    pairs = [(i, i + 1) for i in range(first, lax.axis_size(axis) - 1, 2)]
    return lax.ppermute(values, axis, pairs + [(b, a) for a, b in pairs])


def body(material, face_open):
    whole = pl.BlockSpec(memory_space=pltpu.VMEM)
    page = jax.ShapeDtypeStruct((ROWS, LANES), jnp.float32)
    edge = jax.ShapeDtypeStruct((14, 4, LANES), jnp.float32)
    small = pltpu.CompilerParams(vmem_limit_bytes=1 << 20)
    own, far, near = pl.pallas_call(
        couplings_kernel,
        out_shape=(jax.ShapeDtypeStruct((12, ROWS, LANES), jnp.float32), page, page),
        in_specs=[whole],
        out_specs=(whole,) * 3,
        compiler_params=small,
        name="couplings",
    )(face_open * 4 + material[None])
    far_columns = swapped(far, "gy", 1)
    near_columns = swapped(near, "gy", 0)
    far, near = pl.pallas_call(
        edges_kernel,
        out_shape=(edge, edge),
        in_specs=[whole] * 3,
        out_specs=(whole,) * 2,
        compiler_params=small,
        name="edges",
    )(own, far_columns, near_columns)
    far_rows = swapped(far, "gx", 1)
    near_rows = swapped(near, "gx", 0)
    return pl.pallas_call(
        operator_kernel,
        out_shape=(
            jax.ShapeDtypeStruct((27, 2, 4, 64), jnp.float32),
            jax.ShapeDtypeStruct((27, 1, 2, 32), jnp.float32),
        ),
        in_specs=[whole] * 5,
        out_specs=(whole,) * 2,
        scratch_shapes=[pltpu.VMEM((14, 16, LANES), jnp.float32)],
        compiler_params=pltpu.CompilerParams(vmem_limit_bytes=2 << 20),
        name="operators",
    )(own, far_columns, near_columns, far_rows, near_rows)


def solution(mesh):
    placed = (P(None, "gx", "gy"), P(None, None, "gx", "gy"))
    return jax.shard_map(
        body,
        mesh=mesh,
        in_specs=placed,
        out_specs=(P(None, None, "gx", "gy"), P(None, None, "gx", "gy")),
        check_vma=False,
    )
```

```python
import functools

import jax
import jax.numpy as jnp
from jax import lax
from jax.experimental import pallas as pl
from jax.experimental.pallas import tpu as pltpu
from jax.sharding import PartitionSpec as P

permit_levels = (1.0 / 80.0, 4.0 / 80.0, 20.0 / 80.0, 1.0)

ROWS, LANES = 8, 128


def permittivity(material):
    values = jnp.zeros(material.shape, jnp.float32)
    for material_id in range(4):
        values = values + jnp.where(material == material_id, permit_levels[material_id], 0.0)
    return values


def shifted(values, by_x, by_y):
    if by_x:
        values = pltpu.roll(values, (-by_x) % ROWS, 0)
    if by_y:
        values = pltpu.roll(values, (-by_y) % LANES, 1)
    return values


def pick_lanes(values, index):
    return jnp.take_along_axis(values, index, axis=1)


def times(a, b):
    if a is None:
        return b
    if b is None:
        return a
    return a * b


def minus(a, b):
    return (1.0 if a is None else a) - (1.0 if b is None else b)


def line_terms(lower, upper):
    total = lower + upper
    inverse = 1.0 / jnp.where(total > 0.0, total, 1.0)
    f = lower * inverse
    g = upper * inverse
    return f, g, lower * g, lower * f, upper * g


def first_operator(c, last_x, last_y, rows, lanes):
    lines = {}
    for z in range(4):
        for p in range(2):
            lines[1, z, p] = line_terms(c[1][z][0][p], c[1][z][1][p])
            lines[2, z, p] = line_terms(c[2][z][p][0], c[2][z][p][1])
    for zc in range(2):
        for px in range(2):
            for py in range(2):
                lines[0, zc, px, py] = line_terms(c[0][2 * zc][px][py], c[0][2 * zc + 1][px][py])

    rolled = {}

    def fraction(dim, zc, node, raised):
        pz, px, py = node
        if raised == 0:
            zc, raised = zc + 1, None
        if dim == 0:
            key = (0, zc, px, py)
        elif dim == 1:
            key = (1, 2 * zc + pz, py)
        else:
            key = (2, 2 * zc + pz, px)
        if raised is None:
            return lines[key][:2]
        if (key, raised) not in rolled:
            f = shifted(lines[key][0], int(raised == 1), int(raised == 2))
            rolled[key, raised] = (f, 1.0 - f)
        return rolled[key, raised]

    def transverse(d, zc, node, raised):
        dims = [dim for dim in range(3) if dim != d]
        entries = {(0, 0, 0): None}
        for dim in dims:
            if not node[dim]:
                continue
            pair = fraction(dim, zc, node, raised)
            fresh = {}
            for corner, weight in entries.items():
                for side in range(2):
                    moved = list(corner)
                    moved[dim] = side
                    if dim == 0 and side == 1 and zc == 1:
                        continue
                    fresh[tuple(moved)] = times(weight, pair[side])
            entries = fresh
        return entries

    sums = {}

    def put(zc, low, high, value):
        offset = tuple(b - a for a, b in zip(low, high))
        if offset < (0, 0, 0):
            low, high = high, low
            offset = tuple(-o for o in offset)
        if zc + low[0] > 1 or zc + high[0] > 1:
            return
        key = (offset, zc + low[0], low[1], low[2])
        sums[key] = sums[key] + value if key in sums else value

    for d in range(3):
        dims = [dim for dim in range(3) if dim != d]
        for zc in range(2):
            top = d == 0 and zc == 1
            for q1 in range(2):
                for q2 in range(2):
                    node = [0, 0, 0]
                    node[dims[0]], node[dims[1]] = q1, q2
                    odd = list(node)
                    odd[d] = 1
                    if d == 0:
                        key = (0, zc, node[1], node[2])
                    elif d == 1:
                        key = (1, 2 * zc + node[0], node[2])
                    else:
                        key = (2, 2 * zc + node[0], node[1])
                    _, _, s, h, k = lines[key]

                    def raised_corner(corner):
                        moved = list(corner)
                        moved[d] = 1
                        return tuple(moved)

                    zero = (0, 0, 0)
                    if not (q1 or q2):
                        put(zc, zero, zero, s)
                        if not top:
                            up = raised_corner(zero)
                            put(zc, up, up, s)
                            put(zc, zero, up, -s)
                        continue
                    alpha = transverse(d, zc, node, None)
                    beta = transverse(d, zc, odd, None)
                    corners = list(alpha)
                    delta = {t: minus(alpha[t], beta[t]) for t in corners}
                    for i, t in enumerate(corners):
                        s_alpha, h_delta = s * alpha[t], h * delta[t]
                        for u in corners[i:]:
                            put(zc, t, u, s_alpha * alpha[u] + h_delta * delta[u])
                    if top:
                        continue
                    gamma = transverse(d, zc, node, d)
                    epsilon = {t: minus(gamma[t], beta[t]) for t in corners}
                    for i, t in enumerate(corners):
                        s_gamma, k_epsilon = s * gamma[t], k * epsilon[t]
                        for u in corners[i:]:
                            put(zc, raised_corner(t), raised_corner(u), s_gamma * gamma[u] + k_epsilon * epsilon[u])
                    for t in corners:
                        s_delta, s_alpha = s * delta[t], s * alpha[t]
                        for u in corners:
                            put(zc, t, raised_corner(u), s_delta * epsilon[u] - s_alpha * gamma[u])

    drop_x = (rows == ROWS // 2 - 1) & last_x
    drop_y = (lanes == LANES // 2 - 1) & last_y

    def inside(values, offset):
        if offset[1] == 1 and offset[2] == 1:
            return jnp.where(drop_x | drop_y, 0.0, values)
        if offset[1] == 1:
            return jnp.where(drop_x, 0.0, values)
        if offset[2] == 1:
            return jnp.where(drop_y, 0.0, values)
        return values

    operator = {}
    keys = sorted({(offset, z) for offset, z, _, _ in sums})
    for offset, z in keys:
        total = None
        for ax in range(2):
            part = sums.get((offset, z, ax, 0))
            side = sums.get((offset, z, ax, 1))
            if side is not None:
                side = shifted(side, 0, -1)
                part = side if part is None else part + side
            if part is None:
                continue
            part = shifted(part, -ax, 0)
            total = part if total is None else total + part
        operator[offset, z] = inside(total, offset)
        if offset != (0, 0, 0):
            mirror = tuple(-o for o in offset)
            operator[mirror, z + offset[0]] = inside(shifted(total, -offset[1], -offset[2]), mirror)

    chain = [
        [lines[0, z, 0, 0][2] for z in range(2)],
        [lines[1, 2 * z, 0][2] for z in range(2)],
        [lines[2, 2 * z, 0][2] for z in range(2)],
    ]
    return operator, chain


def second_operator(operator, chain, last_x, last_y, rows, lanes):
    odd = {1: rows % 2 == 1, 2: lanes % 2 == 1}
    depth = line_terms(chain[0][0], chain[0][1])[0]
    down, up = {}, {}
    for d in (1, 2):
        for z in range(2):
            here = chain[d][z]
            before = shifted(here, -int(d == 1), -int(d == 2))
            f, g = line_terms(before, here)[:2]
            down[d, z] = jnp.where(odd[d], f, 1.0)
            up[d, z] = jnp.where(odd[d], g, 1.0)
    down_z = {0: down[1, 0], 1: down[1, 1] * depth}
    up_z = {0: up[1, 0], 1: up[1, 1] * depth}

    reaches = ((-1, -1), (0, -1), (0, 0), (0, 1), (1, 0), (1, 1))

    def factors(d, lower, upper):
        base = {}
        for j, o in reaches:
            source = lower if (j, o) in ((-1, -1), (0, 0), (0, 1)) else upper
            source = shifted(source, o if d == 1 else 0, o if d == 2 else 0)
            if (j, o) == (0, 1):
                source = jnp.where(odd[d], 0.0, source)
            if (j, o) == (1, 0):
                source = jnp.where(odd[d], source, 0.0)
            base[j, o] = source
        return {
            (j, o, across): shifted(base[j, o], 0 if d == 1 else across, across if d == 1 else 0)
            for j, o in reaches
            for across in (-1, 0, 1)
        }

    spread = {}
    for far in range(2):
        along_x = factors(1, down_z[far], up_z[far])
        along_y = factors(2, down[2, far], up[2, far])
        for jx, ox in reaches:
            for jy, oy in reaches:
                weight = along_x[jx, ox, oy] * along_y[jy, oy, ox]
                for z in range(2):
                    term = operator[(far - z, ox, oy), z] * weight
                    key = (z, jx, jy)
                    spread[key] = spread[key] + term if key in spread else term

    sides = {
        (z, d): {-1: up_z[z] if d == 1 else up[2, z], 0: depth if (d == 1 and z == 1) else None, 1: down_z[z] if d == 1 else down[2, z]}
        for z in range(2)
        for d in (1, 2)
    }
    own = {(z, mx, my): times(sides[z, 1][mx], sides[z, 2][my]) for z in range(2) for mx in (-1, 0, 1) for my in (-1, 0, 1)}

    def taken(offset):
        return [(m, offset + 1 if m == -1 else offset) for m in (-1, 0, 1) if m * offset != -1]

    drop_x = (rows == ROWS // 2 - 2) & last_x
    drop_y = (lanes == LANES // 2 - 2) & last_y
    results = {}
    for ox in (-1, 0, 1):
        for oy in (-1, 0, 1):
            total = None
            for my, jy in taken(oy):
                part = None
                for mx, jx in taken(ox):
                    term = times(own[0, mx, my], spread[0, jx, jy]) + times(own[1, mx, my], spread[1, jx, jy])
                    term = shifted(term, mx, 0)
                    part = term if part is None else part + term
                part = shifted(part, 0, my)
                total = part if total is None else total + part
            if ox == 1:
                total = jnp.where(drop_x, 0.0, total)
            if oy == 1:
                total = jnp.where(drop_y, 0.0, total)
            results[ox, oy] = total
    return results


def couplings_kernel(inputs_ref, own_ref, near_ref, far_ref):
    odd_y = lax.axis_index("gy") % 2 == 1
    lanes = lax.broadcasted_iota(jnp.int32, (ROWS, LANES), 1)
    low = jnp.zeros((ROWS, LANES), jnp.float32)
    high = jnp.zeros((ROWS, LANES), jnp.float32)
    eps = [permittivity(inputs_ref[0, z] & 3) for z in range(4)]
    for r in range(12):
        values = (inputs_ref[r // 4, r % 4] >> 2).astype(jnp.float32) / 64.0 * eps[r % 4]
        own_ref[r] = values
        turned = pltpu.roll(values, 4 * r + 4, 1)
        low = jnp.where((lanes >= 4 * r) & (lanes < 4 * r + 4), turned, low)
        high = jnp.where(lanes == 4 * r + 4, turned, high)
    far_ref[...] = jnp.where(odd_y, low, high)
    near_ref[...] = jnp.where(odd_y, high, low)


def beside(near_ref, far_ref):
    odd_y = lax.axis_index("gy") % 2 == 1
    far, near = far_ref[...], near_ref[...]
    return jnp.where(odd_y, near, far), jnp.where(odd_y, far, near)


def edges_kernel(own_ref, near_columns_ref, far_columns_ref, far_ref, near_ref):
    odd_x = lax.axis_index("gx") % 2 == 1
    tiles = [own_ref[r] for r in range(12)] + list(beside(near_columns_ref, far_columns_ref))
    for r, values in enumerate(tiles):
        far_ref[r] = jnp.where(odd_x, values[4:8, :], values[0:4, :])
        near_ref[r] = jnp.where(odd_x, values[0:4, :], values[4:8, :])


def operator_kernel(own_ref, near_columns_ref, far_columns_ref, far_ref, near_ref, first_ref, second_ref, block):
    rows = lax.broadcasted_iota(jnp.int32, (ROWS, LANES), 0)
    lanes = lax.broadcasted_iota(jnp.int32, (ROWS, LANES), 1)
    odd_x = lax.axis_index("gx") % 2 == 1
    last_x = lax.axis_index("gx") == lax.axis_size("gx") - 1
    last_y = lax.axis_index("gy") == lax.axis_size("gy") - 1

    tiles = [own_ref[r] for r in range(12)] + list(beside(near_columns_ref, far_columns_ref))
    for r, values in enumerate(tiles):
        block[r, 0:8, :] = values
        block[r, 8:12, :] = jnp.where(odd_x, far_ref[r], near_ref[r])
        block[r, 12:16, :] = jnp.where(odd_x, near_ref[r], far_ref[r])

    source = ((lanes + 2) % LANES // 2 * 4 + 2 * (lanes % 2)) % LANES
    at_even = (lanes >= 126) | (lanes == 64)
    at_odd = lanes >= 126
    even_lanes = (2 * lanes) % LANES
    odd_lanes = (2 * lanes + 1) % LANES

    c = [[[[None, None], [None, None]] for _ in range(4)] for _ in range(3)]
    for px in range(2):
        left = block[12, pl.ds(px, 8, stride=2), :]
        right = block[13, pl.ds(px, 8, stride=2), :]
        above = pick_lanes(right, (2 * lanes + 4) % LANES)
        edge_even = jnp.where((lanes >= 64) & (lanes < 112), above, pick_lanes(left, source))
        edge_odd = pick_lanes(left, (source + 1) % LANES)
        for r in range(12):
            values = block[r, pl.ds(px, 8, stride=2), :]
            planes = c[r // 4][r % 4][px]
            planes[0] = jnp.where(at_even, shifted(edge_even, 0, 2 * r), pick_lanes(values, even_lanes))
            planes[1] = jnp.where(at_odd, shifted(edge_odd, 0, 2 * r), pick_lanes(values, odd_lanes))

    operator, chain = first_operator(c, last_x, last_y, rows, lanes)
    empty = jnp.zeros((ROWS, LANES), jnp.float32)
    full = {}
    for o in range(27):
        offset = (o // 9 - 1, o // 3 % 3 - 1, o % 3 - 1)
        for z in range(2):
            values = operator.get((offset, z), empty)
            full[offset, z] = values
            first_ref[o, z] = values[0:4, 0:64]

    results = second_operator(full, chain, last_x, last_y, rows, lanes)
    second_ref[...] = jnp.zeros(second_ref.shape, jnp.float32)
    for (ox, oy), values in results.items():
        o = 9 + (ox + 1) * 3 + oy + 1
        compact = pick_lanes(values, even_lanes)
        second_ref[o, 0, 0:1, :] = compact[0:1, 0:32]
        second_ref[o, 0, 1:2, :] = compact[2:3, 0:32]


def swapped(values, axis, first):
    pairs = [(i, i + 1) for i in range(first, lax.axis_size(axis) - 1, 2)]
    return lax.ppermute(values, axis, pairs + [(b, a) for a, b in pairs])


def body(material, face_open):
    whole = pl.BlockSpec(memory_space=pltpu.VMEM)
    page = jax.ShapeDtypeStruct((ROWS, LANES), jnp.float32)
    edge = jax.ShapeDtypeStruct((14, 4, LANES), jnp.float32)
    small = pltpu.CompilerParams(vmem_limit_bytes=1 << 20)
    own, near, far = pl.pallas_call(
        couplings_kernel,
        out_shape=(jax.ShapeDtypeStruct((12, ROWS, LANES), jnp.float32), page, page),
        in_specs=[whole],
        out_specs=(whole,) * 3,
        compiler_params=small,
        name="couplings",
    )(face_open * 4 + material[None])
    near_columns = swapped(near, "gy", 0)
    far_columns = swapped(far, "gy", 1)
    far, near = pl.pallas_call(
        edges_kernel,
        out_shape=(edge, edge),
        in_specs=[whole] * 3,
        out_specs=(whole,) * 2,
        compiler_params=small,
        name="edges",
    )(own, near_columns, far_columns)
    far_rows = swapped(far, "gx", 1)
    near_rows = swapped(near, "gx", 0)
    return pl.pallas_call(
        operator_kernel,
        out_shape=(
            jax.ShapeDtypeStruct((27, 2, 4, 64), jnp.float32),
            jax.ShapeDtypeStruct((27, 1, 2, 32), jnp.float32),
        ),
        in_specs=[whole] * 5,
        out_specs=(whole,) * 2,
        scratch_shapes=[pltpu.VMEM((14, 16, LANES), jnp.float32)],
        compiler_params=pltpu.CompilerParams(vmem_limit_bytes=2 << 20),
        name="operators",
    )(own, near_columns, far_columns, far_rows, near_rows)


def solution(mesh):
    placed = (P(None, "gx", "gy"), P(None, None, "gx", "gy"))
    return jax.shard_map(
        body,
        mesh=mesh,
        in_specs=placed,
        out_specs=(P(None, None, "gx", "gy"), P(None, None, "gx", "gy")),
        check_vma=False,
    )
```

```python
import functools

import jax
import jax.numpy as jnp
from jax import lax
from jax.experimental import pallas as pl
from jax.experimental.pallas import tpu as pltpu
from jax.sharding import PartitionSpec as P

permit_levels = (1.0 / 80.0, 4.0 / 80.0, 20.0 / 80.0, 1.0)

ROWS, LANES = 8, 128


def permittivity(material):
    values = jnp.zeros(material.shape, jnp.float32)
    for material_id in range(4):
        values = values + jnp.where(material == material_id, permit_levels[material_id], 0.0)
    return values


def shifted(values, by_x, by_y):
    if by_x:
        values = pltpu.roll(values, (-by_x) % ROWS, 0)
    if by_y:
        values = pltpu.roll(values, (-by_y) % LANES, 1)
    return values


def pick_lanes(values, index):
    return jnp.take_along_axis(values, index, axis=1)


def times(a, b):
    if a is None:
        return b
    if b is None:
        return a
    return a * b


def minus(a, b):
    return (1.0 if a is None else a) - (1.0 if b is None else b)


def line_terms(lower, upper):
    total = lower + upper
    inverse = 1.0 / jnp.where(total > 0.0, total, 1.0)
    f = lower * inverse
    g = upper * inverse
    return f, g, lower * g, lower * f, upper * g


def edge_masks(last_x, last_y, rows, lanes, step):
    return (rows == ROWS // 2 - step) & last_x, (lanes == LANES // 2 - step) & last_y


def dropped(values, offset_x, offset_y, masks):
    if offset_x == 1:
        values = jnp.where(masks[0], 0.0, values)
    if offset_y == 1:
        values = jnp.where(masks[1], 0.0, values)
    return values


def first_operator(c, masks, hold=None):
    factors = {}
    lines = {}
    for z in range(4):
        for p in range(2):
            lines[1, z, p] = line_terms(c[1][z][0][p], c[1][z][1][p])
            lines[2, z, p] = line_terms(c[2][z][p][0], c[2][z][p][1])
    for zc in range(2):
        for px in range(2):
            for py in range(2):
                lines[0, zc, px, py] = line_terms(c[0][2 * zc][px][py], c[0][2 * zc + 1][px][py])

    rolled = {}

    def fraction(dim, zc, node, raised):
        pz, px, py = node
        if raised == 0:
            zc, raised = zc + 1, None
        if dim == 0:
            key = (0, zc, px, py)
        elif dim == 1:
            key = (1, 2 * zc + pz, py)
        else:
            key = (2, 2 * zc + pz, px)
        if raised is None:
            return lines[key][:2]
        if (key, raised) not in rolled:
            f = shifted(lines[key][0], int(raised == 1), int(raised == 2))
            rolled[key, raised] = (f, 1.0 - f)
        return rolled[key, raised]

    def transverse(d, zc, node, raised):
        dims = [dim for dim in range(3) if dim != d]
        entries = {(0, 0, 0): None}
        for dim in dims:
            if not node[dim]:
                continue
            pair = fraction(dim, zc, node, raised)
            fresh = {}
            for corner, weight in entries.items():
                for side in range(2):
                    moved = list(corner)
                    moved[dim] = side
                    if dim == 0 and side == 1 and zc == 1:
                        continue
                    fresh[tuple(moved)] = times(weight, pair[side])
            entries = fresh
        return entries

    sums = {}

    def put(zc, low, high, value):
        offset = tuple(b - a for a, b in zip(low, high))
        if offset < (0, 0, 0):
            low, high = high, low
            offset = tuple(-o for o in offset)
        if zc + low[0] > 1 or zc + high[0] > 1:
            return
        key = (offset, zc + low[0], low[1], low[2])
        sums[key] = sums[key] + value if key in sums else value

    for d in range(3):
        dims = [dim for dim in range(3) if dim != d]
        for zc in range(2):
            top = d == 0 and zc == 1
            for q1 in range(2):
                for q2 in range(2):
                    node = [0, 0, 0]
                    node[dims[0]], node[dims[1]] = q1, q2
                    odd = list(node)
                    odd[d] = 1
                    if d == 0:
                        key = (0, zc, node[1], node[2])
                    elif d == 1:
                        key = (1, 2 * zc + node[0], node[2])
                    else:
                        key = (2, 2 * zc + node[0], node[1])
                    _, _, s, h, k = lines[key]

                    def raised_corner(corner):
                        moved = list(corner)
                        moved[d] = 1
                        return tuple(moved)

                    zero = (0, 0, 0)
                    if not (q1 or q2):
                        put(zc, zero, zero, s)
                        if not top:
                            up = raised_corner(zero)
                            put(zc, up, up, s)
                            put(zc, zero, up, -s)
                        continue
                    alpha = transverse(d, zc, node, None)
                    beta = transverse(d, zc, odd, None)
                    corners = list(alpha)
                    delta = {t: minus(alpha[t], beta[t]) for t in corners}
                    for i, t in enumerate(corners):
                        s_alpha, h_delta = s * alpha[t], h * delta[t]
                        for u in corners[i:]:
                            put(zc, t, u, s_alpha * alpha[u] + h_delta * delta[u])
                    if top:
                        continue
                    gamma = transverse(d, zc, node, d)
                    epsilon = {t: minus(gamma[t], beta[t]) for t in corners}
                    for i, t in enumerate(corners):
                        s_gamma, k_epsilon = s * gamma[t], k * epsilon[t]
                        for u in corners[i:]:
                            put(zc, raised_corner(t), raised_corner(u), s_gamma * gamma[u] + k_epsilon * epsilon[u])
                    waiting = hold is not None and d == 1
                    for t in corners:
                        s_delta, s_beta = s * delta[t], s * beta[t]
                        if waiting:
                            factors[zc, q1, q2, t] = s_beta
                            s_beta = jnp.where(hold, 0.0, s_beta)
                        for u in corners:
                            put(zc, t, raised_corner(u), -(s_delta * beta[u] + s_beta * gamma[u]))

    operator = {}
    keys = sorted({(offset, z) for offset, z, _, _ in sums})
    for offset, z in keys:
        total = None
        for ax in range(2):
            part = sums.get((offset, z, ax, 0))
            side = sums.get((offset, z, ax, 1))
            if side is not None:
                side = shifted(side, 0, -1)
                part = side if part is None else part + side
            if part is None:
                continue
            part = shifted(part, -ax, 0)
            total = part if total is None else total + part
        operator[offset, z] = dropped(total, *offset[1:], masks)
        if offset != (0, 0, 0):
            mirror = tuple(-o for o in offset)
            operator[mirror, z + offset[0]] = dropped(shifted(total, -offset[1], -offset[2]), *mirror[1:], masks)

    chain = [
        [lines[0, z, 0, 0][2] for z in range(2)],
        [lines[1, 2 * z, 0][2] for z in range(2)],
        [lines[2, 2 * z, 0][2] for z in range(2)],
    ]
    return operator, chain, factors


reaches = ((-1, -1), (0, -1), (0, 0), (0, 1), (1, 0), (1, 1))


def taken(offset):
    return [(m, offset + 1 if m == -1 else offset) for m in (-1, 0, 1) if m * offset != -1]


def from_below(j, o):
    return (j, o) in ((-1, -1), (0, 0), (0, 1))


def reaching(j, o, source, odd):
    if (j, o) == (0, 1):
        return jnp.where(odd, 0.0, source)
    if (j, o) == (1, 0):
        return jnp.where(odd, source, 0.0)
    return source


def second_operator(operator, chain, rows, lanes, hold=None):
    odd = {1: rows % 2 == 1, 2: lanes % 2 == 1}
    depth = line_terms(chain[0][0], chain[0][1])[0]
    down, up = {}, {}
    for d in (1, 2):
        for z in range(2):
            here = chain[d][z]
            before = shifted(here, -int(d == 1), -int(d == 2))
            f, g = line_terms(before, here)[:2]
            down[d, z] = jnp.where(odd[d], f, 1.0)
            up[d, z] = jnp.where(odd[d], g, 1.0)
    down_z = {0: down[1, 0], 1: down[1, 1] * depth}
    up_z = {0: up[1, 0], 1: up[1, 1] * depth}

    def factors(d, lower, upper):
        base = {}
        for j, o in reaches:
            source = lower if from_below(j, o) else upper
            source = reaching(j, o, shifted(source, o if d == 1 else 0, o if d == 2 else 0), odd[d])
            if hold is not None and d == 1 and (j, o) == (1, 1):
                source = jnp.where(hold, 0.0, source)
            base[j, o] = source
        return {
            (j, o, across): shifted(base[j, o], 0 if d == 1 else across, across if d == 1 else 0)
            for j, o in reaches
            for across in (-1, 0, 1)
        }

    spread = {}
    for far in range(2):
        along_x = factors(1, down_z[far], up_z[far])
        along_y = factors(2, down[2, far], up[2, far])
        for jx, ox in reaches:
            for jy, oy in reaches:
                weight = along_x[jx, ox, oy] * along_y[jy, oy, ox]
                for z in range(2):
                    term = operator[(far - z, ox, oy), z] * weight
                    key = (z, jx, jy)
                    spread[key] = spread[key] + term if key in spread else term

    sides = {
        (z, d): {-1: up_z[z] if d == 1 else up[2, z], 0: depth if (d == 1 and z == 1) else None, 1: down_z[z] if d == 1 else down[2, z]}
        for z in range(2)
        for d in (1, 2)
    }
    own = {(z, mx, my): times(sides[z, 1][mx], sides[z, 2][my]) for z in range(2) for mx in (-1, 0, 1) for my in (-1, 0, 1)}

    results = {}
    for ox in (-1, 0, 1):
        for oy in (-1, 0, 1):
            total = None
            for my, jy in taken(oy):
                part = None
                for mx, jx in taken(ox):
                    term = times(own[0, mx, my], spread[0, jx, jy]) + times(own[1, mx, my], spread[1, jx, jy])
                    term = shifted(term, mx, 0)
                    part = term if part is None else part + term
                part = shifted(part, 0, my)
                total = part if total is None else total + part
            results[ox, oy] = total
    return results, own


def couplings_kernel(inputs_ref, own_ref, near_ref, far_ref):
    odd_y = lax.axis_index("gy") % 2 == 1
    lanes = lax.broadcasted_iota(jnp.int32, (ROWS, LANES), 1)
    low = jnp.zeros((ROWS, LANES), jnp.float32)
    high = jnp.zeros((ROWS, LANES), jnp.float32)
    eps = [permittivity(inputs_ref[0, z] & 3) for z in range(4)]
    for r in range(12):
        values = (inputs_ref[r // 4, r % 4] >> 2).astype(jnp.float32) / 64.0 * eps[r % 4]
        own_ref[r] = values
        turned = pltpu.roll(values, 4 * r + 4, 1)
        low = jnp.where((lanes >= 4 * r) & (lanes < 4 * r + 4), turned, low)
        high = jnp.where(lanes == 4 * r + 4, turned, high)
    far_ref[...] = jnp.where(odd_y, low, high)
    near_ref[...] = jnp.where(odd_y, high, low)


def beside(near_ref, far_ref):
    odd_y = lax.axis_index("gy") % 2 == 1
    far, near = far_ref[...], near_ref[...]
    return jnp.where(odd_y, near, far), jnp.where(odd_y, far, near)


def edges_kernel(own_ref, near_columns_ref, far_columns_ref, far_ref, near_ref):
    odd_x = lax.axis_index("gx") % 2 == 1
    tiles = [own_ref[r] for r in range(12)] + list(beside(near_columns_ref, far_columns_ref))
    for r, values in enumerate(tiles):
        far_ref[r] = jnp.where(odd_x, values[4:8, :], values[0:4, :])
        near_ref[r] = jnp.where(odd_x, values[0:4, :], values[4:8, :])


def lane_picks(lanes):
    source = ((lanes + 2) % LANES // 2 * 4 + 2 * (lanes % 2)) % LANES
    return source, (2 * lanes) % LANES, (lanes >= 126) | (lanes == 64), lanes >= 126


def columns_beside(left, right, lanes, source):
    above = pick_lanes(right, (2 * lanes + 4) % LANES)
    even = jnp.where((lanes >= 64) & (lanes < 112), above, pick_lanes(left, source))
    return even, pick_lanes(left, (source + 1) % LANES)


def split_lanes(values, r, edges, picks):
    _, even_lanes, at_even, at_odd = picks
    even = jnp.where(at_even, shifted(edges[0], 0, 2 * r), pick_lanes(values, even_lanes))
    odd = jnp.where(at_odd, shifted(edges[1], 0, 2 * r), pick_lanes(values, even_lanes + 1))
    return even, odd


def split_couplings(block, lanes):
    picks = lane_picks(lanes)
    c = [[[[None, None], [None, None]] for _ in range(4)] for _ in range(3)]
    for px in range(2):
        left = block[12, pl.ds(px, 8, stride=2), :]
        right = block[13, pl.ds(px, 8, stride=2), :]
        edges = columns_beside(left, right, lanes, picks[0])
        for r in range(12):
            values = block[r, pl.ds(px, 8, stride=2), :]
            c[r // 4][r % 4][px][:] = split_lanes(values, r, edges, picks)
    return c


def places():
    rows = lax.broadcasted_iota(jnp.int32, (ROWS, LANES), 0)
    lanes = lax.broadcasted_iota(jnp.int32, (ROWS, LANES), 1)
    last_x = lax.axis_index("gx") == lax.axis_size("gx") - 1
    last_y = lax.axis_index("gy") == lax.axis_size("gy") - 1
    return rows, lanes, last_x, last_y


def operators(block, first_ref, second_ref, hold_row=None):
    rows, lanes, last_x, last_y = places()
    hold = None if hold_row is None else rows == hold_row
    c = split_couplings(block, lanes)
    operator, chain, factors = first_operator(c, edge_masks(last_x, last_y, rows, lanes, 1), hold)
    empty = jnp.zeros((ROWS, LANES), jnp.float32)
    full = {}
    for o in range(27):
        offset = (o // 9 - 1, o // 3 % 3 - 1, o % 3 - 1)
        for z in range(2):
            full[offset, z] = operator.get((offset, z), empty)
            first_ref[o, z] = full[offset, z][0:4, 0:64]
    results, own = second_operator(full, chain, rows, lanes, hold)
    masks = edge_masks(last_x, last_y, rows, lanes, 2)
    second_ref[...] = jnp.zeros(second_ref.shape, jnp.float32)
    for (ox, oy), values in results.items():
        compact = pick_lanes(dropped(values, ox, oy, masks), (2 * lanes) % LANES)
        second_ref[9 + (ox + 1) * 3 + oy + 1, 0, 0:1, :] = compact[0:1, 0:32]
        second_ref[9 + (ox + 1) * 3 + oy + 1, 0, 1:2, :] = compact[2:3, 0:32]
    return operator, factors, results, own


fix_entries = [((oz, 1, oy), z) for z in (0, 1) for oz in (-z, 1 - z) for oy in (-1, 0, 1)]
fix_factors = [
    (zc, qz, qy, (tz, 0, ty))
    for zc in (0, 1)
    for qz in (0, 1)
    for qy in (0, 1)
    if qz or qy
    for tz in range(1 + (qz if zc == 0 else 0))
    for ty in range(1 + qy)
]
fix_sides = [(z, 1, my) for z in (0, 1) for my in (-1, 0, 1)]
fix_results = [(1, oy) for oy in (-1, 0, 1)]
fix_count = len(fix_entries) + len(fix_factors) + len(fix_sides) + len(fix_results)


def early_kernel(own_ref, near_columns_ref, far_columns_ref, far_ref, first_ref, second_ref, kept_ref, block):
    tiles = [own_ref[r] for r in range(12)] + list(beside(near_columns_ref, far_columns_ref))
    for r, values in enumerate(tiles):
        block[r, 0:8, :] = values
        block[r, 8:12, :] = jnp.zeros((4, LANES), jnp.float32)
        block[r, 12:16, :] = far_ref[r]
    operator, factors, results, own = operators(block, first_ref, second_ref, ROWS // 2 - 1)
    kept = [operator[e] for e in fix_entries] + [factors[e] for e in fix_factors]
    kept += [own[e] for e in fix_sides] + [results[e] for e in fix_results]
    for i, values in enumerate(kept):
        kept_ref[i] = values


def add_row_above(near_ref, early_second_ref, kept_ref, first_ref, second_ref):
    rows, lanes, last_x, last_y = places()
    kept = {e: kept_ref[i] for i, e in enumerate(fix_entries + fix_factors + fix_sides + fix_results)}

    def row(r):
        return jnp.broadcast_to(near_ref[r, 0:1, :], (ROWS, LANES))

    picks = lane_picks(lanes)
    edges = columns_beside(row(12), row(13), lanes, picks[0])
    c = {(d, z): split_lanes(row(d * 4 + z), d * 4 + z, edges, picks) for d in (0, 2) for z in range(4)}
    line_y = {z: line_terms(*c[2, z]) for z in range(4)}
    line_z = {(zc, py): line_terms(c[0, 2 * zc][py], c[0, 2 * zc + 1][py]) for zc in range(2) for py in range(2)}

    sums = {}
    for zc, qz, qy, t in fix_factors:
        pair_z = line_z[zc, qy][:2] if qz else (None,)
        pair_y = line_y[2 * zc + qz][:2] if qy else (None,)
        for uz in range(1 + (qz if zc == 0 else 0)):
            for uy in range(1 + qy):
                key = ((uz - t[0], 1, uy - t[2]), zc + t[0], t[2])
                term = kept[zc, qz, qy, t] * times(pair_z[uz], pair_y[uy])
                sums[key] = sums[key] + term if key in sums else term
    masks = edge_masks(last_x, last_y, rows, lanes, 1)
    entries = {}
    for offset, z in fix_entries:
        total = kept[offset, z]
        if (offset, z, 0) in sums:
            total = total - sums[offset, z, 0]
        if (offset, z, 1) in sums:
            total = total - shifted(sums[offset, z, 1], 0, -1)
        entries[offset, z] = dropped(total, *offset[1:], masks)
        whole = jnp.where(rows == ROWS // 2 - 1, entries[offset, z], kept[offset, z])
        first_ref[(offset[0] + 1) * 3 + offset[2] + 1, z] = whole[0:4, 0:64]
    for offset, z in (((-1, 1), 0), ((1, 1), 1)):
        for oy in range(3):
            first_ref[(offset[0] + 1) * 3 + oy, z] = jnp.zeros((4, 64), jnp.float32)

    depth = line_terms(line_z[0, 0][2], line_z[1, 0][2])[0]
    odd = lanes % 2 == 1
    spread = {}
    for far in range(2):
        here = line_y[2 * far][2]
        f, g = line_terms(shifted(here, 0, -1), here)[:2]
        down, up = jnp.where(odd, f, 1.0), jnp.where(odd, g, 1.0)
        if far == 1:
            down, up = down * depth, up * depth
        for jy, oy in reaches:
            weight = reaching(jy, oy, shifted(down if from_below(jy, oy) else up, 0, oy), odd)
            for z in range(2):
                term = entries[(far - z, 1, oy), z] * weight
                spread[z, jy] = spread[z, jy] + term if (z, jy) in spread else term
    masks = edge_masks(last_x, last_y, rows, lanes, 2)
    for oy in (-1, 0, 1):
        total = None
        for my, jy in taken(oy):
            part = shifted(kept[0, 1, my] * spread[0, jy] + kept[1, 1, my] * spread[1, jy], 0, my)
            total = part if total is None else total + part
        total = dropped(kept[1, oy] + shifted(total, 1, 0), 1, oy, masks)
        compact = pick_lanes(total, (2 * lanes) % LANES)
        second_ref[oy + 1, 0, 0:1, :] = early_second_ref[16 + oy, 0, 0:1, :]
        second_ref[oy + 1, 0, 1:2, :] = compact[2:3, 0:32]


def last_kernel(
    own_ref, near_columns_ref, far_columns_ref, far_ref, early_first_ref, early_second_ref, kept_ref, near_ref,
    first_hbm, second_hbm, block, first_ref, second_ref, first_fix, second_fix, sems,
):
    odd_x = lax.axis_index("gx") % 2 == 1

    def send(parts):
        copies = [pltpu.make_async_copy(source, target, sems.at[i]) for i, source, target in parts]
        for copy in copies:
            copy.start()
        return copies

    @pl.when(odd_x)
    def _():
        tiles = [own_ref[r] for r in range(12)] + list(beside(near_columns_ref, far_columns_ref))
        for r, values in enumerate(tiles):
            block[r, 0:8, :] = values
            block[r, 8:12, :] = far_ref[r]
            block[r, 12:16, :] = near_ref[r]
        operators(block, first_ref, second_ref)
        for copy in send([(0, first_ref, first_hbm), (1, second_ref, second_hbm)]):
            copy.wait()

    @pl.when(jnp.logical_not(odd_x))
    def _():
        parts = [(oz, early_first_ref.at[pl.ds(oz * 9, 6)], first_hbm.at[pl.ds(oz * 9, 6)]) for oz in range(3)]
        parts.append((3, early_second_ref.at[pl.ds(0, 15)], second_hbm.at[pl.ds(0, 15)]))
        parts.append((4, early_second_ref.at[pl.ds(18, 9)], second_hbm.at[pl.ds(18, 9)]))
        copies = send(parts)
        add_row_above(near_ref, early_second_ref, kept_ref, first_fix, second_fix)
        parts = [(5 + oz, first_fix.at[pl.ds(oz * 3, 3)], first_hbm.at[pl.ds(oz * 9 + 6, 3)]) for oz in range(3)]
        parts.append((8, second_fix, second_hbm.at[pl.ds(15, 3)]))
        for copy in copies + send(parts):
            copy.wait()


def swapped(values, axis, first):
    pairs = [(i, i + 1) for i in range(first, lax.axis_size(axis) - 1, 2)]
    return lax.ppermute(values, axis, pairs + [(b, a) for a, b in pairs])


def body(material, face_open):
    whole = pl.BlockSpec(memory_space=pltpu.VMEM)
    page = jax.ShapeDtypeStruct((ROWS, LANES), jnp.float32)
    edge = jax.ShapeDtypeStruct((14, 4, LANES), jnp.float32)
    small = pltpu.CompilerParams(vmem_limit_bytes=1 << 20)
    own, near, far = pl.pallas_call(
        couplings_kernel,
        out_shape=(jax.ShapeDtypeStruct((12, ROWS, LANES), jnp.float32), page, page),
        in_specs=[whole],
        out_specs=(whole,) * 3,
        compiler_params=small,
        name="couplings",
    )(face_open * 4 + material[None])
    near_columns = swapped(near, "gy", 0)
    far_columns = swapped(far, "gy", 1)
    far, near = pl.pallas_call(
        edges_kernel,
        out_shape=(edge, edge),
        in_specs=[whole] * 3,
        out_specs=(whole,) * 2,
        compiler_params=small,
        name="edges",
    )(own, near_columns, far_columns)
    far_rows = swapped(far, "gx", 1)
    near_rows = swapped(near, "gx", 0)
    first = jax.ShapeDtypeStruct((27, 2, 4, 64), jnp.float32)
    second = jax.ShapeDtypeStruct((27, 1, 2, 32), jnp.float32)
    large = pltpu.CompilerParams(vmem_limit_bytes=3 << 20)
    block = pltpu.VMEM((14, 16, LANES), jnp.float32)
    early = pl.pallas_call(
        early_kernel,
        out_shape=(first, second, jax.ShapeDtypeStruct((fix_count, ROWS, LANES), jnp.float32)),
        in_specs=[whole] * 4,
        out_specs=(whole,) * 3,
        scratch_shapes=[block],
        compiler_params=large,
        cost_estimate=pl.CostEstimate(flops=3 << 20, bytes_accessed=1 << 20, transcendentals=0),
        name="early",
    )(own, near_columns, far_columns, far_rows)
    return pl.pallas_call(
        last_kernel,
        out_shape=(first, second),
        in_specs=[whole] * 8,
        out_specs=(pl.BlockSpec(memory_space=pltpu.HBM),) * 2,
        scratch_shapes=[
            block,
            pltpu.VMEM(first.shape, jnp.float32),
            pltpu.VMEM(second.shape, jnp.float32),
            pltpu.VMEM((9, 2, 4, 64), jnp.float32),
            pltpu.VMEM((3, 1, 2, 32), jnp.float32),
            pltpu.SemaphoreType.DMA((9,)),
        ],
        compiler_params=large,
        name="last",
    )(own, near_columns, far_columns, far_rows, *early, near_rows)


def solution(mesh):
    placed = (P(None, "gx", "gy"), P(None, None, "gx", "gy"))
    return jax.shard_map(
        body,
        mesh=mesh,
        in_specs=placed,
        out_specs=(P(None, None, "gx", "gy"), P(None, None, "gx", "gy")),
        check_vma=False,
    )
```

```python
import functools

import jax
import jax.numpy as jnp
from jax import lax
from jax.experimental import pallas as pl
from jax.experimental.pallas import tpu as pltpu
from jax.sharding import PartitionSpec as P

permit_levels = (1.0 / 80.0, 4.0 / 80.0, 20.0 / 80.0, 1.0)

ROWS, LANES = 8, 128


def permittivity(material):
    values = jnp.zeros(material.shape, jnp.float32)
    for material_id in range(4):
        values = values + jnp.where(material == material_id, permit_levels[material_id], 0.0)
    return values


def shifted(values, by_x, by_y):
    if by_x:
        values = pltpu.roll(values, (-by_x) % ROWS, 0)
    if by_y:
        values = pltpu.roll(values, (-by_y) % LANES, 1)
    return values


def pick_lanes(values, index):
    return jnp.take_along_axis(values, index, axis=1)


def times(a, b):
    if a is None:
        return b
    if b is None:
        return a
    return a * b


def minus(a, b):
    return (1.0 if a is None else a) - (1.0 if b is None else b)


def line_terms(lower, upper):
    total = lower + upper
    inverse = 1.0 / jnp.where(total > 0.0, total, 1.0)
    f = lower * inverse
    g = upper * inverse
    return f, g, lower * g, lower * f, upper * g


def edge_masks(last_x, last_y, rows, lanes, step):
    return (rows == ROWS // 2 - step) & last_x, (lanes == LANES // 2 - step) & last_y


def dropped(values, offset_x, offset_y, masks):
    if offset_x == 1:
        values = jnp.where(masks[0], 0.0, values)
    if offset_y == 1:
        values = jnp.where(masks[1], 0.0, values)
    return values


def first_operator(c, masks, hold=None):
    factors = {}
    lines = {}
    for z in range(4):
        for p in range(2):
            lines[1, z, p] = line_terms(c[1][z][0][p], c[1][z][1][p])
            lines[2, z, p] = line_terms(c[2][z][p][0], c[2][z][p][1])
    for zc in range(2):
        for px in range(2):
            for py in range(2):
                lines[0, zc, px, py] = line_terms(c[0][2 * zc][px][py], c[0][2 * zc + 1][px][py])

    rolled = {}

    def fraction(dim, zc, node, raised):
        pz, px, py = node
        if raised == 0:
            zc, raised = zc + 1, None
        if dim == 0:
            key = (0, zc, px, py)
        elif dim == 1:
            key = (1, 2 * zc + pz, py)
        else:
            key = (2, 2 * zc + pz, px)
        if raised is None:
            return lines[key][:2]
        if (key, raised) not in rolled:
            f = shifted(lines[key][0], int(raised == 1), int(raised == 2))
            rolled[key, raised] = (f, 1.0 - f)
        return rolled[key, raised]

    def transverse(d, zc, node, raised):
        dims = [dim for dim in range(3) if dim != d]
        entries = {(0, 0, 0): None}
        for dim in dims:
            if not node[dim]:
                continue
            pair = fraction(dim, zc, node, raised)
            fresh = {}
            for corner, weight in entries.items():
                for side in range(2):
                    moved = list(corner)
                    moved[dim] = side
                    if dim == 0 and side == 1 and zc == 1:
                        continue
                    fresh[tuple(moved)] = times(weight, pair[side])
            entries = fresh
        return entries

    sums = {}

    def put(zc, low, high, value):
        offset = tuple(b - a for a, b in zip(low, high))
        if offset < (0, 0, 0):
            low, high = high, low
            offset = tuple(-o for o in offset)
        if zc + low[0] > 1 or zc + high[0] > 1:
            return
        key = (offset, zc + low[0], low[1], low[2])
        sums[key] = sums[key] + value if key in sums else value

    for d in range(3):
        dims = [dim for dim in range(3) if dim != d]
        for zc in range(2):
            top = d == 0 and zc == 1
            for q1 in range(2):
                for q2 in range(2):
                    node = [0, 0, 0]
                    node[dims[0]], node[dims[1]] = q1, q2
                    odd = list(node)
                    odd[d] = 1
                    if d == 0:
                        key = (0, zc, node[1], node[2])
                    elif d == 1:
                        key = (1, 2 * zc + node[0], node[2])
                    else:
                        key = (2, 2 * zc + node[0], node[1])
                    _, _, s, h, k = lines[key]

                    def raised_corner(corner):
                        moved = list(corner)
                        moved[d] = 1
                        return tuple(moved)

                    zero = (0, 0, 0)
                    if not (q1 or q2):
                        put(zc, zero, zero, s)
                        if not top:
                            up = raised_corner(zero)
                            put(zc, up, up, s)
                            put(zc, zero, up, -s)
                        continue
                    alpha = transverse(d, zc, node, None)
                    beta = transverse(d, zc, odd, None)
                    corners = list(alpha)
                    delta = {t: minus(alpha[t], beta[t]) for t in corners}
                    for i, t in enumerate(corners):
                        s_alpha, h_delta = s * alpha[t], h * delta[t]
                        for u in corners[i:]:
                            put(zc, t, u, s_alpha * alpha[u] + h_delta * delta[u])
                    if top:
                        continue
                    gamma = transverse(d, zc, node, d)
                    epsilon = {t: minus(gamma[t], beta[t]) for t in corners}
                    for i, t in enumerate(corners):
                        s_gamma, k_epsilon = s * gamma[t], k * epsilon[t]
                        for u in corners[i:]:
                            put(zc, raised_corner(t), raised_corner(u), s_gamma * gamma[u] + k_epsilon * epsilon[u])
                    waiting = hold is not None and d == 1
                    for t in corners:
                        s_delta, s_beta = s * delta[t], s * beta[t]
                        if waiting:
                            factors[zc, q1, q2, t] = s_beta
                            s_beta = jnp.where(hold, 0.0, s_beta)
                        for u in corners:
                            put(zc, t, raised_corner(u), -(s_delta * beta[u] + s_beta * gamma[u]))

    operator = {}
    keys = sorted({(offset, z) for offset, z, _, _ in sums})
    for offset, z in keys:
        total = None
        for ax in range(2):
            part = sums.get((offset, z, ax, 0))
            side = sums.get((offset, z, ax, 1))
            if side is not None:
                side = shifted(side, 0, -1)
                part = side if part is None else part + side
            if part is None:
                continue
            part = shifted(part, -ax, 0)
            total = part if total is None else total + part
        operator[offset, z] = dropped(total, *offset[1:], masks)
        if offset != (0, 0, 0):
            mirror = tuple(-o for o in offset)
            operator[mirror, z + offset[0]] = dropped(shifted(total, -offset[1], -offset[2]), *mirror[1:], masks)

    chain = [
        [lines[0, z, 0, 0][2] for z in range(2)],
        [lines[1, 2 * z, 0][2] for z in range(2)],
        [lines[2, 2 * z, 0][2] for z in range(2)],
    ]
    return operator, chain, factors


reaches = ((-1, -1), (0, -1), (0, 0), (0, 1), (1, 0), (1, 1))


def taken(offset):
    return [(m, offset + 1 if m == -1 else offset) for m in (-1, 0, 1) if m * offset != -1]


def from_below(j, o):
    return (j, o) in ((-1, -1), (0, 0), (0, 1))


def reaching(j, o, source, odd):
    if (j, o) == (0, 1):
        return jnp.where(odd, 0.0, source)
    if (j, o) == (1, 0):
        return jnp.where(odd, source, 0.0)
    return source


def second_operator(operator, chain, rows, lanes, hold=None):
    odd = {1: rows % 2 == 1, 2: lanes % 2 == 1}
    depth = line_terms(chain[0][0], chain[0][1])[0]
    down, up = {}, {}
    for d in (1, 2):
        for z in range(2):
            here = chain[d][z]
            before = shifted(here, -int(d == 1), -int(d == 2))
            f, g = line_terms(before, here)[:2]
            down[d, z] = jnp.where(odd[d], f, 1.0)
            up[d, z] = jnp.where(odd[d], g, 1.0)
    down_z = {0: down[1, 0], 1: down[1, 1] * depth}
    up_z = {0: up[1, 0], 1: up[1, 1] * depth}

    def factors(d, lower, upper):
        base = {}
        for j, o in reaches:
            source = lower if from_below(j, o) else upper
            source = reaching(j, o, shifted(source, o if d == 1 else 0, o if d == 2 else 0), odd[d])
            if hold is not None and d == 1 and (j, o) == (1, 1):
                source = jnp.where(hold, 0.0, source)
            base[j, o] = source
        return {
            (j, o, across): shifted(base[j, o], 0 if d == 1 else across, across if d == 1 else 0)
            for j, o in reaches
            for across in (-1, 0, 1)
        }

    spread = {}
    for far in range(2):
        along_x = factors(1, down_z[far], up_z[far])
        along_y = factors(2, down[2, far], up[2, far])
        for jx, ox in reaches:
            for jy, oy in reaches:
                weight = along_x[jx, ox, oy] * along_y[jy, oy, ox]
                for z in range(2):
                    term = operator[(far - z, ox, oy), z] * weight
                    key = (z, jx, jy)
                    spread[key] = spread[key] + term if key in spread else term

    sides = {
        (z, d): {-1: up_z[z] if d == 1 else up[2, z], 0: depth if (d == 1 and z == 1) else None, 1: down_z[z] if d == 1 else down[2, z]}
        for z in range(2)
        for d in (1, 2)
    }
    own = {(z, mx, my): times(sides[z, 1][mx], sides[z, 2][my]) for z in range(2) for mx in (-1, 0, 1) for my in (-1, 0, 1)}

    results = {}
    for ox in (-1, 0, 1):
        for oy in (-1, 0, 1):
            total = None
            for my, jy in taken(oy):
                part = None
                for mx, jx in taken(ox):
                    term = times(own[0, mx, my], spread[0, jx, jy]) + times(own[1, mx, my], spread[1, jx, jy])
                    term = shifted(term, mx, 0)
                    part = term if part is None else part + term
                part = shifted(part, 0, my)
                total = part if total is None else total + part
            results[ox, oy] = total
    return results, own


def couplings_kernel(inputs_ref, own_ref, near_ref, far_ref):
    odd_y = lax.axis_index("gy") % 2 == 1
    lanes = lax.broadcasted_iota(jnp.int32, (ROWS, LANES), 1)
    low = jnp.zeros((ROWS, LANES), jnp.float32)
    high = jnp.zeros((ROWS, LANES), jnp.float32)
    eps = [permittivity(inputs_ref[0, z] & 3) for z in range(4)]
    for r in range(12):
        values = (inputs_ref[r // 4, r % 4] >> 2).astype(jnp.float32) / 64.0 * eps[r % 4]
        own_ref[r] = values
        turned = pltpu.roll(values, 4 * r + 4, 1)
        low = jnp.where((lanes >= 4 * r) & (lanes < 4 * r + 4), turned, low)
        high = jnp.where(lanes == 4 * r + 4, turned, high)
    far_ref[...] = jnp.where(odd_y, low, high)
    near_ref[...] = jnp.where(odd_y, high, low)


def beside(near_ref, far_ref):
    odd_y = lax.axis_index("gy") % 2 == 1
    far, near = far_ref[...], near_ref[...]
    return jnp.where(odd_y, near, far), jnp.where(odd_y, far, near)


def edges_kernel(own_ref, near_columns_ref, far_columns_ref, far_ref, near_ref):
    odd_x = lax.axis_index("gx") % 2 == 1
    tiles = [own_ref[r] for r in range(12)] + list(beside(near_columns_ref, far_columns_ref))
    for r, values in enumerate(tiles):
        far_ref[r] = jnp.where(odd_x, values[4:8, :], values[0:4, :])
        near_ref[r] = jnp.where(odd_x, values[0:4, :], values[4:8, :])


def lane_picks(lanes):
    source = ((lanes + 2) % LANES // 2 * 4 + 2 * (lanes % 2)) % LANES
    return source, (2 * lanes) % LANES, (lanes >= 126) | (lanes == 64), lanes >= 126


def columns_beside(left, right, lanes, source):
    above = pick_lanes(right, (2 * lanes + 4) % LANES)
    even = jnp.where((lanes >= 64) & (lanes < 112), above, pick_lanes(left, source))
    return even, pick_lanes(left, (source + 1) % LANES)


def split_lanes(values, r, edges, picks):
    _, even_lanes, at_even, at_odd = picks
    even = jnp.where(at_even, shifted(edges[0], 0, 2 * r), pick_lanes(values, even_lanes))
    odd = jnp.where(at_odd, shifted(edges[1], 0, 2 * r), pick_lanes(values, even_lanes + 1))
    return even, odd


def split_couplings(block, lanes):
    picks = lane_picks(lanes)
    c = [[[[None, None], [None, None]] for _ in range(4)] for _ in range(3)]
    for px in range(2):
        left = block[12, pl.ds(px, 8, stride=2), :]
        right = block[13, pl.ds(px, 8, stride=2), :]
        edges = columns_beside(left, right, lanes, picks[0])
        for r in range(12):
            values = block[r, pl.ds(px, 8, stride=2), :]
            c[r // 4][r % 4][px][:] = split_lanes(values, r, edges, picks)
    return c


def places():
    rows = lax.broadcasted_iota(jnp.int32, (ROWS, LANES), 0)
    lanes = lax.broadcasted_iota(jnp.int32, (ROWS, LANES), 1)
    last_x = lax.axis_index("gx") == lax.axis_size("gx") - 1
    last_y = lax.axis_index("gy") == lax.axis_size("gy") - 1
    return rows, lanes, last_x, last_y


def operators(block, first_ref, second_ref, hold_row=None):
    rows, lanes, last_x, last_y = places()
    hold = None if hold_row is None else rows == hold_row
    c = split_couplings(block, lanes)
    operator, chain, factors = first_operator(c, edge_masks(last_x, last_y, rows, lanes, 1), hold)
    empty = jnp.zeros((ROWS, LANES), jnp.float32)
    full = {}
    for o in range(27):
        offset = (o // 9 - 1, o // 3 % 3 - 1, o % 3 - 1)
        for z in range(2):
            full[offset, z] = operator.get((offset, z), empty)
            first_ref[o // 9, o % 9, z] = full[offset, z][0:4, 0:64]
    results, own = second_operator(full, chain, rows, lanes, hold)
    masks = edge_masks(last_x, last_y, rows, lanes, 2)
    second_ref[...] = jnp.zeros(second_ref.shape, jnp.float32)
    for (ox, oy), values in results.items():
        compact = pick_lanes(dropped(values, ox, oy, masks), (2 * lanes) % LANES)
        second_ref[9 + (ox + 1) * 3 + oy + 1, 0, 0:1, :] = compact[0:1, 0:32]
        second_ref[9 + (ox + 1) * 3 + oy + 1, 0, 1:2, :] = compact[2:3, 0:32]
    return operator, factors, own


fix_entries = [((oz, 1, oy), z) for z in (0, 1) for oz in (-z, 1 - z) for oy in (-1, 0, 1)]
fix_factors = [
    (zc, qz, qy, (tz, 0, ty))
    for zc in (0, 1)
    for qz in (0, 1)
    for qy in (0, 1)
    if qz or qy
    for tz in range(1 + (qz if zc == 0 else 0))
    for ty in range(1 + qy)
]
fix_sides = [(z, 1, my) for z in (0, 1) for my in (-1, 0, 1)]
fix_count = len(fix_entries) + len(fix_factors) + len(fix_sides)


def early_kernel(own_ref, near_columns_ref, far_columns_ref, far_ref, first_ref, second_ref, kept_ref, block):
    tiles = [own_ref[r] for r in range(12)] + list(beside(near_columns_ref, far_columns_ref))
    for r, values in enumerate(tiles):
        block[r, 0:8, :] = values
        block[r, 8:12, :] = jnp.zeros((4, LANES), jnp.float32)
        block[r, 12:16, :] = far_ref[r]
    operator, factors, own = operators(block, first_ref, second_ref, ROWS // 2 - 1)
    kept = [operator[e] for e in fix_entries] + [factors[e] for e in fix_factors]
    kept += [own[e] for e in fix_sides]
    for i, values in enumerate(kept):
        kept_ref[i] = values


def add_row_above(near_ref, early_second_ref, kept_ref, first_ref, second_ref, send_first):
    rows, lanes, last_x, last_y = places()
    kept = {e: kept_ref[i] for i, e in enumerate(fix_entries + fix_factors + fix_sides)}

    def row(r):
        return jnp.broadcast_to(near_ref[r, 0:1, :], (ROWS, LANES))

    _, even_lanes, at_even, at_odd = lane_picks(lanes)
    left, right = row(12), row(13)
    in_left = 2 * (lanes % 2)
    c = {}
    for d in (0, 2):
        for z in range(4):
            r = d * 4 + z
            values = row(r)
            below = [pick_lanes(left, in_left + (4 * r + py)) for py in range(2)]
            above = pick_lanes(right, jnp.full((ROWS, LANES), 4 * r + 4, jnp.int32))
            even = jnp.where(at_even, jnp.where(at_odd, below[0], above), pick_lanes(values, even_lanes))
            c[d, z] = (even, jnp.where(at_odd, below[1], pick_lanes(values, even_lanes + 1)))
    line_y = {z: line_terms(*c[2, z]) for z in range(4)}
    line_z = {(zc, py): line_terms(c[0, 2 * zc][py], c[0, 2 * zc + 1][py]) for zc in range(2) for py in range(2)}

    sums = {}
    for zc, qz, qy, t in fix_factors:
        pair_z = line_z[zc, qy][:2] if qz else (None,)
        pair_y = line_y[2 * zc + qz][:2] if qy else (None,)
        for uz in range(1 + (qz if zc == 0 else 0)):
            for uy in range(1 + qy):
                key = ((uz - t[0], 1, uy - t[2]), zc + t[0], t[2])
                term = kept[zc, qz, qy, t] * times(pair_z[uz], pair_y[uy])
                sums[key] = sums[key] + term if key in sums else term
    masks = edge_masks(last_x, last_y, rows, lanes, 1)
    entries = {}
    for offset, z in fix_entries:
        total = kept[offset, z]
        if (offset, z, 0) in sums:
            total = total - sums[offset, z, 0]
        if (offset, z, 1) in sums:
            total = total - shifted(sums[offset, z, 1], 0, -1)
        entries[offset, z] = dropped(total, *offset[1:], masks)
        whole = jnp.where(rows == ROWS // 2 - 1, entries[offset, z], kept[offset, z])
        first_ref[offset[0] + 1, offset[2] + 1, z] = whole[0:4, 0:64]
    for oz, z in ((0, 0), (2, 1)):
        for oy in range(3):
            first_ref[oz, oy, z] = jnp.zeros((4, 64), jnp.float32)
    send_first()

    near_y = {(far, j): shifted(line_y[2 * far][2], 0, j) for far in range(2) for j in (-2, -1, 0, 1)}
    near_z = {(z, j): shifted(line_z[z, 0][2], 0, j) for z in range(2) for j in (-1, 0, 1)}
    odd = lanes % 2 == 1
    spread = {}
    for far in range(2):
        weights = {}
        for oy in (-1, 0, 1):
            f, g = line_terms(near_y[far, oy - 1], near_y[far, oy])[:2]
            there = odd if oy == 0 else ~odd
            pair = jnp.where(there, f, 1.0), jnp.where(there, g, 1.0)
            if far == 1:
                depth = line_terms(near_z[0, oy], near_z[1, oy])[0]
                pair = pair[0] * depth, pair[1] * depth
            weights[oy] = pair
        for jy, oy in reaches:
            weight = reaching(jy, oy, weights[oy][0 if from_below(jy, oy) else 1], odd)
            for z in range(2):
                term = entries[(far - z, 1, oy), z] * weight
                spread[z, jy] = spread[z, jy] + term if (z, jy) in spread else term
    for oy in (-1, 0, 1):
        total = None
        for my, jy in taken(oy):
            part = kept[0, 1, my] * spread[0, jy] + kept[1, 1, my] * spread[1, jy]
            part = pick_lanes(part, (2 * lanes + my) % LANES)
            total = part if total is None else total + part
        total = jnp.where(last_x, 0.0, total)
        if oy == 1:
            total = jnp.where((lanes == LANES // 4 - 1) & last_y, 0.0, total)
        second_ref[oy + 1, 0, 0:1, :] = early_second_ref[16 + oy, 0, 0:1, :]
        row_two = early_second_ref[16 + oy, 0, 1:2, :]
        second_ref[oy + 1, 0, 1:2, :] = row_two + total[ROWS // 2 - 1:ROWS // 2, 0:32]


def last_kernel(
    own_ref, near_columns_ref, far_columns_ref, far_ref, early_first_ref, early_second_ref, kept_ref, near_ref,
    first_hbm, second_hbm, block, first_ref, second_ref, first_fix, second_fix, sems,
):
    odd_x = lax.axis_index("gx") % 2 == 1

    def send(parts):
        copies = [pltpu.make_async_copy(source, target, sems.at[i]) for i, source, target in parts]
        for copy in copies:
            copy.start()
        return copies

    @pl.when(odd_x)
    def _():
        tiles = [own_ref[r] for r in range(12)] + list(beside(near_columns_ref, far_columns_ref))
        for r, values in enumerate(tiles):
            block[r, 0:8, :] = values
            block[r, 8:12, :] = far_ref[r]
            block[r, 12:16, :] = near_ref[r]
        operators(block, first_ref, second_ref)
        for copy in send([(0, first_ref, first_hbm), (1, second_ref, second_hbm)]):
            copy.wait()

    @pl.when(jnp.logical_not(odd_x))
    def _():
        copies = send([
            (0, early_first_ref.at[:, pl.ds(0, 6)], first_hbm.at[:, pl.ds(0, 6)]),
            (1, early_second_ref.at[pl.ds(0, 15)], second_hbm.at[pl.ds(0, 15)]),
            (2, early_second_ref.at[pl.ds(18, 9)], second_hbm.at[pl.ds(18, 9)]),
        ])

        def send_first():
            copies.extend(send([(3, first_fix, first_hbm.at[:, pl.ds(6, 3)])]))

        add_row_above(near_ref, early_second_ref, kept_ref, first_fix, second_fix, send_first)
        for copy in copies + send([(4, second_fix, second_hbm.at[pl.ds(15, 3)])]):
            copy.wait()


def swapped(values, axis, first):
    pairs = [(i, i + 1) for i in range(first, lax.axis_size(axis) - 1, 2)]
    return lax.ppermute(values, axis, pairs + [(b, a) for a, b in pairs])


def body(material, face_open):
    whole = pl.BlockSpec(memory_space=pltpu.VMEM)
    page = jax.ShapeDtypeStruct((ROWS, LANES), jnp.float32)
    edge = jax.ShapeDtypeStruct((14, 4, LANES), jnp.float32)
    small = pltpu.CompilerParams(vmem_limit_bytes=1 << 20)
    own, near, far = pl.pallas_call(
        couplings_kernel,
        out_shape=(jax.ShapeDtypeStruct((12, ROWS, LANES), jnp.float32), page, page),
        in_specs=[whole],
        out_specs=(whole,) * 3,
        compiler_params=small,
        name="couplings",
    )(face_open * 4 + material[None])
    near_columns = swapped(near, "gy", 0)
    far_columns = swapped(far, "gy", 1)
    far, near = pl.pallas_call(
        edges_kernel,
        out_shape=(edge, edge),
        in_specs=[whole] * 3,
        out_specs=(whole,) * 2,
        compiler_params=small,
        name="edges",
    )(own, near_columns, far_columns)
    far_rows = swapped(far, "gx", 1)
    near_rows = swapped(near, "gx", 0)
    first = jax.ShapeDtypeStruct((3, 9, 2, 4, 64), jnp.float32)
    second = jax.ShapeDtypeStruct((27, 1, 2, 32), jnp.float32)
    large = pltpu.CompilerParams(vmem_limit_bytes=3 << 20)
    block = pltpu.VMEM((14, 16, LANES), jnp.float32)
    early = pl.pallas_call(
        early_kernel,
        out_shape=(first, second, jax.ShapeDtypeStruct((fix_count, ROWS, LANES), jnp.float32)),
        in_specs=[whole] * 4,
        out_specs=(whole,) * 3,
        scratch_shapes=[block],
        compiler_params=large,
        cost_estimate=pl.CostEstimate(flops=3 << 20, bytes_accessed=1 << 20, transcendentals=0),
        name="early",
    )(own, near_columns, far_columns, far_rows)
    first_level, second_level = pl.pallas_call(
        last_kernel,
        out_shape=(first, second),
        in_specs=[whole] * 8,
        out_specs=(pl.BlockSpec(memory_space=pltpu.HBM),) * 2,
        scratch_shapes=[
            block,
            pltpu.VMEM(first.shape, jnp.float32),
            pltpu.VMEM(second.shape, jnp.float32),
            pltpu.VMEM((3, 3, 2, 4, 64), jnp.float32),
            pltpu.VMEM((3, 1, 2, 32), jnp.float32),
            pltpu.SemaphoreType.DMA((5,)),
        ],
        compiler_params=large,
        name="last",
    )(own, near_columns, far_columns, far_rows, *early, near_rows)
    return first_level.reshape(27, 2, 4, 64), second_level


def solution(mesh):
    placed = (P(None, "gx", "gy"), P(None, None, "gx", "gy"))
    return jax.shard_map(
        body,
        mesh=mesh,
        in_specs=placed,
        out_specs=(P(None, None, "gx", "gy"), P(None, None, "gx", "gy")),
        check_vma=False,
    )
```

```python
import functools

import jax
import jax.numpy as jnp
import numpy as np
from jax import lax
from jax.experimental import pallas as pl
from jax.experimental.pallas import tpu as pltpu
from jax.sharding import PartitionSpec as P

permit_levels = (1.0 / 80.0, 4.0 / 80.0, 20.0 / 80.0, 1.0)

ROWS, LANES = 8, 128


def permittivity(material):
    values = jnp.zeros(material.shape, jnp.float32)
    for material_id in range(4):
        values = values + jnp.where(material == material_id, permit_levels[material_id], 0.0)
    return values


def shifted(values, by_x, by_y):
    if by_x:
        values = pltpu.roll(values, (-by_x) % ROWS, 0)
    if by_y:
        values = pltpu.roll(values, (-by_y) % LANES, 1)
    return values


def pick_lanes(values, index):
    return jnp.take_along_axis(values, index, axis=1)


def times(a, b):
    if a is None:
        return b
    if b is None:
        return a
    return a * b


def minus(a, b):
    return (1.0 if a is None else a) - (1.0 if b is None else b)


def line_terms(lower, upper):
    total = lower + upper
    inverse = 1.0 / jnp.where(total > 0.0, total, 1.0)
    f = lower * inverse
    g = upper * inverse
    return f, g, lower * g, lower * f, upper * g


def edge_masks(last_x, last_y, rows, lanes, step):
    return (rows == ROWS // 2 - step) & last_x, (lanes == LANES // 2 - step) & last_y


def dropped(values, offset_x, offset_y, masks):
    if offset_x == 1:
        values = jnp.where(masks[0], 0.0, values)
    if offset_y == 1:
        values = jnp.where(masks[1], 0.0, values)
    return values


def first_operator(c, masks, hold=None):
    factors = {}
    lines = {}
    for z in range(4):
        for p in range(2):
            lines[1, z, p] = line_terms(c[1][z][0][p], c[1][z][1][p])
            lines[2, z, p] = line_terms(c[2][z][p][0], c[2][z][p][1])
    for zc in range(2):
        for px in range(2):
            for py in range(2):
                lines[0, zc, px, py] = line_terms(c[0][2 * zc][px][py], c[0][2 * zc + 1][px][py])

    rolled = {}

    def fraction(dim, zc, node, raised):
        pz, px, py = node
        if raised == 0:
            zc, raised = zc + 1, None
        if dim == 0:
            key = (0, zc, px, py)
        elif dim == 1:
            key = (1, 2 * zc + pz, py)
        else:
            key = (2, 2 * zc + pz, px)
        if raised is None:
            return lines[key][:2]
        if (key, raised) not in rolled:
            f = shifted(lines[key][0], int(raised == 1), int(raised == 2))
            rolled[key, raised] = (f, 1.0 - f)
        return rolled[key, raised]

    def transverse(d, zc, node, raised):
        dims = [dim for dim in range(3) if dim != d]
        entries = {(0, 0, 0): None}
        for dim in dims:
            if not node[dim]:
                continue
            pair = fraction(dim, zc, node, raised)
            fresh = {}
            for corner, weight in entries.items():
                for side in range(2):
                    moved = list(corner)
                    moved[dim] = side
                    if dim == 0 and side == 1 and zc == 1:
                        continue
                    fresh[tuple(moved)] = times(weight, pair[side])
            entries = fresh
        return entries

    sums = {}

    def put(zc, low, high, value):
        offset = tuple(b - a for a, b in zip(low, high))
        if offset < (0, 0, 0):
            low, high = high, low
            offset = tuple(-o for o in offset)
        if zc + low[0] > 1 or zc + high[0] > 1:
            return
        key = (offset, zc + low[0], low[1], low[2])
        sums[key] = sums[key] + value if key in sums else value

    for d in range(3):
        dims = [dim for dim in range(3) if dim != d]
        for zc in range(2):
            top = d == 0 and zc == 1
            for q1 in range(2):
                for q2 in range(2):
                    node = [0, 0, 0]
                    node[dims[0]], node[dims[1]] = q1, q2
                    odd = list(node)
                    odd[d] = 1
                    if d == 0:
                        key = (0, zc, node[1], node[2])
                    elif d == 1:
                        key = (1, 2 * zc + node[0], node[2])
                    else:
                        key = (2, 2 * zc + node[0], node[1])
                    _, _, s, h, k = lines[key]

                    def raised_corner(corner):
                        moved = list(corner)
                        moved[d] = 1
                        return tuple(moved)

                    zero = (0, 0, 0)
                    if not (q1 or q2):
                        put(zc, zero, zero, s)
                        if not top:
                            up = raised_corner(zero)
                            put(zc, up, up, s)
                            put(zc, zero, up, -s)
                        continue
                    alpha = transverse(d, zc, node, None)
                    beta = transverse(d, zc, odd, None)
                    corners = list(alpha)
                    delta = {t: minus(alpha[t], beta[t]) for t in corners}
                    for i, t in enumerate(corners):
                        s_alpha, h_delta = s * alpha[t], h * delta[t]
                        for u in corners[i:]:
                            put(zc, t, u, s_alpha * alpha[u] + h_delta * delta[u])
                    if top:
                        continue
                    gamma = transverse(d, zc, node, d)
                    epsilon = {t: minus(gamma[t], beta[t]) for t in corners}
                    for i, t in enumerate(corners):
                        s_gamma, k_epsilon = s * gamma[t], k * epsilon[t]
                        for u in corners[i:]:
                            put(zc, raised_corner(t), raised_corner(u), s_gamma * gamma[u] + k_epsilon * epsilon[u])
                    waiting = hold is not None and d == 1
                    for t in corners:
                        s_delta, s_beta = s * delta[t], s * beta[t]
                        if waiting:
                            factors[zc, q1, q2, t] = s_beta
                            s_beta = jnp.where(hold, 0.0, s_beta)
                        for u in corners:
                            put(zc, t, raised_corner(u), -(s_delta * beta[u] + s_beta * gamma[u]))

    operator = {}
    keys = sorted({(offset, z) for offset, z, _, _ in sums})
    for offset, z in keys:
        total = None
        for ax in range(2):
            part = sums.get((offset, z, ax, 0))
            side = sums.get((offset, z, ax, 1))
            if side is not None:
                side = shifted(side, 0, -1)
                part = side if part is None else part + side
            if part is None:
                continue
            part = shifted(part, -ax, 0)
            total = part if total is None else total + part
        operator[offset, z] = dropped(total, *offset[1:], masks)
        if offset != (0, 0, 0):
            mirror = tuple(-o for o in offset)
            operator[mirror, z + offset[0]] = dropped(shifted(total, -offset[1], -offset[2]), *mirror[1:], masks)

    chain = [
        [lines[0, z, 0, 0][2] for z in range(2)],
        [lines[1, 2 * z, 0][2] for z in range(2)],
        [lines[2, 2 * z, 0][2] for z in range(2)],
    ]
    return operator, chain, factors


reaches = ((-1, -1), (0, -1), (0, 0), (0, 1), (1, 0), (1, 1))


def taken(offset):
    return [(m, offset + 1 if m == -1 else offset) for m in (-1, 0, 1) if m * offset != -1]


def from_below(j, o):
    return (j, o) in ((-1, -1), (0, 0), (0, 1))


def reaching(j, o, source, odd):
    if (j, o) == (0, 1):
        return jnp.where(odd, 0.0, source)
    if (j, o) == (1, 0):
        return jnp.where(odd, source, 0.0)
    return source


def second_operator(operator, chain, rows, lanes, hold=None):
    odd = {1: rows % 2 == 1, 2: lanes % 2 == 1}
    depth = line_terms(chain[0][0], chain[0][1])[0]
    down, up = {}, {}
    for d in (1, 2):
        for z in range(2):
            here = chain[d][z]
            before = shifted(here, -int(d == 1), -int(d == 2))
            f, g = line_terms(before, here)[:2]
            down[d, z] = jnp.where(odd[d], f, 1.0)
            up[d, z] = jnp.where(odd[d], g, 1.0)
    down_z = {0: down[1, 0], 1: down[1, 1] * depth}
    up_z = {0: up[1, 0], 1: up[1, 1] * depth}

    def factors(d, lower, upper):
        base = {}
        for j, o in reaches:
            source = lower if from_below(j, o) else upper
            source = reaching(j, o, shifted(source, o if d == 1 else 0, o if d == 2 else 0), odd[d])
            if hold is not None and d == 1 and (j, o) == (1, 1):
                source = jnp.where(hold, 0.0, source)
            base[j, o] = source
        return {
            (j, o, across): shifted(base[j, o], 0 if d == 1 else across, across if d == 1 else 0)
            for j, o in reaches
            for across in (-1, 0, 1)
        }

    spread = {}
    for far in range(2):
        along_x = factors(1, down_z[far], up_z[far])
        along_y = factors(2, down[2, far], up[2, far])
        for jx, ox in reaches:
            for jy, oy in reaches:
                weight = along_x[jx, ox, oy] * along_y[jy, oy, ox]
                for z in range(2):
                    term = operator[(far - z, ox, oy), z] * weight
                    key = (z, jx, jy)
                    spread[key] = spread[key] + term if key in spread else term

    sides = {
        (z, d): {-1: up_z[z] if d == 1 else up[2, z], 0: depth if (d == 1 and z == 1) else None, 1: down_z[z] if d == 1 else down[2, z]}
        for z in range(2)
        for d in (1, 2)
    }
    own = {(z, mx, my): times(sides[z, 1][mx], sides[z, 2][my]) for z in range(2) for mx in (-1, 0, 1) for my in (-1, 0, 1)}

    results = {}
    for ox in (-1, 0, 1):
        for oy in (-1, 0, 1):
            total = None
            for my, jy in taken(oy):
                part = None
                for mx, jx in taken(ox):
                    term = times(own[0, mx, my], spread[0, jx, jy]) + times(own[1, mx, my], spread[1, jx, jy])
                    term = shifted(term, mx, 0)
                    part = term if part is None else part + term
                part = shifted(part, 0, my)
                total = part if total is None else total + part
            results[ox, oy] = total
    return results, own


def swap_order(row, edge, half, where):
    below_half, inner, at_half = (where(test, 1, 0) for test in (edge < half, row > 0, edge == half))
    cores_first, border = inner * below_half, inner * at_half
    order = cores_first * (edge % 2) + (1 - cores_first) * (1 - edge % 2)
    return border * 2 + (1 - border) * order


def own_swaps():
    row, column, size = lax.axis_index("gx"), lax.axis_index("gy"), lax.axis_size("gy")

    def order(edge):
        return swap_order(row, edge, size // 2, jnp.where)

    return jnp.where(column > 0, order(column - 1 + (column == 0)), -1), jnp.where(column < size - 1, order(column), -1)


def couplings_kernel(inputs_ref, own_ref, *message_refs):
    lanes = lax.broadcasted_iota(jnp.int32, (ROWS, LANES), 1)
    low = jnp.zeros((ROWS, LANES), jnp.float32)
    high = jnp.zeros((ROWS, LANES), jnp.float32)
    eps = [permittivity(inputs_ref[0, z] & 3) for z in range(4)]
    for r in range(12):
        values = (inputs_ref[r // 4, r % 4] >> 2).astype(jnp.float32) / 64.0 * eps[r % 4]
        own_ref[r] = values
        turned = pltpu.roll(values, 4 * r + 4, 1)
        low = jnp.where((lanes >= 4 * r) & (lanes < 4 * r + 4), turned, low)
        high = jnp.where(lanes == 4 * r + 4, turned, high)
    _, above = own_swaps()
    for k, ref in enumerate(message_refs):
        ref[...] = jnp.where(above == k, low, high)


def beside(column_refs):
    sides = []
    for swap in own_swaps():
        values = jnp.zeros((ROWS, LANES), jnp.float32)
        for k, ref in enumerate(column_refs):
            values = jnp.where(swap == k, ref[...], values)
        sides.append(values)
    return sides


def edges_kernel(own_ref, first_columns_ref, second_columns_ref, third_columns_ref, far_ref, near_ref):
    odd_x = lax.axis_index("gx") % 2 == 1
    tiles = [own_ref[r] for r in range(12)] + beside((first_columns_ref, second_columns_ref, third_columns_ref))
    for r, values in enumerate(tiles):
        far_ref[r] = jnp.where(odd_x, values[4:8, :], values[0:4, :])
        near_ref[r] = jnp.where(odd_x, values[0:4, :], values[4:8, :])


def lane_picks(lanes):
    source = ((lanes + 2) % LANES // 2 * 4 + 2 * (lanes % 2)) % LANES
    return source, (2 * lanes) % LANES, (lanes >= 126) | (lanes == 64), lanes >= 126


def columns_beside(left, right, lanes, source):
    above = pick_lanes(right, (2 * lanes + 4) % LANES)
    even = jnp.where((lanes >= 64) & (lanes < 112), above, pick_lanes(left, source))
    return even, pick_lanes(left, (source + 1) % LANES)


def split_lanes(values, r, edges, picks):
    _, even_lanes, at_even, at_odd = picks
    even = jnp.where(at_even, shifted(edges[0], 0, 2 * r), pick_lanes(values, even_lanes))
    odd = jnp.where(at_odd, shifted(edges[1], 0, 2 * r), pick_lanes(values, even_lanes + 1))
    return even, odd


def split_couplings(block, lanes):
    picks = lane_picks(lanes)
    c = [[[[None, None], [None, None]] for _ in range(4)] for _ in range(3)]
    for px in range(2):
        left = block[12, pl.ds(px, 8, stride=2), :]
        right = block[13, pl.ds(px, 8, stride=2), :]
        edges = columns_beside(left, right, lanes, picks[0])
        for r in range(12):
            values = block[r, pl.ds(px, 8, stride=2), :]
            c[r // 4][r % 4][px][:] = split_lanes(values, r, edges, picks)
    return c


def places():
    rows = lax.broadcasted_iota(jnp.int32, (ROWS, LANES), 0)
    lanes = lax.broadcasted_iota(jnp.int32, (ROWS, LANES), 1)
    last_x = lax.axis_index("gx") == lax.axis_size("gx") - 1
    last_y = lax.axis_index("gy") == lax.axis_size("gy") - 1
    return rows, lanes, last_x, last_y


def operators(block, first_ref, second_ref, hold_row=None):
    rows, lanes, last_x, last_y = places()
    hold = None if hold_row is None else rows == hold_row
    c = split_couplings(block, lanes)
    operator, chain, factors = first_operator(c, edge_masks(last_x, last_y, rows, lanes, 1), hold)
    empty = jnp.zeros((ROWS, LANES), jnp.float32)
    full = {}
    for o in range(27):
        offset = (o // 9 - 1, o // 3 % 3 - 1, o % 3 - 1)
        for z in range(2):
            full[offset, z] = operator.get((offset, z), empty)
            first_ref[o // 9, o % 9, z] = full[offset, z][0:4, 0:64]
    results, own = second_operator(full, chain, rows, lanes, hold)
    masks = edge_masks(last_x, last_y, rows, lanes, 2)
    second_ref[...] = jnp.zeros(second_ref.shape, jnp.float32)
    for (ox, oy), values in results.items():
        compact = pick_lanes(dropped(values, ox, oy, masks), (2 * lanes) % LANES)
        second_ref[9 + (ox + 1) * 3 + oy + 1, 0, 0:1, :] = compact[0:1, 0:32]
        second_ref[9 + (ox + 1) * 3 + oy + 1, 0, 1:2, :] = compact[2:3, 0:32]
    return operator, factors, own


fix_entries = [((oz, 1, oy), z) for z in (0, 1) for oz in (-z, 1 - z) for oy in (-1, 0, 1)]
fix_factors = [
    (zc, qz, qy, (tz, 0, ty))
    for zc in (0, 1)
    for qz in (0, 1)
    for qy in (0, 1)
    if qz or qy
    for tz in range(1 + (qz if zc == 0 else 0))
    for ty in range(1 + qy)
]
fix_sides = [(z, 1, my) for z in (0, 1) for my in (-1, 0, 1)]
fix_count = len(fix_entries) + len(fix_factors) + len(fix_sides)


def early_kernel(
    own_ref, first_columns_ref, second_columns_ref, third_columns_ref, far_ref,
    first_ref, second_ref, kept_ref, block,
):
    tiles = [own_ref[r] for r in range(12)] + beside((first_columns_ref, second_columns_ref, third_columns_ref))
    for r, values in enumerate(tiles):
        block[r, 0:8, :] = values
        block[r, 8:12, :] = jnp.zeros((4, LANES), jnp.float32)
        block[r, 12:16, :] = far_ref[r]
    operator, factors, own = operators(block, first_ref, second_ref, ROWS // 2 - 1)
    kept = [operator[e] for e in fix_entries] + [factors[e] for e in fix_factors]
    kept += [own[e] for e in fix_sides]
    for i, values in enumerate(kept):
        kept_ref[i] = values


def add_row_above(near_ref, early_second_ref, kept_ref, first_ref, second_ref, send_first):
    rows, lanes, last_x, last_y = places()
    kept = {e: kept_ref[i] for i, e in enumerate(fix_entries + fix_factors + fix_sides)}

    def row(r):
        return jnp.broadcast_to(near_ref[r, 0:1, :], (ROWS, LANES))

    _, even_lanes, at_even, at_odd = lane_picks(lanes)
    left, right = row(12), row(13)
    in_left = 2 * (lanes % 2)
    c = {}
    for d in (0, 2):
        for z in range(4):
            r = d * 4 + z
            values = row(r)
            below = [pick_lanes(left, in_left + (4 * r + py)) for py in range(2)]
            above = pick_lanes(right, jnp.full((ROWS, LANES), 4 * r + 4, jnp.int32))
            even = jnp.where(at_even, jnp.where(at_odd, below[0], above), pick_lanes(values, even_lanes))
            c[d, z] = (even, jnp.where(at_odd, below[1], pick_lanes(values, even_lanes + 1)))
    line_y = {z: line_terms(*c[2, z]) for z in range(4)}
    line_z = {(zc, py): line_terms(c[0, 2 * zc][py], c[0, 2 * zc + 1][py]) for zc in range(2) for py in range(2)}

    sums = {}
    for zc, qz, qy, t in fix_factors:
        pair_z = line_z[zc, qy][:2] if qz else (None,)
        pair_y = line_y[2 * zc + qz][:2] if qy else (None,)
        for uz in range(1 + (qz if zc == 0 else 0)):
            for uy in range(1 + qy):
                key = ((uz - t[0], 1, uy - t[2]), zc + t[0], t[2])
                term = kept[zc, qz, qy, t] * times(pair_z[uz], pair_y[uy])
                sums[key] = sums[key] + term if key in sums else term
    masks = edge_masks(last_x, last_y, rows, lanes, 1)
    entries = {}
    for offset, z in fix_entries:
        total = kept[offset, z]
        if (offset, z, 0) in sums:
            total = total - sums[offset, z, 0]
        if (offset, z, 1) in sums:
            total = total - shifted(sums[offset, z, 1], 0, -1)
        entries[offset, z] = dropped(total, *offset[1:], masks)
        whole = jnp.where(rows == ROWS // 2 - 1, entries[offset, z], kept[offset, z])
        first_ref[offset[0] + 1, offset[2] + 1, z] = whole[0:4, 0:64]
    for oz, z in ((0, 0), (2, 1)):
        for oy in range(3):
            first_ref[oz, oy, z] = jnp.zeros((4, 64), jnp.float32)
    send_first()

    near_y = {(far, j): shifted(line_y[2 * far][2], 0, j) for far in range(2) for j in (-2, -1, 0, 1)}
    near_z = {(z, j): shifted(line_z[z, 0][2], 0, j) for z in range(2) for j in (-1, 0, 1)}
    odd = lanes % 2 == 1
    spread = {}
    for far in range(2):
        weights = {}
        for oy in (-1, 0, 1):
            f, g = line_terms(near_y[far, oy - 1], near_y[far, oy])[:2]
            there = odd if oy == 0 else ~odd
            pair = jnp.where(there, f, 1.0), jnp.where(there, g, 1.0)
            if far == 1:
                depth = line_terms(near_z[0, oy], near_z[1, oy])[0]
                pair = pair[0] * depth, pair[1] * depth
            weights[oy] = pair
        for jy, oy in reaches:
            weight = reaching(jy, oy, weights[oy][0 if from_below(jy, oy) else 1], odd)
            for z in range(2):
                term = entries[(far - z, 1, oy), z] * weight
                spread[z, jy] = spread[z, jy] + term if (z, jy) in spread else term
    for oy in (-1, 0, 1):
        total = None
        for my, jy in taken(oy):
            part = kept[0, 1, my] * spread[0, jy] + kept[1, 1, my] * spread[1, jy]
            part = pick_lanes(part, (2 * lanes + my) % LANES)
            total = part if total is None else total + part
        total = jnp.where(last_x, 0.0, total)
        if oy == 1:
            total = jnp.where((lanes == LANES // 4 - 1) & last_y, 0.0, total)
        second_ref[oy + 1, 0, 0:1, :] = early_second_ref[16 + oy, 0, 0:1, :]
        row_two = early_second_ref[16 + oy, 0, 1:2, :]
        second_ref[oy + 1, 0, 1:2, :] = row_two + total[ROWS // 2 - 1:ROWS // 2, 0:32]


def last_kernel(
    own_ref, first_columns_ref, second_columns_ref, third_columns_ref, far_ref,
    early_first_ref, early_second_ref, kept_ref, near_ref,
    first_hbm, second_hbm, block, first_ref, second_ref, first_fix, second_fix, sems,
):
    odd_x = lax.axis_index("gx") % 2 == 1

    def send(parts):
        copies = [pltpu.make_async_copy(source, target, sems.at[i]) for i, source, target in parts]
        for copy in copies:
            copy.start()
        return copies

    @pl.when(odd_x)
    def _():
        tiles = [own_ref[r] for r in range(12)] + beside((first_columns_ref, second_columns_ref, third_columns_ref))
        for r, values in enumerate(tiles):
            block[r, 0:8, :] = values
            block[r, 8:12, :] = far_ref[r]
            block[r, 12:16, :] = near_ref[r]
        operators(block, first_ref, second_ref)
        for copy in send([(0, first_ref, first_hbm), (1, second_ref, second_hbm)]):
            copy.wait()

    @pl.when(jnp.logical_not(odd_x))
    def _():
        copies = send([
            (0, early_first_ref.at[:, pl.ds(0, 6)], first_hbm.at[:, pl.ds(0, 6)]),
            (1, early_second_ref.at[pl.ds(0, 15)], second_hbm.at[pl.ds(0, 15)]),
            (2, early_second_ref.at[pl.ds(18, 9)], second_hbm.at[pl.ds(18, 9)]),
        ])

        def send_first():
            copies.extend(send([(3, first_fix, first_hbm.at[:, pl.ds(6, 3)])]))

        add_row_above(near_ref, early_second_ref, kept_ref, first_fix, second_fix, send_first)
        for copy in copies + send([(4, second_fix, second_hbm.at[pl.ds(15, 3)])]):
            copy.wait()


def swapped(values, axis, first):
    pairs = [(i, i + 1) for i in range(first, lax.axis_size(axis) - 1, 2)]
    return lax.ppermute(values, axis, pairs + [(b, a) for a, b in pairs])


def swapped_columns(values, which):
    count_x, count_y = lax.axis_size("gx"), lax.axis_size("gy")
    pairs = [
        (row * count_y + edge, row * count_y + edge + 1)
        for row in range(count_x)
        for edge in range(count_y - 1)
        if swap_order(row, edge, count_y // 2, np.where) == which
    ]
    return lax.ppermute(values, ("gx", "gy"), pairs + [(b, a) for a, b in pairs])


def body(material, face_open):
    whole = pl.BlockSpec(memory_space=pltpu.VMEM)
    page = jax.ShapeDtypeStruct((ROWS, LANES), jnp.float32)
    edge = jax.ShapeDtypeStruct((14, 4, LANES), jnp.float32)
    small = pltpu.CompilerParams(vmem_limit_bytes=1 << 20)
    own, *messages = pl.pallas_call(
        couplings_kernel,
        out_shape=(jax.ShapeDtypeStruct((12, ROWS, LANES), jnp.float32),) + (page,) * 3,
        in_specs=[whole],
        out_specs=(whole,) * 4,
        compiler_params=small,
        name="couplings",
    )(face_open * 4 + material[None])
    columns = [swapped_columns(message, k) for k, message in enumerate(messages)]
    far, near = pl.pallas_call(
        edges_kernel,
        out_shape=(edge, edge),
        in_specs=[whole] * 4,
        out_specs=(whole,) * 2,
        compiler_params=small,
        name="edges",
    )(own, *columns)
    far_rows = swapped(far, "gx", 1)
    near_rows = swapped(near, "gx", 0)
    first = jax.ShapeDtypeStruct((3, 9, 2, 4, 64), jnp.float32)
    second = jax.ShapeDtypeStruct((27, 1, 2, 32), jnp.float32)
    large = pltpu.CompilerParams(vmem_limit_bytes=3 << 20)
    block = pltpu.VMEM((14, 16, LANES), jnp.float32)
    early = pl.pallas_call(
        early_kernel,
        out_shape=(first, second, jax.ShapeDtypeStruct((fix_count, ROWS, LANES), jnp.float32)),
        in_specs=[whole] * 5,
        out_specs=(whole,) * 3,
        scratch_shapes=[block],
        compiler_params=large,
        cost_estimate=pl.CostEstimate(flops=3 << 20, bytes_accessed=1 << 20, transcendentals=0),
        name="early",
    )(own, *columns, far_rows)
    first_level, second_level = pl.pallas_call(
        last_kernel,
        out_shape=(first, second),
        in_specs=[whole] * 9,
        out_specs=(pl.BlockSpec(memory_space=pltpu.HBM),) * 2,
        scratch_shapes=[
            block,
            pltpu.VMEM(first.shape, jnp.float32),
            pltpu.VMEM(second.shape, jnp.float32),
            pltpu.VMEM((3, 3, 2, 4, 64), jnp.float32),
            pltpu.VMEM((3, 1, 2, 32), jnp.float32),
            pltpu.SemaphoreType.DMA((5,)),
        ],
        compiler_params=large,
        name="last",
    )(own, *columns, far_rows, *early, near_rows)
    return first_level.reshape(27, 2, 4, 64), second_level


def solution(mesh):
    placed = (P(None, "gx", "gy"), P(None, None, "gx", "gy"))
    return jax.shard_map(
        body,
        mesh=mesh,
        in_specs=placed,
        out_specs=(P(None, None, "gx", "gy"), P(None, None, "gx", "gy")),
        check_vma=False,
    )
```

```python
import functools

import jax
import jax.numpy as jnp
import numpy as np
from jax import lax
from jax.experimental import pallas as pl
from jax.experimental.pallas import tpu as pltpu
from jax.sharding import PartitionSpec as P

permit_levels = (1.0 / 80.0 / 64.0, 4.0 / 80.0 / 64.0, 20.0 / 80.0 / 64.0, 1.0 / 64.0)

ROWS, LANES = 8, 128


def permittivity(material):
    values = jnp.full(material.shape, permit_levels[3], jnp.float32)
    for material_id in range(3):
        values = jnp.where(material == material_id, permit_levels[material_id], values)
    return values


def shifted(values, by_x, by_y):
    if by_x:
        values = pltpu.roll(values, (-by_x) % ROWS, 0)
    if by_y:
        values = pltpu.roll(values, (-by_y) % LANES, 1)
    return values


def pick_lanes(values, index):
    return jnp.take_along_axis(values, index, axis=1)


def times(a, b):
    if a is None:
        return b
    if b is None:
        return a
    return a * b


def minus(a, b):
    return (1.0 if a is None else a) - (1.0 if b is None else b)


def line_terms(lower, upper):
    total = lower + upper
    inverse = 1.0 / jnp.where(total > 0.0, total, 1.0)
    f = lower * inverse
    g = upper * inverse
    return f, g, lower * g, lower * f, upper * g


def edge_masks(last_x, last_y, rows, lanes, step):
    return (rows == ROWS // 2 - step) & last_x, (lanes == LANES // 2 - step) & last_y


def dropped(values, offset_x, offset_y, masks):
    if offset_x == 1:
        values = jnp.where(masks[0], 0.0, values)
    if offset_y == 1:
        values = jnp.where(masks[1], 0.0, values)
    return values


def first_operator(c, masks, hold=None):
    factors = {}
    lines = {}
    for z in range(4):
        for p in range(2):
            lines[1, z, p] = line_terms(c[1][z][0][p], c[1][z][1][p])
            lines[2, z, p] = line_terms(c[2][z][p][0], c[2][z][p][1])
    for zc in range(2):
        for px in range(2):
            for py in range(2):
                lines[0, zc, px, py] = line_terms(c[0][2 * zc][px][py], c[0][2 * zc + 1][px][py])

    rolled = {}

    def fraction(dim, zc, node, raised):
        pz, px, py = node
        if raised == 0:
            zc, raised = zc + 1, None
        if dim == 0:
            key = (0, zc, px, py)
        elif dim == 1:
            key = (1, 2 * zc + pz, py)
        else:
            key = (2, 2 * zc + pz, px)
        if raised is None:
            return lines[key][:2]
        if (key, raised) not in rolled:
            f = shifted(lines[key][0], int(raised == 1), int(raised == 2))
            rolled[key, raised] = (f, 1.0 - f)
        return rolled[key, raised]

    def transverse(d, zc, node, raised):
        dims = [dim for dim in range(3) if dim != d]
        entries = {(0, 0, 0): None}
        for dim in dims:
            if not node[dim]:
                continue
            pair = fraction(dim, zc, node, raised)
            fresh = {}
            for corner, weight in entries.items():
                for side in range(2):
                    moved = list(corner)
                    moved[dim] = side
                    if dim == 0 and side == 1 and zc == 1:
                        continue
                    fresh[tuple(moved)] = times(weight, pair[side])
            entries = fresh
        return entries

    sums = {}

    def put(zc, low, high, value):
        offset = tuple(b - a for a, b in zip(low, high))
        if offset < (0, 0, 0):
            low, high = high, low
            offset = tuple(-o for o in offset)
        if zc + low[0] > 1 or zc + high[0] > 1:
            return
        key = (offset, zc + low[0], low[1], low[2])
        sums[key] = sums[key] + value if key in sums else value

    for d in range(3):
        dims = [dim for dim in range(3) if dim != d]
        for zc in range(2):
            top = d == 0 and zc == 1
            for q1 in range(2):
                for q2 in range(2):
                    node = [0, 0, 0]
                    node[dims[0]], node[dims[1]] = q1, q2
                    odd = list(node)
                    odd[d] = 1
                    if d == 0:
                        key = (0, zc, node[1], node[2])
                    elif d == 1:
                        key = (1, 2 * zc + node[0], node[2])
                    else:
                        key = (2, 2 * zc + node[0], node[1])
                    _, _, s, h, k = lines[key]

                    def raised_corner(corner):
                        moved = list(corner)
                        moved[d] = 1
                        return tuple(moved)

                    zero = (0, 0, 0)
                    if not (q1 or q2):
                        put(zc, zero, zero, s)
                        if not top:
                            up = raised_corner(zero)
                            put(zc, up, up, s)
                            put(zc, zero, up, -s)
                        continue
                    alpha = transverse(d, zc, node, None)
                    beta = transverse(d, zc, odd, None)
                    corners = list(alpha)
                    delta = {t: minus(alpha[t], beta[t]) for t in corners}
                    for i, t in enumerate(corners):
                        s_alpha, h_delta = s * alpha[t], h * delta[t]
                        for u in corners[i:]:
                            put(zc, t, u, s_alpha * alpha[u] + h_delta * delta[u])
                    if top:
                        continue
                    gamma = transverse(d, zc, node, d)
                    epsilon = {t: minus(gamma[t], beta[t]) for t in corners}
                    for i, t in enumerate(corners):
                        s_gamma, k_epsilon = s * gamma[t], k * epsilon[t]
                        for u in corners[i:]:
                            put(zc, raised_corner(t), raised_corner(u), s_gamma * gamma[u] + k_epsilon * epsilon[u])
                    waiting = hold is not None and d == 1
                    for t in corners:
                        s_delta, s_beta = s * delta[t], s * beta[t]
                        if waiting:
                            factors[zc, q1, q2, t] = s_beta
                            s_beta = jnp.where(hold, 0.0, s_beta)
                        for u in corners:
                            put(zc, t, raised_corner(u), -(s_delta * beta[u] + s_beta * gamma[u]))

    operator = {}
    keys = sorted({(offset, z) for offset, z, _, _ in sums})
    for offset, z in keys:
        total = None
        for ax in range(2):
            part = sums.get((offset, z, ax, 0))
            side = sums.get((offset, z, ax, 1))
            if side is not None:
                side = shifted(side, 0, -1)
                part = side if part is None else part + side
            if part is None:
                continue
            part = shifted(part, -ax, 0)
            total = part if total is None else total + part
        operator[offset, z] = dropped(total, *offset[1:], masks)
        if offset != (0, 0, 0):
            mirror = tuple(-o for o in offset)
            operator[mirror, z + offset[0]] = dropped(shifted(total, -offset[1], -offset[2]), *mirror[1:], masks)

    chain = [
        [lines[0, z, 0, 0][2] for z in range(2)],
        [lines[1, 2 * z, 0][2] for z in range(2)],
        [lines[2, 2 * z, 0][2] for z in range(2)],
    ]
    return operator, chain, factors


reaches = ((-1, -1), (0, -1), (0, 0), (0, 1), (1, 0), (1, 1))


def taken(offset):
    return [(m, offset + 1 if m == -1 else offset) for m in (-1, 0, 1) if m * offset != -1]


def from_below(j, o):
    return (j, o) in ((-1, -1), (0, 0), (0, 1))


def reaching(j, o, source, odd):
    if (j, o) == (0, 1):
        return jnp.where(odd, 0.0, source)
    if (j, o) == (1, 0):
        return jnp.where(odd, source, 0.0)
    return source


def second_operator(operator, chain, rows, lanes, hold=None):
    odd = {1: rows % 2 == 1, 2: lanes % 2 == 1}
    depth = line_terms(chain[0][0], chain[0][1])[0]
    down, up = {}, {}
    for d in (1, 2):
        for z in range(2):
            here = chain[d][z]
            before = shifted(here, -int(d == 1), -int(d == 2))
            f, g = line_terms(before, here)[:2]
            down[d, z] = jnp.where(odd[d], f, 1.0)
            up[d, z] = jnp.where(odd[d], g, 1.0)
    down_z = {0: down[1, 0], 1: down[1, 1] * depth}
    up_z = {0: up[1, 0], 1: up[1, 1] * depth}

    def factors(d, lower, upper):
        base = {}
        for j, o in reaches:
            source = lower if from_below(j, o) else upper
            source = reaching(j, o, shifted(source, o if d == 1 else 0, o if d == 2 else 0), odd[d])
            if hold is not None and d == 1 and (j, o) == (1, 1):
                source = jnp.where(hold, 0.0, source)
            base[j, o] = source
        return {
            (j, o, across): shifted(base[j, o], 0 if d == 1 else across, across if d == 1 else 0)
            for j, o in reaches
            for across in (-1, 0, 1)
        }

    spread = {}
    for far in range(2):
        along_x = factors(1, down_z[far], up_z[far])
        along_y = factors(2, down[2, far], up[2, far])
        for jx, ox in reaches:
            for jy, oy in reaches:
                weight = along_x[jx, ox, oy] * along_y[jy, oy, ox]
                for z in range(2):
                    term = operator[(far - z, ox, oy), z] * weight
                    key = (z, jx, jy)
                    spread[key] = spread[key] + term if key in spread else term

    sides = {
        (z, d): {-1: up_z[z] if d == 1 else up[2, z], 0: depth if (d == 1 and z == 1) else None, 1: down_z[z] if d == 1 else down[2, z]}
        for z in range(2)
        for d in (1, 2)
    }
    own = {(z, mx, my): times(sides[z, 1][mx], sides[z, 2][my]) for z in range(2) for mx in (-1, 0, 1) for my in (-1, 0, 1)}

    results = {}
    for ox in (-1, 0, 1):
        for oy in (-1, 0, 1):
            total = None
            for my, jy in taken(oy):
                part = None
                for mx, jx in taken(ox):
                    term = times(own[0, mx, my], spread[0, jx, jy]) + times(own[1, mx, my], spread[1, jx, jy])
                    term = shifted(term, mx, 0)
                    part = term if part is None else part + term
                part = shifted(part, 0, my)
                total = part if total is None else total + part
            results[ox, oy] = total
    return results, own


def swap_order(row, edge, half, where):
    below_half, inner, at_half = (where(test, 1, 0) for test in (edge < half, row > 0, edge == half))
    cores_first, border = inner * below_half, inner * at_half
    order = cores_first * (edge % 2) + (1 - cores_first) * (1 - edge % 2)
    return border * 2 + (1 - border) * order


def own_swaps():
    row, column, size = lax.axis_index("gx"), lax.axis_index("gy"), lax.axis_size("gy")

    def order(edge):
        return swap_order(row, edge, size // 2, jnp.where)

    return jnp.where(column > 0, order(column - 1 + (column == 0)), -1), jnp.where(column < size - 1, order(column), -1)


def couplings_kernel(inputs_ref, own_ref, *message_refs):
    lanes = lax.broadcasted_iota(jnp.int32, (ROWS, LANES), 1)
    low = jnp.zeros((ROWS, LANES), jnp.float32)
    high = jnp.zeros((ROWS, LANES), jnp.float32)
    eps = [permittivity(inputs_ref[0, z] & 3) for z in range(4)]
    for r in range(12):
        values = (inputs_ref[r // 4, r % 4] >> 2).astype(jnp.float32) * eps[r % 4]
        own_ref[r] = values
        turned = pltpu.roll(values, 4 * r + 4, 1)
        low = jnp.where((lanes >= 4 * r) & (lanes < 4 * r + 4), turned, low)
        high = jnp.where(lanes == 4 * r + 4, turned, high)
    _, above = own_swaps()
    for k, ref in enumerate(message_refs):
        ref[...] = jnp.where(above == k, low, high)


def beside(column_refs):
    sides = []
    for swap in own_swaps():
        values = jnp.zeros((ROWS, LANES), jnp.float32)
        for k, ref in enumerate(column_refs):
            values = jnp.where(swap == k, ref[...], values)
        sides.append(values)
    return sides


def edges_kernel(own_ref, first_columns_ref, second_columns_ref, third_columns_ref, far_ref, near_ref):
    odd_x = lax.axis_index("gx") % 2 == 1
    tiles = [own_ref[r] for r in range(12)] + beside((first_columns_ref, second_columns_ref, third_columns_ref))
    for r, values in enumerate(tiles):
        far_ref[r] = jnp.where(odd_x, values[4:8, :], values[0:4, :])
        near_ref[r] = jnp.where(odd_x, values[0:4, :], values[4:8, :])


def lane_picks(lanes):
    source = ((lanes + 2) % LANES // 2 * 4 + 2 * (lanes % 2)) % LANES
    return source, (2 * lanes) % LANES, (lanes >= 126) | (lanes == 64), lanes >= 126


def columns_beside(left, right, lanes, source):
    above = pick_lanes(right, (2 * lanes + 4) % LANES)
    even = jnp.where((lanes >= 64) & (lanes < 112), above, pick_lanes(left, source))
    return even, pick_lanes(left, (source + 1) % LANES)


def split_lanes(values, r, edges, picks):
    _, even_lanes, at_even, at_odd = picks
    even = jnp.where(at_even, shifted(edges[0], 0, 2 * r), pick_lanes(values, even_lanes))
    odd = jnp.where(at_odd, shifted(edges[1], 0, 2 * r), pick_lanes(values, even_lanes + 1))
    return even, odd


def split_couplings(block, lanes):
    picks = lane_picks(lanes)
    c = [[[[None, None], [None, None]] for _ in range(4)] for _ in range(3)]
    for px in range(2):
        left = block[12, pl.ds(px, 8, stride=2), :]
        right = block[13, pl.ds(px, 8, stride=2), :]
        edges = columns_beside(left, right, lanes, picks[0])
        for r in range(12):
            values = block[r, pl.ds(px, 8, stride=2), :]
            c[r // 4][r % 4][px][:] = split_lanes(values, r, edges, picks)
    return c


def places():
    rows = lax.broadcasted_iota(jnp.int32, (ROWS, LANES), 0)
    lanes = lax.broadcasted_iota(jnp.int32, (ROWS, LANES), 1)
    last_x = lax.axis_index("gx") == lax.axis_size("gx") - 1
    last_y = lax.axis_index("gy") == lax.axis_size("gy") - 1
    return rows, lanes, last_x, last_y


def operators(block, first_ref, second_ref, hold_row=None):
    rows, lanes, last_x, last_y = places()
    hold = None if hold_row is None else rows == hold_row
    c = split_couplings(block, lanes)
    operator, chain, factors = first_operator(c, edge_masks(last_x, last_y, rows, lanes, 1), hold)
    empty = jnp.zeros((ROWS, LANES), jnp.float32)
    full = {}
    for o in range(27):
        offset = (o // 9 - 1, o // 3 % 3 - 1, o % 3 - 1)
        for z in range(2):
            full[offset, z] = operator.get((offset, z), empty)
            first_ref[o // 9, o % 9, z] = full[offset, z][0:4, 0:64]
    results, own = second_operator(full, chain, rows, lanes, hold)
    masks = edge_masks(last_x, last_y, rows, lanes, 2)
    second_ref[...] = jnp.zeros(second_ref.shape, jnp.float32)
    for (ox, oy), values in results.items():
        compact = pick_lanes(dropped(values, ox, oy, masks), (2 * lanes) % LANES)
        second_ref[9 + (ox + 1) * 3 + oy + 1, 0, 0:1, :] = compact[0:1, 0:32]
        second_ref[9 + (ox + 1) * 3 + oy + 1, 0, 1:2, :] = compact[2:3, 0:32]
    return operator, factors, own


fix_entries = [((oz, 1, oy), z) for z in (0, 1) for oz in (-z, 1 - z) for oy in (-1, 0, 1)]
fix_factors = [
    (zc, qz, qy, (tz, 0, ty))
    for zc in (0, 1)
    for qz in (0, 1)
    for qy in (0, 1)
    if qz or qy
    for tz in range(1 + (qz if zc == 0 else 0))
    for ty in range(1 + qy)
]
fix_sides = [(z, 1, my) for z in (0, 1) for my in (-1, 0, 1)]
fix_count = len(fix_entries) + len(fix_factors) + len(fix_sides)


def early_kernel(
    own_ref, first_columns_ref, second_columns_ref, third_columns_ref, far_ref,
    first_ref, second_ref, kept_ref, block,
):
    tiles = [own_ref[r] for r in range(12)] + beside((first_columns_ref, second_columns_ref, third_columns_ref))
    for r, values in enumerate(tiles):
        block[r, 0:8, :] = values
        block[r, 8:12, :] = jnp.zeros((4, LANES), jnp.float32)
        block[r, 12:16, :] = far_ref[r]
    operator, factors, own = operators(block, first_ref, second_ref, ROWS // 2 - 1)
    kept = [operator[e] for e in fix_entries] + [factors[e] for e in fix_factors]
    kept += [own[e] for e in fix_sides]
    for i, values in enumerate(kept):
        kept_ref[i] = values


def add_row_above(near_ref, early_second_ref, kept_ref, first_ref, second_ref, send_first):
    rows, lanes, last_x, last_y = places()
    kept = {e: kept_ref[i] for i, e in enumerate(fix_entries + fix_factors + fix_sides)}

    def row(r):
        return jnp.broadcast_to(near_ref[r, 0:1, :], (ROWS, LANES))

    _, even_lanes, at_even, at_odd = lane_picks(lanes)
    left, right = row(12), row(13)
    in_left = 2 * (lanes % 2)
    c = {}
    for d in (0, 2):
        for z in range(4):
            r = d * 4 + z
            values = row(r)
            below = [pick_lanes(left, in_left + (4 * r + py)) for py in range(2)]
            above = pick_lanes(right, jnp.full((ROWS, LANES), 4 * r + 4, jnp.int32))
            even = jnp.where(at_even, jnp.where(at_odd, below[0], above), pick_lanes(values, even_lanes))
            c[d, z] = (even, jnp.where(at_odd, below[1], pick_lanes(values, even_lanes + 1)))
    line_y = {z: line_terms(*c[2, z]) for z in range(4)}
    line_z = {(zc, py): line_terms(c[0, 2 * zc][py], c[0, 2 * zc + 1][py]) for zc in range(2) for py in range(2)}

    near_y = {(far, j): shifted(line_y[2 * far][2], 0, j) for far in range(2) for j in (-2, -1, 0, 1)}
    near_z = {(z, j): shifted(line_z[z, 0][2], 0, j) for z in range(2) for j in (-1, 0, 1)}
    odd = lanes % 2 == 1
    weights = {}
    for far in range(2):
        for oy in (-1, 0, 1):
            f, g = line_terms(near_y[far, oy - 1], near_y[far, oy])[:2]
            there = odd if oy == 0 else ~odd
            pair = jnp.where(there, f, 1.0), jnp.where(there, g, 1.0)
            if far == 1:
                depth = line_terms(near_z[0, oy], near_z[1, oy])[0]
                pair = pair[0] * depth, pair[1] * depth
            for jy, o in reaches:
                if o == oy:
                    weights[far, jy, oy] = reaching(jy, oy, pair[0 if from_below(jy, oy) else 1], odd)

    sums = {}
    for zc, qz, qy, t in fix_factors:
        pair_z = line_z[zc, qy][:2] if qz else (None,)
        pair_y = line_y[2 * zc + qz][:2] if qy else (None,)
        for uz in range(1 + (qz if zc == 0 else 0)):
            for uy in range(1 + qy):
                key = ((uz - t[0], 1, uy - t[2]), zc + t[0], t[2])
                term = kept[zc, qz, qy, t] * times(pair_z[uz], pair_y[uy])
                sums[key] = sums[key] + term if key in sums else term
    masks = edge_masks(last_x, last_y, rows, lanes, 1)
    entries = {}
    for offset, z in fix_entries:
        total = kept[offset, z]
        if (offset, z, 0) in sums:
            total = total - sums[offset, z, 0]
        if (offset, z, 1) in sums:
            total = total - shifted(sums[offset, z, 1], 0, -1)
        entries[offset, z] = dropped(total, *offset[1:], masks)
        whole = jnp.where(rows == ROWS // 2 - 1, entries[offset, z], kept[offset, z])
        first_ref[offset[0] + 1, offset[2] + 1, z] = whole[0:4, 0:64]
    for oz, z in ((0, 0), (2, 1)):
        for oy in range(3):
            first_ref[oz, oy, z] = jnp.zeros((4, 64), jnp.float32)
    send_first()

    spread = {}
    for far in range(2):
        for jy, oy in reaches:
            for z in range(2):
                term = entries[(far - z, 1, oy), z] * weights[far, jy, oy]
                spread[z, jy] = spread[z, jy] + term if (z, jy) in spread else term
    for oy in (-1, 0, 1):
        total = None
        for my, jy in taken(oy):
            part = kept[0, 1, my] * spread[0, jy] + kept[1, 1, my] * spread[1, jy]
            part = pick_lanes(part, (2 * lanes + my) % LANES)
            total = part if total is None else total + part
        total = jnp.where(last_x, 0.0, total)
        if oy == 1:
            total = jnp.where((lanes == LANES // 4 - 1) & last_y, 0.0, total)
        second_ref[oy + 1, 0, 0:1, :] = early_second_ref[16 + oy, 0, 0:1, :]
        row_two = early_second_ref[16 + oy, 0, 1:2, :]
        second_ref[oy + 1, 0, 1:2, :] = row_two + total[ROWS // 2 - 1:ROWS // 2, 0:32]


def last_kernel(
    own_ref, first_columns_ref, second_columns_ref, third_columns_ref, far_ref,
    early_first_ref, early_second_ref, kept_ref, near_ref,
    first_hbm, second_hbm, block, first_ref, second_ref, first_fix, second_fix, sems,
):
    odd_x = lax.axis_index("gx") % 2 == 1

    def send(parts):
        copies = [pltpu.make_async_copy(source, target, sems.at[i]) for i, source, target in parts]
        for copy in copies:
            copy.start()
        return copies

    @pl.when(odd_x)
    def _():
        tiles = [own_ref[r] for r in range(12)] + beside((first_columns_ref, second_columns_ref, third_columns_ref))
        for r, values in enumerate(tiles):
            block[r, 0:8, :] = values
            block[r, 8:12, :] = far_ref[r]
            block[r, 12:16, :] = near_ref[r]
        operators(block, first_ref, second_ref)
        for copy in send([(0, first_ref, first_hbm), (1, second_ref, second_hbm)]):
            copy.wait()

    @pl.when(jnp.logical_not(odd_x))
    def _():
        copies = []

        def send_first():
            copies.extend(send([
                (0, first_fix, first_hbm.at[:, pl.ds(6, 3)]),
                (1, early_first_ref.at[:, pl.ds(0, 6)], first_hbm.at[:, pl.ds(0, 6)]),
                (2, early_second_ref.at[pl.ds(0, 15)], second_hbm.at[pl.ds(0, 15)]),
                (3, early_second_ref.at[pl.ds(18, 9)], second_hbm.at[pl.ds(18, 9)]),
            ]))

        add_row_above(near_ref, early_second_ref, kept_ref, first_fix, second_fix, send_first)
        for copy in copies + send([(4, second_fix, second_hbm.at[pl.ds(15, 3)])]):
            copy.wait()


def swapped(values, axis, first):
    pairs = [(i, i + 1) for i in range(first, lax.axis_size(axis) - 1, 2)]
    return lax.ppermute(values, axis, pairs + [(b, a) for a, b in pairs])


def swapped_columns(values, which):
    count_x, count_y = lax.axis_size("gx"), lax.axis_size("gy")
    pairs = [
        (row * count_y + edge, row * count_y + edge + 1)
        for row in range(count_x)
        for edge in range(count_y - 1)
        if swap_order(row, edge, count_y // 2, np.where) == which
    ]
    return lax.ppermute(values, ("gx", "gy"), pairs + [(b, a) for a, b in pairs])


def body(material, face_open):
    whole = pl.BlockSpec(memory_space=pltpu.VMEM)
    page = jax.ShapeDtypeStruct((ROWS, LANES), jnp.float32)
    edge = jax.ShapeDtypeStruct((14, 4, LANES), jnp.float32)
    small = pltpu.CompilerParams(vmem_limit_bytes=1 << 20)
    own, *messages = pl.pallas_call(
        couplings_kernel,
        out_shape=(jax.ShapeDtypeStruct((12, ROWS, LANES), jnp.float32),) + (page,) * 3,
        in_specs=[whole],
        out_specs=(whole,) * 4,
        compiler_params=small,
        name="couplings",
    )(face_open * 4 + material[None])
    columns = [swapped_columns(message, k) for k, message in enumerate(messages)]
    far, near = pl.pallas_call(
        edges_kernel,
        out_shape=(edge, edge),
        in_specs=[whole] * 4,
        out_specs=(whole,) * 2,
        compiler_params=small,
        name="edges",
    )(own, *columns)
    far_rows = swapped(far, "gx", 1)
    near_rows = swapped(near, "gx", 0)
    first = jax.ShapeDtypeStruct((3, 9, 2, 4, 64), jnp.float32)
    second = jax.ShapeDtypeStruct((27, 1, 2, 32), jnp.float32)
    large = pltpu.CompilerParams(vmem_limit_bytes=3 << 20)
    block = pltpu.VMEM((14, 16, LANES), jnp.float32)
    early = pl.pallas_call(
        early_kernel,
        out_shape=(first, second, jax.ShapeDtypeStruct((fix_count, ROWS, LANES), jnp.float32)),
        in_specs=[whole] * 5,
        out_specs=(whole,) * 3,
        scratch_shapes=[block],
        compiler_params=large,
        cost_estimate=pl.CostEstimate(flops=3 << 20, bytes_accessed=1 << 20, transcendentals=0),
        name="early",
    )(own, *columns, far_rows)
    first_level, second_level = pl.pallas_call(
        last_kernel,
        out_shape=(first, second),
        in_specs=[whole] * 9,
        out_specs=(pl.BlockSpec(memory_space=pltpu.HBM),) * 2,
        scratch_shapes=[
            block,
            pltpu.VMEM(first.shape, jnp.float32),
            pltpu.VMEM(second.shape, jnp.float32),
            pltpu.VMEM((3, 3, 2, 4, 64), jnp.float32),
            pltpu.VMEM((3, 1, 2, 32), jnp.float32),
            pltpu.SemaphoreType.DMA((5,)),
        ],
        compiler_params=large,
        name="last",
    )(own, *columns, far_rows, *early, near_rows)
    return first_level.reshape(27, 2, 4, 64), second_level


def solution(mesh):
    placed = (P(None, "gx", "gy"), P(None, None, "gx", "gy"))
    return jax.shard_map(
        body,
        mesh=mesh,
        in_specs=placed,
        out_specs=(P(None, None, "gx", "gy"), P(None, None, "gx", "gy")),
        check_vma=False,
    )
```

```python
import functools

import jax
import jax.numpy as jnp
import numpy as np
from jax import lax
from jax.experimental import pallas as pl
from jax.experimental.pallas import tpu as pltpu
from jax.sharding import PartitionSpec as P

permit_levels = (1.0 / 80.0 / 64.0, 4.0 / 80.0 / 64.0, 20.0 / 80.0 / 64.0, 1.0 / 64.0)

ROWS, LANES = 8, 128


def permittivity(material):
    values = jnp.full(material.shape, permit_levels[3], jnp.float32)
    for material_id in range(3):
        values = jnp.where(material == material_id, permit_levels[material_id], values)
    return values


def shifted(values, by_x, by_y):
    if by_x:
        values = pltpu.roll(values, (-by_x) % ROWS, 0)
    if by_y:
        values = pltpu.roll(values, (-by_y) % LANES, 1)
    return values


def pick_lanes(values, index):
    return jnp.take_along_axis(values, index, axis=1)


def times(a, b):
    if a is None:
        return b
    if b is None:
        return a
    return a * b


def minus(a, b):
    return (1.0 if a is None else a) - (1.0 if b is None else b)


def line_terms(lower, upper):
    total = lower + upper
    inverse = 1.0 / jnp.where(total > 0.0, total, 1.0)
    f = lower * inverse
    g = upper * inverse
    return f, g, lower * g, lower * f, upper * g


def edge_masks(last_x, last_y, rows, lanes, step):
    return (rows == ROWS // 2 - step) & last_x, (lanes == LANES // 2 - step) & last_y


def dropped(values, offset_x, offset_y, masks):
    if offset_x == 1:
        values = jnp.where(masks[0], 0.0, values)
    if offset_y == 1:
        values = jnp.where(masks[1], 0.0, values)
    return values


def first_operator(c, masks, hold=None):
    factors = {}
    lines = {}
    for z in range(4):
        for p in range(2):
            lines[1, z, p] = line_terms(c[1][z][0][p], c[1][z][1][p])
            lines[2, z, p] = line_terms(c[2][z][p][0], c[2][z][p][1])
    for zc in range(2):
        for px in range(2):
            for py in range(2):
                lines[0, zc, px, py] = line_terms(c[0][2 * zc][px][py], c[0][2 * zc + 1][px][py])

    rolled = {}

    def fraction(dim, zc, node, raised):
        pz, px, py = node
        if raised == 0:
            zc, raised = zc + 1, None
        if dim == 0:
            key = (0, zc, px, py)
        elif dim == 1:
            key = (1, 2 * zc + pz, py)
        else:
            key = (2, 2 * zc + pz, px)
        if raised is None:
            return lines[key][:2]
        if (key, raised) not in rolled:
            f = shifted(lines[key][0], int(raised == 1), int(raised == 2))
            rolled[key, raised] = (f, 1.0 - f)
        return rolled[key, raised]

    def transverse(d, zc, node, raised):
        dims = [dim for dim in range(3) if dim != d]
        entries = {(0, 0, 0): None}
        for dim in dims:
            if not node[dim]:
                continue
            pair = fraction(dim, zc, node, raised)
            fresh = {}
            for corner, weight in entries.items():
                for side in range(2):
                    moved = list(corner)
                    moved[dim] = side
                    if dim == 0 and side == 1 and zc == 1:
                        continue
                    fresh[tuple(moved)] = times(weight, pair[side])
            entries = fresh
        return entries

    sums = {}

    def put(zc, low, high, value):
        offset = tuple(b - a for a, b in zip(low, high))
        if offset < (0, 0, 0):
            low, high = high, low
            offset = tuple(-o for o in offset)
        if zc + low[0] > 1 or zc + high[0] > 1:
            return
        key = (offset, zc + low[0], low[1], low[2])
        sums[key] = sums[key] + value if key in sums else value

    for d in range(3):
        dims = [dim for dim in range(3) if dim != d]
        for zc in range(2):
            top = d == 0 and zc == 1
            for q1 in range(2):
                for q2 in range(2):
                    node = [0, 0, 0]
                    node[dims[0]], node[dims[1]] = q1, q2
                    odd = list(node)
                    odd[d] = 1
                    if d == 0:
                        key = (0, zc, node[1], node[2])
                    elif d == 1:
                        key = (1, 2 * zc + node[0], node[2])
                    else:
                        key = (2, 2 * zc + node[0], node[1])
                    _, _, s, h, k = lines[key]

                    def raised_corner(corner):
                        moved = list(corner)
                        moved[d] = 1
                        return tuple(moved)

                    zero = (0, 0, 0)
                    if not (q1 or q2):
                        put(zc, zero, zero, s)
                        if not top:
                            up = raised_corner(zero)
                            put(zc, up, up, s)
                            put(zc, zero, up, -s)
                        continue
                    alpha = transverse(d, zc, node, None)
                    beta = transverse(d, zc, odd, None)
                    corners = list(alpha)
                    delta = {t: minus(alpha[t], beta[t]) for t in corners}
                    for i, t in enumerate(corners):
                        s_alpha, h_delta = s * alpha[t], h * delta[t]
                        for u in corners[i:]:
                            put(zc, t, u, s_alpha * alpha[u] + h_delta * delta[u])
                    if top:
                        continue
                    gamma = transverse(d, zc, node, d)
                    epsilon = {t: minus(gamma[t], beta[t]) for t in corners}
                    for i, t in enumerate(corners):
                        s_gamma, k_epsilon = s * gamma[t], k * epsilon[t]
                        for u in corners[i:]:
                            put(zc, raised_corner(t), raised_corner(u), s_gamma * gamma[u] + k_epsilon * epsilon[u])
                    waiting = hold is not None and d == 1
                    for t in corners:
                        s_delta, s_beta = s * delta[t], s * beta[t]
                        if waiting:
                            factors[zc, q1, q2, t] = s_beta
                            s_beta = jnp.where(hold, 0.0, s_beta)
                        for u in corners:
                            put(zc, t, raised_corner(u), -(s_delta * beta[u] + s_beta * gamma[u]))

    operator = {}
    keys = sorted({(offset, z) for offset, z, _, _ in sums})
    for offset, z in keys:
        total = None
        for ax in range(2):
            part = sums.get((offset, z, ax, 0))
            side = sums.get((offset, z, ax, 1))
            if side is not None:
                side = shifted(side, 0, -1)
                part = side if part is None else part + side
            if part is None:
                continue
            part = shifted(part, -ax, 0)
            total = part if total is None else total + part
        operator[offset, z] = dropped(total, *offset[1:], masks)
        if offset != (0, 0, 0):
            mirror = tuple(-o for o in offset)
            operator[mirror, z + offset[0]] = dropped(shifted(total, -offset[1], -offset[2]), *mirror[1:], masks)

    chain = [
        [lines[0, z, 0, 0][2] for z in range(2)],
        [lines[1, 2 * z, 0][2] for z in range(2)],
        [lines[2, 2 * z, 0][2] for z in range(2)],
    ]
    return operator, chain, factors


reaches = ((-1, -1), (0, -1), (0, 0), (0, 1), (1, 0), (1, 1))


def taken(offset):
    return [(m, offset + 1 if m == -1 else offset) for m in (-1, 0, 1) if m * offset != -1]


def from_below(j, o):
    return (j, o) in ((-1, -1), (0, 0), (0, 1))


def reaching(j, o, source, odd):
    if (j, o) == (0, 1):
        return jnp.where(odd, 0.0, source)
    if (j, o) == (1, 0):
        return jnp.where(odd, source, 0.0)
    return source


def second_operator(operator, chain, rows, lanes, hold=None):
    odd = {1: rows % 2 == 1, 2: lanes % 2 == 1}
    depth = line_terms(chain[0][0], chain[0][1])[0]
    down, up = {}, {}
    for d in (1, 2):
        for z in range(2):
            here = chain[d][z]
            before = shifted(here, -int(d == 1), -int(d == 2))
            f, g = line_terms(before, here)[:2]
            down[d, z] = jnp.where(odd[d], f, 1.0)
            up[d, z] = jnp.where(odd[d], g, 1.0)
    down_z = {0: down[1, 0], 1: down[1, 1] * depth}
    up_z = {0: up[1, 0], 1: up[1, 1] * depth}

    def factors(d, lower, upper):
        base = {}
        for j, o in reaches:
            source = lower if from_below(j, o) else upper
            source = reaching(j, o, shifted(source, o if d == 1 else 0, o if d == 2 else 0), odd[d])
            if hold is not None and d == 1 and (j, o) == (1, 1):
                source = jnp.where(hold, 0.0, source)
            base[j, o] = source
        return {
            (j, o, across): shifted(base[j, o], 0 if d == 1 else across, across if d == 1 else 0)
            for j, o in reaches
            for across in (-1, 0, 1)
        }

    spread = {}
    for far in range(2):
        along_x = factors(1, down_z[far], up_z[far])
        along_y = factors(2, down[2, far], up[2, far])
        for jx, ox in reaches:
            for jy, oy in reaches:
                weight = along_x[jx, ox, oy] * along_y[jy, oy, ox]
                for z in range(2):
                    term = operator[(far - z, ox, oy), z] * weight
                    key = (z, jx, jy)
                    spread[key] = spread[key] + term if key in spread else term

    sides = {
        (z, d): {-1: up_z[z] if d == 1 else up[2, z], 0: depth if (d == 1 and z == 1) else None, 1: down_z[z] if d == 1 else down[2, z]}
        for z in range(2)
        for d in (1, 2)
    }
    own = {(z, mx, my): times(sides[z, 1][mx], sides[z, 2][my]) for z in range(2) for mx in (-1, 0, 1) for my in (-1, 0, 1)}

    results = {}
    for ox in (-1, 0, 1):
        for oy in (-1, 0, 1):
            total = None
            for my, jy in taken(oy):
                part = None
                for mx, jx in taken(ox):
                    term = times(own[0, mx, my], spread[0, jx, jy]) + times(own[1, mx, my], spread[1, jx, jy])
                    term = shifted(term, mx, 0)
                    part = term if part is None else part + term
                part = shifted(part, 0, my)
                total = part if total is None else total + part
            results[ox, oy] = total
    return results, own


def swap_order(row, edge, half, where):
    below_half, inner, at_half = (where(test, 1, 0) for test in (edge < half, row > 0, edge == half))
    cores_first, border = inner * below_half, inner * at_half
    order = cores_first * (edge % 2) + (1 - cores_first) * (1 - edge % 2)
    return border * 2 + (1 - border) * order


def own_swaps():
    row, column, size = lax.axis_index("gx"), lax.axis_index("gy"), lax.axis_size("gy")

    def order(edge):
        return swap_order(row, edge, size // 2, jnp.where)

    return jnp.where(column > 0, order(column - 1 + (column == 0)), -1), jnp.where(column < size - 1, order(column), -1)


def couplings_kernel(inputs_ref, own_ref, *message_refs):
    lanes = lax.broadcasted_iota(jnp.int32, (ROWS, LANES), 1)
    low = jnp.zeros((ROWS, LANES), jnp.float32)
    high = jnp.zeros((ROWS, LANES), jnp.float32)
    eps = [permittivity(inputs_ref[0, z] & 3) for z in range(4)]
    for r in range(12):
        values = (inputs_ref[r // 4, r % 4] >> 2).astype(jnp.float32) * eps[r % 4]
        own_ref[r] = values
        turned = pltpu.roll(values, 4 * r + 4, 1)
        low = jnp.where((lanes >= 4 * r) & (lanes < 4 * r + 4), turned, low)
        high = jnp.where(lanes == 4 * r + 4, turned, high)
    _, above = own_swaps()
    for k, ref in enumerate(message_refs):
        ref[...] = jnp.where(above == k, low, high)


def beside(column_refs):
    sides = []
    for swap in own_swaps():
        values = jnp.zeros((ROWS, LANES), jnp.float32)
        for k, ref in enumerate(column_refs):
            values = jnp.where(swap == k, ref[...], values)
        sides.append(values)
    return sides


def edges_kernel(own_ref, first_columns_ref, second_columns_ref, third_columns_ref, far_ref, near_ref):
    odd_x = lax.axis_index("gx") % 2 == 1
    tiles = [own_ref[r] for r in range(12)] + beside((first_columns_ref, second_columns_ref, third_columns_ref))
    for r, values in enumerate(tiles):
        far_ref[r] = jnp.where(odd_x, values[4:8, :], values[0:4, :])
        near_ref[r] = jnp.where(odd_x, values[0:4, :], values[4:8, :])


def lane_picks(lanes):
    source = ((lanes + 2) % LANES // 2 * 4 + 2 * (lanes % 2)) % LANES
    return source, (2 * lanes) % LANES, (lanes >= 126) | (lanes == 64), lanes >= 126


def columns_beside(left, right, lanes, source):
    above = pick_lanes(right, (2 * lanes + 4) % LANES)
    even = jnp.where((lanes >= 64) & (lanes < 112), above, pick_lanes(left, source))
    return even, pick_lanes(left, (source + 1) % LANES)


def split_lanes(values, r, edges, picks):
    _, even_lanes, at_even, at_odd = picks
    even = jnp.where(at_even, shifted(edges[0], 0, 2 * r), pick_lanes(values, even_lanes))
    odd = jnp.where(at_odd, shifted(edges[1], 0, 2 * r), pick_lanes(values, even_lanes + 1))
    return even, odd


def split_couplings(block, lanes):
    picks = lane_picks(lanes)
    c = [[[[None, None], [None, None]] for _ in range(4)] for _ in range(3)]
    for px in range(2):
        left = block[12, pl.ds(px, 8, stride=2), :]
        right = block[13, pl.ds(px, 8, stride=2), :]
        edges = columns_beside(left, right, lanes, picks[0])
        for r in range(12):
            values = block[r, pl.ds(px, 8, stride=2), :]
            c[r // 4][r % 4][px][:] = split_lanes(values, r, edges, picks)
    return c


def places():
    rows = lax.broadcasted_iota(jnp.int32, (ROWS, LANES), 0)
    lanes = lax.broadcasted_iota(jnp.int32, (ROWS, LANES), 1)
    last_x = lax.axis_index("gx") == lax.axis_size("gx") - 1
    last_y = lax.axis_index("gy") == lax.axis_size("gy") - 1
    return rows, lanes, last_x, last_y


def operators(block, first_ref, second_ref, hold_row=None):
    rows, lanes, last_x, last_y = places()
    hold = None if hold_row is None else rows == hold_row
    c = split_couplings(block, lanes)
    operator, chain, factors = first_operator(c, edge_masks(last_x, last_y, rows, lanes, 1), hold)
    empty = jnp.zeros((ROWS, LANES), jnp.float32)
    full = {}
    for o in range(27):
        offset = (o // 9 - 1, o // 3 % 3 - 1, o % 3 - 1)
        for z in range(2):
            full[offset, z] = operator.get((offset, z), empty)
            first_ref[o // 9, o % 9, z] = full[offset, z][0:4, 0:64]
    results, own = second_operator(full, chain, rows, lanes, hold)
    masks = edge_masks(last_x, last_y, rows, lanes, 2)
    second_ref[...] = jnp.zeros(second_ref.shape, jnp.float32)
    for (ox, oy), values in results.items():
        compact = pick_lanes(dropped(values, ox, oy, masks), (2 * lanes) % LANES)
        second_ref[9 + (ox + 1) * 3 + oy + 1, 0, 0:1, :] = compact[0:1, 0:32]
        second_ref[9 + (ox + 1) * 3 + oy + 1, 0, 1:2, :] = compact[2:3, 0:32]
    return operator, factors, own


fix_entries = [((oz, 1, oy), z) for z in (0, 1) for oz in (-z, 1 - z) for oy in (-1, 0, 1)]
fix_factors = [
    (zc, qz, qy, (tz, 0, ty))
    for zc in (0, 1)
    for qz in (0, 1)
    for qy in (0, 1)
    if qz or qy
    for tz in range(1 + (qz if zc == 0 else 0))
    for ty in range(1 + qy)
]
fix_sides = [(z, 1, my) for z in (0, 1) for my in (-1, 0, 1)]
fix_count = len(fix_entries) + len(fix_factors) + len(fix_sides)


def early_kernel(
    own_ref, first_columns_ref, second_columns_ref, third_columns_ref, far_ref,
    first_hbm, second_hbm, kept_ref, rows_ref, block, first_ref, second_ref, sems,
):
    tiles = [own_ref[r] for r in range(12)] + beside((first_columns_ref, second_columns_ref, third_columns_ref))
    for r, values in enumerate(tiles):
        block[r, 0:8, :] = values
        block[r, 8:12, :] = jnp.zeros((4, LANES), jnp.float32)
        block[r, 12:16, :] = far_ref[r]
    operator, factors, own = operators(block, first_ref, second_ref, ROWS // 2 - 1)
    kept = [operator[e] for e in fix_entries] + [factors[e] for e in fix_factors]
    kept += [own[e] for e in fix_sides]
    for i, values in enumerate(kept):
        kept_ref[i] = values
    rows_ref[...] = second_ref[15:18]
    copies = [
        pltpu.make_async_copy(first_ref, first_hbm, sems.at[0]),
        pltpu.make_async_copy(second_ref, second_hbm, sems.at[1]),
    ]
    for copy in copies:
        copy.start()
    for copy in copies:
        copy.wait()


def add_row_above(near_ref, early_rows_ref, kept_ref, first_ref, second_ref, send_first):
    rows, lanes, last_x, last_y = places()
    kept = {e: kept_ref[i] for i, e in enumerate(fix_entries + fix_factors + fix_sides)}

    def row(r):
        return jnp.broadcast_to(near_ref[r, 0:1, :], (ROWS, LANES))

    _, even_lanes, at_even, at_odd = lane_picks(lanes)
    left, right = row(12), row(13)
    in_left = 2 * (lanes % 2)
    c = {}
    for d in (0, 2):
        for z in range(4):
            r = d * 4 + z
            values = row(r)
            below = [pick_lanes(left, in_left + (4 * r + py)) for py in range(2)]
            above = pick_lanes(right, jnp.full((ROWS, LANES), 4 * r + 4, jnp.int32))
            even = jnp.where(at_even, jnp.where(at_odd, below[0], above), pick_lanes(values, even_lanes))
            c[d, z] = (even, jnp.where(at_odd, below[1], pick_lanes(values, even_lanes + 1)))
    line_y = {z: line_terms(*c[2, z]) for z in range(4)}
    line_z = {(zc, py): line_terms(c[0, 2 * zc][py], c[0, 2 * zc + 1][py]) for zc in range(2) for py in range(2)}

    near_y = {(far, j): shifted(line_y[2 * far][2], 0, j) for far in range(2) for j in (-2, -1, 0, 1)}
    near_z = {(z, j): shifted(line_z[z, 0][2], 0, j) for z in range(2) for j in (-1, 0, 1)}
    odd = lanes % 2 == 1
    weights = {}
    for far in range(2):
        for oy in (-1, 0, 1):
            f, g = line_terms(near_y[far, oy - 1], near_y[far, oy])[:2]
            there = odd if oy == 0 else ~odd
            pair = jnp.where(there, f, 1.0), jnp.where(there, g, 1.0)
            if far == 1:
                depth = line_terms(near_z[0, oy], near_z[1, oy])[0]
                pair = pair[0] * depth, pair[1] * depth
            for jy, o in reaches:
                if o == oy:
                    weights[far, jy, oy] = reaching(jy, oy, pair[0 if from_below(jy, oy) else 1], odd)

    sums = {}
    for zc, qz, qy, t in fix_factors:
        pair_z = line_z[zc, qy][:2] if qz else (None,)
        pair_y = line_y[2 * zc + qz][:2] if qy else (None,)
        for uz in range(1 + (qz if zc == 0 else 0)):
            for uy in range(1 + qy):
                key = ((uz - t[0], 1, uy - t[2]), zc + t[0], t[2])
                term = kept[zc, qz, qy, t] * times(pair_z[uz], pair_y[uy])
                sums[key] = sums[key] + term if key in sums else term
    masks = edge_masks(last_x, last_y, rows, lanes, 1)
    entries = {}
    for offset, z in fix_entries:
        total = kept[offset, z]
        if (offset, z, 0) in sums:
            total = total - sums[offset, z, 0]
        if (offset, z, 1) in sums:
            total = total - shifted(sums[offset, z, 1], 0, -1)
        entries[offset, z] = dropped(total, *offset[1:], masks)
        whole = jnp.where(rows == ROWS // 2 - 1, entries[offset, z], kept[offset, z])
        first_ref[offset[0] + 1, offset[2] + 1, z] = whole[0:4, 0:64]
    for oz, z in ((0, 0), (2, 1)):
        for oy in range(3):
            first_ref[oz, oy, z] = jnp.zeros((4, 64), jnp.float32)
    send_first()

    spread = {}
    for far in range(2):
        for jy, oy in reaches:
            for z in range(2):
                term = entries[(far - z, 1, oy), z] * weights[far, jy, oy]
                spread[z, jy] = spread[z, jy] + term if (z, jy) in spread else term
    for oy in (-1, 0, 1):
        total = None
        for my, jy in taken(oy):
            part = kept[0, 1, my] * spread[0, jy] + kept[1, 1, my] * spread[1, jy]
            part = pick_lanes(part, (2 * lanes + my) % LANES)
            total = part if total is None else total + part
        total = jnp.where(last_x, 0.0, total)
        if oy == 1:
            total = jnp.where((lanes == LANES // 4 - 1) & last_y, 0.0, total)
        second_ref[oy + 1, 0, 0:1, :] = early_rows_ref[oy + 1, 0, 0:1, :]
        row_two = early_rows_ref[oy + 1, 0, 1:2, :]
        second_ref[oy + 1, 0, 1:2, :] = row_two + total[ROWS // 2 - 1:ROWS // 2, 0:32]


def last_kernel(
    own_ref, first_columns_ref, second_columns_ref, third_columns_ref, far_ref,
    early_first_hbm, early_second_hbm, kept_ref, early_rows_ref, near_ref,
    first_hbm, second_hbm, block, first_ref, second_ref, first_fix, second_fix, sems,
):
    odd_x = lax.axis_index("gx") % 2 == 1

    def send(parts):
        copies = [pltpu.make_async_copy(source, target, sems.at[i]) for i, source, target in parts]
        for copy in copies:
            copy.start()
        return copies

    @pl.when(odd_x)
    def _():
        tiles = [own_ref[r] for r in range(12)] + beside((first_columns_ref, second_columns_ref, third_columns_ref))
        for r, values in enumerate(tiles):
            block[r, 0:8, :] = values
            block[r, 8:12, :] = far_ref[r]
            block[r, 12:16, :] = near_ref[r]
        operators(block, first_ref, second_ref)
        for copy in send([(0, first_ref, first_hbm), (1, second_ref, second_hbm)]):
            copy.wait()

    @pl.when(jnp.logical_not(odd_x))
    def _():
        copies = []

        def send_first():
            copies.extend(send([(0, first_fix, first_hbm.at[:, pl.ds(6, 3)])]))

        add_row_above(near_ref, early_rows_ref, kept_ref, first_fix, second_fix, send_first)
        for copy in copies + send([(1, second_fix, second_hbm.at[pl.ds(15, 3)])]):
            copy.wait()


def swapped(values, axis, first):
    pairs = [(i, i + 1) for i in range(first, lax.axis_size(axis) - 1, 2)]
    return lax.ppermute(values, axis, pairs + [(b, a) for a, b in pairs])


def swapped_columns(values, which):
    count_x, count_y = lax.axis_size("gx"), lax.axis_size("gy")
    pairs = [
        (row * count_y + edge, row * count_y + edge + 1)
        for row in range(count_x)
        for edge in range(count_y - 1)
        if swap_order(row, edge, count_y // 2, np.where) == which
    ]
    return lax.ppermute(values, ("gx", "gy"), pairs + [(b, a) for a, b in pairs])


def body(material, face_open):
    whole = pl.BlockSpec(memory_space=pltpu.VMEM)
    outside = pl.BlockSpec(memory_space=pltpu.HBM)
    page = jax.ShapeDtypeStruct((ROWS, LANES), jnp.float32)
    edge = jax.ShapeDtypeStruct((14, 4, LANES), jnp.float32)
    small = pltpu.CompilerParams(vmem_limit_bytes=1 << 20)
    own, *messages = pl.pallas_call(
        couplings_kernel,
        out_shape=(jax.ShapeDtypeStruct((12, ROWS, LANES), jnp.float32),) + (page,) * 3,
        in_specs=[whole],
        out_specs=(whole,) * 4,
        compiler_params=small,
        name="couplings",
    )(face_open * 4 + material[None])
    columns = [swapped_columns(message, k) for k, message in enumerate(messages)]
    far, near = pl.pallas_call(
        edges_kernel,
        out_shape=(edge, edge),
        in_specs=[whole] * 4,
        out_specs=(whole,) * 2,
        compiler_params=small,
        name="edges",
    )(own, *columns)
    far_rows = swapped(far, "gx", 1)
    near_rows = swapped(near, "gx", 0)
    first = jax.ShapeDtypeStruct((3, 9, 2, 4, 64), jnp.float32)
    second = jax.ShapeDtypeStruct((27, 1, 2, 32), jnp.float32)
    large = pltpu.CompilerParams(vmem_limit_bytes=3 << 20)
    block = pltpu.VMEM((14, 16, LANES), jnp.float32)
    early = pl.pallas_call(
        early_kernel,
        out_shape=(
            pltpu.HBM(first.shape, jnp.float32),
            pltpu.HBM(second.shape, jnp.float32),
            jax.ShapeDtypeStruct((fix_count, ROWS, LANES), jnp.float32),
            jax.ShapeDtypeStruct((3, 1, 2, 32), jnp.float32),
        ),
        in_specs=[whole] * 5,
        out_specs=(outside, outside, whole, whole),
        scratch_shapes=[
            block,
            pltpu.VMEM(first.shape, jnp.float32),
            pltpu.VMEM(second.shape, jnp.float32),
            pltpu.SemaphoreType.DMA((2,)),
        ],
        compiler_params=large,
        cost_estimate=pl.CostEstimate(flops=3 << 20, bytes_accessed=1 << 20, transcendentals=0),
        name="early",
    )(own, *columns, far_rows)
    held = [pltpu.with_memory_space_constraint(values, pltpu.HBM) for values in early[:2]]
    first_level, second_level = pl.pallas_call(
        last_kernel,
        out_shape=(first, second),
        in_specs=[whole] * 5 + [outside] * 2 + [whole] * 3,
        out_specs=(outside,) * 2,
        input_output_aliases={5: 0, 6: 1},
        scratch_shapes=[
            block,
            pltpu.VMEM(first.shape, jnp.float32),
            pltpu.VMEM(second.shape, jnp.float32),
            pltpu.VMEM((3, 3, 2, 4, 64), jnp.float32),
            pltpu.VMEM((3, 1, 2, 32), jnp.float32),
            pltpu.SemaphoreType.DMA((2,)),
        ],
        compiler_params=large,
        name="last",
    )(own, *columns, far_rows, *held, *early[2:], near_rows)
    return first_level.reshape(27, 2, 4, 64), second_level


def solution(mesh):
    placed = (P(None, "gx", "gy"), P(None, None, "gx", "gy"))
    return jax.shard_map(
        body,
        mesh=mesh,
        in_specs=placed,
        out_specs=(P(None, None, "gx", "gy"), P(None, None, "gx", "gy")),
        check_vma=False,
    )
```

```python
import functools

import jax
import jax.numpy as jnp
import numpy as np
from jax import lax
from jax.experimental import pallas as pl
from jax.experimental.pallas import tpu as pltpu
from jax.sharding import PartitionSpec as P

permit_levels = (1.0 / 80.0 / 64.0, 4.0 / 80.0 / 64.0, 20.0 / 80.0 / 64.0, 1.0 / 64.0)

ROWS, LANES = 8, 128


def permittivity(material):
    values = jnp.full(material.shape, permit_levels[3], jnp.float32)
    for material_id in range(3):
        values = jnp.where(material == material_id, permit_levels[material_id], values)
    return values


def shifted(values, by_x, by_y):
    if by_x:
        values = pltpu.roll(values, (-by_x) % ROWS, 0)
    if by_y:
        values = pltpu.roll(values, (-by_y) % LANES, 1)
    return values


def pick_lanes(values, index):
    return jnp.take_along_axis(values, index, axis=1)


def times(a, b):
    if a is None:
        return b
    if b is None:
        return a
    return a * b


def minus(a, b):
    return (1.0 if a is None else a) - (1.0 if b is None else b)


def line_terms(lower, upper):
    total = lower + upper
    inverse = 1.0 / jnp.where(total > 0.0, total, 1.0)
    f = lower * inverse
    g = upper * inverse
    return f, g, lower * g, lower * f, upper * g


def edge_masks(last_x, last_y, rows, lanes, step):
    return (rows == ROWS // 2 - step) & last_x, (lanes == LANES // 2 - step) & last_y


def dropped(values, offset_x, offset_y, masks):
    if offset_x == 1:
        values = jnp.where(masks[0], 0.0, values)
    if offset_y == 1:
        values = jnp.where(masks[1], 0.0, values)
    return values


def first_operator(c, masks, hold=None):
    factors = {}
    lines = {}
    for z in range(4):
        for p in range(2):
            lines[1, z, p] = line_terms(c[1][z][0][p], c[1][z][1][p])
            lines[2, z, p] = line_terms(c[2][z][p][0], c[2][z][p][1])
    for zc in range(2):
        for px in range(2):
            for py in range(2):
                lines[0, zc, px, py] = line_terms(c[0][2 * zc][px][py], c[0][2 * zc + 1][px][py])

    rolled = {}

    def fraction(dim, zc, node, raised):
        pz, px, py = node
        if raised == 0:
            zc, raised = zc + 1, None
        if dim == 0:
            key = (0, zc, px, py)
        elif dim == 1:
            key = (1, 2 * zc + pz, py)
        else:
            key = (2, 2 * zc + pz, px)
        if raised is None:
            return lines[key][:2]
        if (key, raised) not in rolled:
            f = shifted(lines[key][0], int(raised == 1), int(raised == 2))
            rolled[key, raised] = (f, 1.0 - f)
        return rolled[key, raised]

    def transverse(d, zc, node, raised):
        dims = [dim for dim in range(3) if dim != d]
        entries = {(0, 0, 0): None}
        for dim in dims:
            if not node[dim]:
                continue
            pair = fraction(dim, zc, node, raised)
            fresh = {}
            for corner, weight in entries.items():
                for side in range(2):
                    moved = list(corner)
                    moved[dim] = side
                    if dim == 0 and side == 1 and zc == 1:
                        continue
                    fresh[tuple(moved)] = times(weight, pair[side])
            entries = fresh
        return entries

    sums = {}

    def put(zc, low, high, value):
        offset = tuple(b - a for a, b in zip(low, high))
        if offset < (0, 0, 0):
            low, high = high, low
            offset = tuple(-o for o in offset)
        if zc + low[0] > 1 or zc + high[0] > 1:
            return
        key = (offset, zc + low[0], low[1], low[2])
        sums[key] = sums[key] + value if key in sums else value

    for d in range(3):
        dims = [dim for dim in range(3) if dim != d]
        for zc in range(2):
            top = d == 0 and zc == 1
            for q1 in range(2):
                for q2 in range(2):
                    node = [0, 0, 0]
                    node[dims[0]], node[dims[1]] = q1, q2
                    odd = list(node)
                    odd[d] = 1
                    if d == 0:
                        key = (0, zc, node[1], node[2])
                    elif d == 1:
                        key = (1, 2 * zc + node[0], node[2])
                    else:
                        key = (2, 2 * zc + node[0], node[1])
                    _, _, s, h, k = lines[key]

                    def raised_corner(corner):
                        moved = list(corner)
                        moved[d] = 1
                        return tuple(moved)

                    zero = (0, 0, 0)
                    if not (q1 or q2):
                        put(zc, zero, zero, s)
                        if not top:
                            up = raised_corner(zero)
                            put(zc, up, up, s)
                            put(zc, zero, up, -s)
                        continue
                    alpha = transverse(d, zc, node, None)
                    beta = transverse(d, zc, odd, None)
                    corners = list(alpha)
                    delta = {t: minus(alpha[t], beta[t]) for t in corners}
                    for i, t in enumerate(corners):
                        s_alpha, h_delta = s * alpha[t], h * delta[t]
                        for u in corners[i:]:
                            put(zc, t, u, s_alpha * alpha[u] + h_delta * delta[u])
                    if top:
                        continue
                    gamma = transverse(d, zc, node, d)
                    epsilon = {t: minus(gamma[t], beta[t]) for t in corners}
                    for i, t in enumerate(corners):
                        s_gamma, k_epsilon = s * gamma[t], k * epsilon[t]
                        for u in corners[i:]:
                            put(zc, raised_corner(t), raised_corner(u), s_gamma * gamma[u] + k_epsilon * epsilon[u])
                    waiting = hold is not None and d == 1
                    for t in corners:
                        s_delta, s_beta = s * delta[t], s * beta[t]
                        if waiting:
                            factors[zc, q1, q2, t] = s_beta
                            s_beta = jnp.where(hold, 0.0, s_beta)
                        for u in corners:
                            put(zc, t, raised_corner(u), -(s_delta * beta[u] + s_beta * gamma[u]))

    operator = {}
    keys = sorted({(offset, z) for offset, z, _, _ in sums})
    for offset, z in keys:
        total = None
        for ax in range(2):
            part = sums.get((offset, z, ax, 0))
            side = sums.get((offset, z, ax, 1))
            if side is not None:
                side = shifted(side, 0, -1)
                part = side if part is None else part + side
            if part is None:
                continue
            part = shifted(part, -ax, 0)
            total = part if total is None else total + part
        operator[offset, z] = dropped(total, *offset[1:], masks)
        if offset != (0, 0, 0):
            mirror = tuple(-o for o in offset)
            operator[mirror, z + offset[0]] = dropped(shifted(total, -offset[1], -offset[2]), *mirror[1:], masks)

    chain = [
        [lines[0, z, 0, 0][2] for z in range(2)],
        [lines[1, 2 * z, 0][2] for z in range(2)],
        [lines[2, 2 * z, 0][2] for z in range(2)],
    ]
    return operator, chain, factors


reaches = ((-1, -1), (0, -1), (0, 0), (0, 1), (1, 0), (1, 1))


def taken(offset):
    return [(m, offset + 1 if m == -1 else offset) for m in (-1, 0, 1) if m * offset != -1]


def from_below(j, o):
    return (j, o) in ((-1, -1), (0, 0), (0, 1))


def reaching(j, o, source, odd):
    if (j, o) == (0, 1):
        return jnp.where(odd, 0.0, source)
    if (j, o) == (1, 0):
        return jnp.where(odd, source, 0.0)
    return source


def second_operator(operator, chain, rows, lanes, hold=None):
    odd = {1: rows % 2 == 1, 2: lanes % 2 == 1}
    depth = line_terms(chain[0][0], chain[0][1])[0]
    down, up = {}, {}
    for d in (1, 2):
        for z in range(2):
            here = chain[d][z]
            before = shifted(here, -int(d == 1), -int(d == 2))
            f, g = line_terms(before, here)[:2]
            down[d, z] = jnp.where(odd[d], f, 1.0)
            up[d, z] = jnp.where(odd[d], g, 1.0)
    down_z = {0: down[1, 0], 1: down[1, 1] * depth}
    up_z = {0: up[1, 0], 1: up[1, 1] * depth}

    def factors(d, lower, upper):
        base = {}
        for j, o in reaches:
            source = lower if from_below(j, o) else upper
            source = reaching(j, o, shifted(source, o if d == 1 else 0, o if d == 2 else 0), odd[d])
            if hold is not None and d == 1 and (j, o) == (1, 1):
                source = jnp.where(hold, 0.0, source)
            base[j, o] = source
        return {
            (j, o, across): shifted(base[j, o], 0 if d == 1 else across, across if d == 1 else 0)
            for j, o in reaches
            for across in (-1, 0, 1)
        }

    spread = {}
    for far in range(2):
        along_x = factors(1, down_z[far], up_z[far])
        along_y = factors(2, down[2, far], up[2, far])
        for jx, ox in reaches:
            for jy, oy in reaches:
                weight = along_x[jx, ox, oy] * along_y[jy, oy, ox]
                for z in range(2):
                    term = operator[(far - z, ox, oy), z] * weight
                    key = (z, jx, jy)
                    spread[key] = spread[key] + term if key in spread else term

    sides = {
        (z, d): {-1: up_z[z] if d == 1 else up[2, z], 0: depth if (d == 1 and z == 1) else None, 1: down_z[z] if d == 1 else down[2, z]}
        for z in range(2)
        for d in (1, 2)
    }
    own = {(z, mx, my): times(sides[z, 1][mx], sides[z, 2][my]) for z in range(2) for mx in (-1, 0, 1) for my in (-1, 0, 1)}

    results = {}
    for ox in (-1, 0, 1):
        for oy in (-1, 0, 1):
            total = None
            for my, jy in taken(oy):
                part = None
                for mx, jx in taken(ox):
                    term = times(own[0, mx, my], spread[0, jx, jy]) + times(own[1, mx, my], spread[1, jx, jy])
                    term = shifted(term, mx, 0)
                    part = term if part is None else part + term
                part = shifted(part, 0, my)
                total = part if total is None else total + part
            results[ox, oy] = total
    return results, own


def swap_order(row, edge, half, where):
    below_half, inner, at_half = (where(test, 1, 0) for test in (edge < half, row > 0, edge == half))
    cores_first, border = inner * below_half, inner * at_half
    order = cores_first * (edge % 2) + (1 - cores_first) * (1 - edge % 2)
    return border * 2 + (1 - border) * order


def own_swaps():
    row, column, size = lax.axis_index("gx"), lax.axis_index("gy"), lax.axis_size("gy")

    def order(edge):
        return swap_order(row, edge, size // 2, jnp.where)

    return jnp.where(column > 0, order(column - 1 + (column == 0)), -1), jnp.where(column < size - 1, order(column), -1)


def couplings_kernel(inputs_ref, own_ref, page_ref):
    lanes = lax.broadcasted_iota(jnp.int32, (ROWS, LANES), 1)
    page = jnp.zeros((ROWS, LANES), jnp.float32)
    eps = [permittivity(inputs_ref[0, z] & 3) for z in range(4)]
    for r in range(12):
        values = (inputs_ref[r // 4, r % 4] >> 2).astype(jnp.float32) * eps[r % 4]
        own_ref[r] = values
        page = jnp.where(lanes >= 5 * r + 1, pltpu.roll(values, 5 * r + 5, 1), page)
    page_ref[...] = page


def beside(column_refs):
    sides = []
    for swap in own_swaps():
        values = jnp.zeros((ROWS, LANES), jnp.float32)
        for k, ref in enumerate(column_refs):
            values = jnp.where(swap == k, ref[...], values)
        sides.append(values)
    lanes = lax.broadcasted_iota(jnp.int32, (ROWS, LANES), 1)
    return [jnp.where(lanes % 5 == 0, sides[1], sides[0])]


def edges_kernel(own_ref, third_columns_ref, second_columns_ref, first_columns_ref, far_ref, near_ref):
    odd_x = lax.axis_index("gx") % 2 == 1
    tiles = [own_ref[r] for r in range(12)] + beside((first_columns_ref, second_columns_ref, third_columns_ref))
    for r, values in enumerate(tiles):
        far_ref[r] = jnp.where(odd_x, values[4:8, :], values[0:4, :])
        near_ref[r] = jnp.where(odd_x, values[0:4, :], values[4:8, :])


def lane_picks(lanes):
    return (2 * lanes) % LANES, (lanes >= 126) | (lanes == 64), lanes >= 126


def columns_beside(tile, lanes):
    first = (lanes + 2) % LANES // 2 * 5 + 1 + 2 * (lanes % 2)
    above = (lanes - 64) // 2 * 5 + 5
    even = jnp.where((lanes >= 64) & (lanes < 112), above, first) % LANES
    return pick_lanes(tile, even), pick_lanes(tile, (first + 1) % LANES)


def split_lanes(values, r, edges, picks):
    even_lanes, at_even, at_odd = picks
    even = jnp.where(at_even, shifted(edges[0], 0, 2 * r), pick_lanes(values, even_lanes))
    odd = jnp.where(at_odd, shifted(edges[1], 0, 2 * r), pick_lanes(values, even_lanes + 1))
    return even, odd


def split_couplings(block, lanes):
    picks = lane_picks(lanes)
    c = [[[[None, None], [None, None]] for _ in range(4)] for _ in range(3)]
    for px in range(2):
        edges = columns_beside(block[12, pl.ds(px, 8, stride=2), :], lanes)
        for r in range(12):
            values = block[r, pl.ds(px, 8, stride=2), :]
            c[r // 4][r % 4][px][:] = split_lanes(values, r, edges, picks)
    return c


def places():
    rows = lax.broadcasted_iota(jnp.int32, (ROWS, LANES), 0)
    lanes = lax.broadcasted_iota(jnp.int32, (ROWS, LANES), 1)
    last_x = lax.axis_index("gx") == lax.axis_size("gx") - 1
    last_y = lax.axis_index("gy") == lax.axis_size("gy") - 1
    return rows, lanes, last_x, last_y


def operators(block, first_ref, second_ref, hold_row=None):
    rows, lanes, last_x, last_y = places()
    hold = None if hold_row is None else rows == hold_row
    c = split_couplings(block, lanes)
    operator, chain, factors = first_operator(c, edge_masks(last_x, last_y, rows, lanes, 1), hold)
    empty = jnp.zeros((ROWS, LANES), jnp.float32)
    full = {}
    for o in range(27):
        offset = (o // 9 - 1, o // 3 % 3 - 1, o % 3 - 1)
        for z in range(2):
            full[offset, z] = operator.get((offset, z), empty)
            first_ref[o // 9, o % 9, z] = full[offset, z][0:4, 0:64]
    results, own = second_operator(full, chain, rows, lanes, hold)
    masks = edge_masks(last_x, last_y, rows, lanes, 2)
    second_ref[...] = jnp.zeros(second_ref.shape, jnp.float32)
    for (ox, oy), values in results.items():
        compact = pick_lanes(dropped(values, ox, oy, masks), (2 * lanes) % LANES)
        second_ref[9 + (ox + 1) * 3 + oy + 1, 0, 0:1, :] = compact[0:1, 0:32]
        second_ref[9 + (ox + 1) * 3 + oy + 1, 0, 1:2, :] = compact[2:3, 0:32]
    return operator, factors, own


fix_entries = [((oz, 1, oy), z) for z in (0, 1) for oz in (-z, 1 - z) for oy in (-1, 0, 1)]
fix_factors = [
    (zc, qz, qy, (tz, 0, ty))
    for zc in (0, 1)
    for qz in (0, 1)
    for qy in (0, 1)
    if qz or qy
    for tz in range(1 + (qz if zc == 0 else 0))
    for ty in range(1 + qy)
]
fix_sides = [(z, 1, my) for z in (0, 1) for my in (-1, 0, 1)]
fix_count = len(fix_entries) + len(fix_factors) + len(fix_sides)


def early_kernel(
    own_ref, third_columns_ref, second_columns_ref, first_columns_ref, far_ref,
    first_ref, second_ref, kept_ref, block,
):
    tiles = [own_ref[r] for r in range(12)] + beside((first_columns_ref, second_columns_ref, third_columns_ref))
    for r, values in enumerate(tiles):
        block[r, 0:8, :] = values
        block[r, 8:12, :] = jnp.zeros((4, LANES), jnp.float32)
        block[r, 12:16, :] = far_ref[r]
    operator, factors, own = operators(block, first_ref, second_ref, ROWS // 2 - 1)
    kept = [operator[e] for e in fix_entries] + [factors[e] for e in fix_factors]
    kept += [own[e] for e in fix_sides]
    for i, values in enumerate(kept):
        kept_ref[i] = values


def add_row_above(near_ref, early_second_ref, kept_ref, first_ref, second_ref, send_first):
    rows, lanes, last_x, last_y = places()
    kept = {e: kept_ref[i] for i, e in enumerate(fix_entries + fix_factors + fix_sides)}

    def row(r):
        return jnp.broadcast_to(near_ref[r, 0:1, :], (ROWS, LANES))

    even_lanes, at_even, at_odd = lane_picks(lanes)
    tile = row(12)
    first = 1 + 2 * (lanes % 2)
    c = {}
    for d in (0, 2):
        for z in range(4):
            r = d * 4 + z
            values = row(r)
            even = pick_lanes(tile, jnp.where(at_odd, first, 5) + 5 * r)
            odd = pick_lanes(tile, first + (5 * r + 1))
            even = jnp.where(at_even, even, pick_lanes(values, even_lanes))
            c[d, z] = (even, jnp.where(at_odd, odd, pick_lanes(values, even_lanes + 1)))
    line_y = {z: line_terms(*c[2, z]) for z in range(4)}
    line_z = {(zc, py): line_terms(c[0, 2 * zc][py], c[0, 2 * zc + 1][py]) for zc in range(2) for py in range(2)}

    near_y = {(far, j): shifted(line_y[2 * far][2], 0, j) for far in range(2) for j in (-2, -1, 0, 1)}
    near_z = {(z, j): shifted(line_z[z, 0][2], 0, j) for z in range(2) for j in (-1, 0, 1)}
    odd = lanes % 2 == 1
    weights = {}
    for far in range(2):
        for oy in (-1, 0, 1):
            f, g = line_terms(near_y[far, oy - 1], near_y[far, oy])[:2]
            there = odd if oy == 0 else ~odd
            pair = jnp.where(there, f, 1.0), jnp.where(there, g, 1.0)
            if far == 1:
                depth = line_terms(near_z[0, oy], near_z[1, oy])[0]
                pair = pair[0] * depth, pair[1] * depth
            for jy, o in reaches:
                if o == oy:
                    weights[far, jy, oy] = reaching(jy, oy, pair[0 if from_below(jy, oy) else 1], odd)

    sums = {}
    for zc, qz, qy, t in fix_factors:
        pair_z = line_z[zc, qy][:2] if qz else (None,)
        pair_y = line_y[2 * zc + qz][:2] if qy else (None,)
        for uz in range(1 + (qz if zc == 0 else 0)):
            for uy in range(1 + qy):
                key = ((uz - t[0], 1, uy - t[2]), zc + t[0], t[2])
                term = kept[zc, qz, qy, t] * times(pair_z[uz], pair_y[uy])
                sums[key] = sums[key] + term if key in sums else term
    masks = edge_masks(last_x, last_y, rows, lanes, 1)
    entries = {}
    for offset, z in fix_entries:
        total = kept[offset, z]
        if (offset, z, 0) in sums:
            total = total - sums[offset, z, 0]
        if (offset, z, 1) in sums:
            total = total - shifted(sums[offset, z, 1], 0, -1)
        entries[offset, z] = dropped(total, *offset[1:], masks)
        whole = jnp.where(rows == ROWS // 2 - 1, entries[offset, z], kept[offset, z])
        first_ref[offset[0] + 1, offset[2] + 1, z] = whole[0:4, 0:64]
    for oz, z in ((0, 0), (2, 1)):
        for oy in range(3):
            first_ref[oz, oy, z] = jnp.zeros((4, 64), jnp.float32)
    send_first()

    spread = {}
    for far in range(2):
        for jy, oy in reaches:
            for z in range(2):
                term = entries[(far - z, 1, oy), z] * weights[far, jy, oy]
                spread[z, jy] = spread[z, jy] + term if (z, jy) in spread else term
    for oy in (-1, 0, 1):
        total = None
        for my, jy in taken(oy):
            part = kept[0, 1, my] * spread[0, jy] + kept[1, 1, my] * spread[1, jy]
            part = pick_lanes(part, (2 * lanes + my) % LANES)
            total = part if total is None else total + part
        total = jnp.where(last_x, 0.0, total)
        if oy == 1:
            total = jnp.where((lanes == LANES // 4 - 1) & last_y, 0.0, total)
        second_ref[oy + 1, 0, 0:1, :] = early_second_ref[16 + oy, 0, 0:1, :]
        row_two = early_second_ref[16 + oy, 0, 1:2, :]
        second_ref[oy + 1, 0, 1:2, :] = row_two + total[ROWS // 2 - 1:ROWS // 2, 0:32]


def last_kernel(
    own_ref, third_columns_ref, second_columns_ref, first_columns_ref, far_ref,
    early_first_ref, early_second_ref, kept_ref, near_ref,
    first_hbm, second_hbm, block, first_ref, second_ref, first_fix, second_fix, sems,
):
    odd_x = lax.axis_index("gx") % 2 == 1

    def send(parts):
        copies = [pltpu.make_async_copy(source, target, sems.at[i]) for i, source, target in parts]
        for copy in copies:
            copy.start()
        return copies

    @pl.when(odd_x)
    def _():
        tiles = [own_ref[r] for r in range(12)] + beside((first_columns_ref, second_columns_ref, third_columns_ref))
        for r, values in enumerate(tiles):
            block[r, 0:8, :] = values
            block[r, 8:12, :] = far_ref[r]
            block[r, 12:16, :] = near_ref[r]
        operators(block, first_ref, second_ref)
        for copy in send([(0, first_ref, first_hbm), (1, second_ref, second_hbm)]):
            copy.wait()

    @pl.when(jnp.logical_not(odd_x))
    def _():
        copies = []

        def send_first():
            copies.extend(send([
                (0, first_fix, first_hbm.at[:, pl.ds(6, 3)]),
                (1, early_first_ref.at[:, pl.ds(0, 6)], first_hbm.at[:, pl.ds(0, 6)]),
                (2, early_second_ref.at[pl.ds(0, 15)], second_hbm.at[pl.ds(0, 15)]),
                (3, early_second_ref.at[pl.ds(18, 9)], second_hbm.at[pl.ds(18, 9)]),
            ]))

        add_row_above(near_ref, early_second_ref, kept_ref, first_fix, second_fix, send_first)
        for copy in copies + send([(4, second_fix, second_hbm.at[pl.ds(15, 3)])]):
            copy.wait()


def swapped(values, axis, first):
    pairs = [(i, i + 1) for i in range(first, lax.axis_size(axis) - 1, 2)]
    return lax.ppermute(values, axis, pairs + [(b, a) for a, b in pairs])


def swapped_columns(values, which):
    count_x, count_y = lax.axis_size("gx"), lax.axis_size("gy")
    pairs = [
        (row * count_y + edge, row * count_y + edge + 1)
        for row in range(count_x)
        for edge in range(count_y - 1)
        if swap_order(row, edge, count_y // 2, np.where) == which
    ]
    return lax.ppermute(values, ("gx", "gy"), pairs + [(b, a) for a, b in pairs])


def body(material, face_open):
    whole = pl.BlockSpec(memory_space=pltpu.VMEM)
    page = jax.ShapeDtypeStruct((ROWS, LANES), jnp.float32)
    edge = jax.ShapeDtypeStruct((13, 4, LANES), jnp.float32)
    small = pltpu.CompilerParams(vmem_limit_bytes=1 << 20)
    own, columns = pl.pallas_call(
        couplings_kernel,
        out_shape=(jax.ShapeDtypeStruct((12, ROWS, LANES), jnp.float32), page),
        in_specs=[whole],
        out_specs=(whole,) * 2,
        compiler_params=small,
        name="couplings",
    )(face_open * 4 + material[None])
    columns = [swapped_columns(columns, k) for k in (2, 1, 0)]
    far, near = pl.pallas_call(
        edges_kernel,
        out_shape=(edge, edge),
        in_specs=[whole] * 4,
        out_specs=(whole,) * 2,
        compiler_params=small,
        name="edges",
    )(own, *columns)
    far_rows = swapped(far, "gx", 1)
    near_rows = swapped(near, "gx", 0)
    first = jax.ShapeDtypeStruct((3, 9, 2, 4, 64), jnp.float32)
    second = jax.ShapeDtypeStruct((27, 1, 2, 32), jnp.float32)
    large = pltpu.CompilerParams(vmem_limit_bytes=3 << 20)
    block = pltpu.VMEM((13, 16, LANES), jnp.float32)
    early = pl.pallas_call(
        early_kernel,
        out_shape=(first, second, jax.ShapeDtypeStruct((fix_count, ROWS, LANES), jnp.float32)),
        in_specs=[whole] * 5,
        out_specs=(whole,) * 3,
        scratch_shapes=[block],
        compiler_params=large,
        cost_estimate=pl.CostEstimate(flops=3 << 20, bytes_accessed=1 << 20, transcendentals=0),
        name="early",
    )(own, *columns, far_rows)
    first_level, second_level = pl.pallas_call(
        last_kernel,
        out_shape=(first, second),
        in_specs=[whole] * 9,
        out_specs=(pl.BlockSpec(memory_space=pltpu.HBM),) * 2,
        scratch_shapes=[
            block,
            pltpu.VMEM(first.shape, jnp.float32),
            pltpu.VMEM(second.shape, jnp.float32),
            pltpu.VMEM((3, 3, 2, 4, 64), jnp.float32),
            pltpu.VMEM((3, 1, 2, 32), jnp.float32),
            pltpu.SemaphoreType.DMA((5,)),
        ],
        compiler_params=large,
        name="last",
    )(own, *columns, far_rows, *early, near_rows)
    return first_level.reshape(27, 2, 4, 64), second_level


def solution(mesh):
    placed = (P(None, "gx", "gy"), P(None, None, "gx", "gy"))
    return jax.shard_map(
        body,
        mesh=mesh,
        in_specs=placed,
        out_specs=(P(None, None, "gx", "gy"), P(None, None, "gx", "gy")),
        check_vma=False,
    )
```

```python
import functools

import jax
import jax.numpy as jnp
import numpy as np
from jax import lax
from jax.experimental import pallas as pl
from jax.experimental.pallas import tpu as pltpu
from jax.sharding import PartitionSpec as P

permit_levels = (1.0 / 80.0 / 64.0, 4.0 / 80.0 / 64.0, 20.0 / 80.0 / 64.0, 1.0 / 64.0)

ROWS, LANES = 8, 128


def permittivity(material):
    values = jnp.full(material.shape, permit_levels[3], jnp.float32)
    for material_id in range(3):
        values = jnp.where(material == material_id, permit_levels[material_id], values)
    return values


def shifted(values, by_x, by_y):
    if by_x:
        values = pltpu.roll(values, (-by_x) % ROWS, 0)
    if by_y:
        values = pltpu.roll(values, (-by_y) % LANES, 1)
    return values


def pick_lanes(values, index):
    return jnp.take_along_axis(values, index, axis=1)


def times(a, b):
    if a is None:
        return b
    if b is None:
        return a
    return a * b


def minus(a, b):
    return (1.0 if a is None else a) - (1.0 if b is None else b)


def line_terms(lower, upper):
    total = lower + upper
    inverse = 1.0 / jnp.where(total > 0.0, total, 1.0)
    f = lower * inverse
    g = upper * inverse
    return f, g, lower * g, lower * f, upper * g


def edge_masks(last_x, last_y, rows, lanes, step):
    return (rows == ROWS // 2 - step) & last_x, (lanes == LANES // 2 - step) & last_y


def dropped(values, offset_x, offset_y, masks):
    if offset_x == 1:
        values = jnp.where(masks[0], 0.0, values)
    if offset_y == 1:
        values = jnp.where(masks[1], 0.0, values)
    return values


def first_operator(c, masks, hold=None):
    factors = {}
    lines = {}
    for z in range(4):
        for p in range(2):
            lines[1, z, p] = line_terms(c[1][z][0][p], c[1][z][1][p])
            lines[2, z, p] = line_terms(c[2][z][p][0], c[2][z][p][1])
    for zc in range(2):
        for px in range(2):
            for py in range(2):
                lines[0, zc, px, py] = line_terms(c[0][2 * zc][px][py], c[0][2 * zc + 1][px][py])

    rolled = {}

    def fraction(dim, zc, node, raised):
        pz, px, py = node
        if raised == 0:
            zc, raised = zc + 1, None
        if dim == 0:
            key = (0, zc, px, py)
        elif dim == 1:
            key = (1, 2 * zc + pz, py)
        else:
            key = (2, 2 * zc + pz, px)
        if raised is None:
            return lines[key][:2]
        if (key, raised) not in rolled:
            f = shifted(lines[key][0], int(raised == 1), int(raised == 2))
            rolled[key, raised] = (f, 1.0 - f)
        return rolled[key, raised]

    def transverse(d, zc, node, raised):
        dims = [dim for dim in range(3) if dim != d]
        entries = {(0, 0, 0): None}
        for dim in dims:
            if not node[dim]:
                continue
            pair = fraction(dim, zc, node, raised)
            fresh = {}
            for corner, weight in entries.items():
                for side in range(2):
                    moved = list(corner)
                    moved[dim] = side
                    if dim == 0 and side == 1 and zc == 1:
                        continue
                    fresh[tuple(moved)] = times(weight, pair[side])
            entries = fresh
        return entries

    sums = {}

    def put(zc, low, high, value):
        offset = tuple(b - a for a, b in zip(low, high))
        if offset < (0, 0, 0):
            low, high = high, low
            offset = tuple(-o for o in offset)
        if zc + low[0] > 1 or zc + high[0] > 1:
            return
        key = (offset, zc + low[0], low[1], low[2])
        sums[key] = sums[key] + value if key in sums else value

    for d in range(3):
        dims = [dim for dim in range(3) if dim != d]
        for zc in range(2):
            top = d == 0 and zc == 1
            for q1 in range(2):
                for q2 in range(2):
                    node = [0, 0, 0]
                    node[dims[0]], node[dims[1]] = q1, q2
                    odd = list(node)
                    odd[d] = 1
                    if d == 0:
                        key = (0, zc, node[1], node[2])
                    elif d == 1:
                        key = (1, 2 * zc + node[0], node[2])
                    else:
                        key = (2, 2 * zc + node[0], node[1])
                    _, _, s, h, k = lines[key]

                    def raised_corner(corner):
                        moved = list(corner)
                        moved[d] = 1
                        return tuple(moved)

                    zero = (0, 0, 0)
                    if not (q1 or q2):
                        put(zc, zero, zero, s)
                        if not top:
                            up = raised_corner(zero)
                            put(zc, up, up, s)
                            put(zc, zero, up, -s)
                        continue
                    alpha = transverse(d, zc, node, None)
                    beta = transverse(d, zc, odd, None)
                    corners = list(alpha)
                    delta = {t: minus(alpha[t], beta[t]) for t in corners}
                    for i, t in enumerate(corners):
                        s_alpha, h_delta = s * alpha[t], h * delta[t]
                        for u in corners[i:]:
                            put(zc, t, u, s_alpha * alpha[u] + h_delta * delta[u])
                    if top:
                        continue
                    gamma = transverse(d, zc, node, d)
                    epsilon = {t: minus(gamma[t], beta[t]) for t in corners}
                    for i, t in enumerate(corners):
                        s_gamma, k_epsilon = s * gamma[t], k * epsilon[t]
                        for u in corners[i:]:
                            put(zc, raised_corner(t), raised_corner(u), s_gamma * gamma[u] + k_epsilon * epsilon[u])
                    waiting = hold is not None and d == 1
                    for t in corners:
                        s_delta, s_beta = s * delta[t], s * beta[t]
                        if waiting:
                            factors[zc, q1, q2, t] = s_beta
                            s_beta = jnp.where(hold, 0.0, s_beta)
                        for u in corners:
                            put(zc, t, raised_corner(u), -(s_delta * beta[u] + s_beta * gamma[u]))

    operator = {}
    keys = sorted({(offset, z) for offset, z, _, _ in sums})
    for offset, z in keys:
        total = None
        for ax in range(2):
            part = sums.get((offset, z, ax, 0))
            side = sums.get((offset, z, ax, 1))
            if side is not None:
                side = shifted(side, 0, -1)
                part = side if part is None else part + side
            if part is None:
                continue
            part = shifted(part, -ax, 0)
            total = part if total is None else total + part
        operator[offset, z] = dropped(total, *offset[1:], masks)
        if offset != (0, 0, 0):
            mirror = tuple(-o for o in offset)
            operator[mirror, z + offset[0]] = dropped(shifted(total, -offset[1], -offset[2]), *mirror[1:], masks)

    chain = [
        [lines[0, z, 0, 0][2] for z in range(2)],
        [lines[1, 2 * z, 0][2] for z in range(2)],
        [lines[2, 2 * z, 0][2] for z in range(2)],
    ]
    return operator, chain, factors


reaches = ((-1, -1), (0, -1), (0, 0), (0, 1), (1, 0), (1, 1))


def taken(offset):
    return [(m, offset + 1 if m == -1 else offset) for m in (-1, 0, 1) if m * offset != -1]


def from_below(j, o):
    return (j, o) in ((-1, -1), (0, 0), (0, 1))


def reaching(j, o, source, odd):
    if (j, o) == (0, 1):
        return jnp.where(odd, 0.0, source)
    if (j, o) == (1, 0):
        return jnp.where(odd, source, 0.0)
    return source


def second_operator(operator, chain, rows, lanes, hold=None):
    odd = {1: rows % 2 == 1, 2: lanes % 2 == 1}
    depth = line_terms(chain[0][0], chain[0][1])[0]
    down, up = {}, {}
    for d in (1, 2):
        for z in range(2):
            here = chain[d][z]
            before = shifted(here, -int(d == 1), -int(d == 2))
            f, g = line_terms(before, here)[:2]
            down[d, z] = jnp.where(odd[d], f, 1.0)
            up[d, z] = jnp.where(odd[d], g, 1.0)
    down_z = {0: down[1, 0], 1: down[1, 1] * depth}
    up_z = {0: up[1, 0], 1: up[1, 1] * depth}

    def factors(d, lower, upper):
        base = {}
        for j, o in reaches:
            source = lower if from_below(j, o) else upper
            source = reaching(j, o, shifted(source, o if d == 1 else 0, o if d == 2 else 0), odd[d])
            if hold is not None and d == 1 and (j, o) == (1, 1):
                source = jnp.where(hold, 0.0, source)
            base[j, o] = source
        return {
            (j, o, across): shifted(base[j, o], 0 if d == 1 else across, across if d == 1 else 0)
            for j, o in reaches
            for across in (-1, 0, 1)
        }

    spread = {}
    for far in range(2):
        along_x = factors(1, down_z[far], up_z[far])
        along_y = factors(2, down[2, far], up[2, far])
        for jx, ox in reaches:
            for jy, oy in reaches:
                weight = along_x[jx, ox, oy] * along_y[jy, oy, ox]
                for z in range(2):
                    term = operator[(far - z, ox, oy), z] * weight
                    key = (z, jx, jy)
                    spread[key] = spread[key] + term if key in spread else term

    sides = {
        (z, d): {-1: up_z[z] if d == 1 else up[2, z], 0: depth if (d == 1 and z == 1) else None, 1: down_z[z] if d == 1 else down[2, z]}
        for z in range(2)
        for d in (1, 2)
    }
    own = {(z, mx, my): times(sides[z, 1][mx], sides[z, 2][my]) for z in range(2) for mx in (-1, 0, 1) for my in (-1, 0, 1)}

    results = {}
    for ox in (-1, 0, 1):
        for oy in (-1, 0, 1):
            total = None
            for my, jy in taken(oy):
                part = None
                for mx, jx in taken(ox):
                    term = times(own[0, mx, my], spread[0, jx, jy]) + times(own[1, mx, my], spread[1, jx, jy])
                    term = shifted(term, mx, 0)
                    part = term if part is None else part + term
                part = shifted(part, 0, my)
                total = part if total is None else total + part
            results[ox, oy] = total
    return results, own


def swap_order(row, edge, half, where):
    below_half, inner, at_half = (where(test, 1, 0) for test in (edge < half, row > 0, edge == half))
    cores_first, border = inner * below_half, inner * at_half
    order = cores_first * (edge % 2) + (1 - cores_first) * (1 - edge % 2)
    return border * 2 + (1 - border) * order


def own_swaps():
    row, column, size = lax.axis_index("gx"), lax.axis_index("gy"), lax.axis_size("gy")

    def order(edge):
        return swap_order(row, edge, size // 2, jnp.where)

    return jnp.where(column > 0, order(column - 1 + (column == 0)), -1), jnp.where(column < size - 1, order(column), -1)


def couplings_kernel(inputs_ref, own_ref, *message_refs):
    lanes = lax.broadcasted_iota(jnp.int32, (ROWS, LANES), 1)
    low = jnp.zeros((ROWS, LANES), jnp.float32)
    high = jnp.zeros((ROWS, LANES), jnp.float32)
    eps = [permittivity(inputs_ref[0, z] & 3) for z in range(4)]
    for r in range(12):
        values = (inputs_ref[r // 4, r % 4] >> 2).astype(jnp.float32) * eps[r % 4]
        own_ref[r] = values
        turned = pltpu.roll(values, 4 * r + 4, 1)
        low = jnp.where((lanes >= 4 * r) & (lanes < 4 * r + 4), turned, low)
        high = jnp.where(lanes == 4 * r + 4, turned, high)
    _, above = own_swaps()
    for k, ref in enumerate(message_refs):
        ref[...] = jnp.where(above == k, low, high)


def beside(column_refs):
    sides = []
    for swap in own_swaps():
        values = jnp.zeros((ROWS, LANES), jnp.float32)
        for k, ref in enumerate(column_refs):
            values = jnp.where(swap == k, ref[...], values)
        sides.append(values)
    return sides


def edges_kernel(own_ref, first_columns_ref, second_columns_ref, third_columns_ref, far_ref, near_ref):
    odd_x = lax.axis_index("gx") % 2 == 1
    tiles = [own_ref[r] for r in range(12)] + beside((first_columns_ref, second_columns_ref, third_columns_ref))
    for r, values in enumerate(tiles):
        far_ref[r] = jnp.where(odd_x, values[4:8, :], values[0:4, :])
        near_ref[r] = jnp.where(odd_x, values[0:4, :], values[4:8, :])


def lane_picks(lanes):
    source = ((lanes + 2) % LANES // 2 * 4 + 2 * (lanes % 2)) % LANES
    return source, (2 * lanes) % LANES, (lanes >= 126) | (lanes == 64), lanes >= 126


def columns_beside(left, right, lanes, source):
    above = pick_lanes(right, (2 * lanes + 4) % LANES)
    even = jnp.where((lanes >= 64) & (lanes < 112), above, pick_lanes(left, source))
    return even, pick_lanes(left, (source + 1) % LANES)


def split_lanes(values, r, edges, picks):
    _, even_lanes, at_even, at_odd = picks
    even = jnp.where(at_even, shifted(edges[0], 0, 2 * r), pick_lanes(values, even_lanes))
    odd = jnp.where(at_odd, shifted(edges[1], 0, 2 * r), pick_lanes(values, even_lanes + 1))
    return even, odd


def split_couplings(block, lanes):
    picks = lane_picks(lanes)
    c = [[[[None, None], [None, None]] for _ in range(4)] for _ in range(3)]
    for px in range(2):
        left = block[12, pl.ds(px, 8, stride=2), :]
        right = block[13, pl.ds(px, 8, stride=2), :]
        edges = columns_beside(left, right, lanes, picks[0])
        for r in range(12):
            values = block[r, pl.ds(px, 8, stride=2), :]
            c[r // 4][r % 4][px][:] = split_lanes(values, r, edges, picks)
    return c


def places():
    rows = lax.broadcasted_iota(jnp.int32, (ROWS, LANES), 0)
    lanes = lax.broadcasted_iota(jnp.int32, (ROWS, LANES), 1)
    last_x = lax.axis_index("gx") == lax.axis_size("gx") - 1
    last_y = lax.axis_index("gy") == lax.axis_size("gy") - 1
    return rows, lanes, last_x, last_y


def operators(block, first_ref, second_ref, hold_row=None):
    rows, lanes, last_x, last_y = places()
    hold = None if hold_row is None else rows == hold_row
    c = split_couplings(block, lanes)
    operator, chain, factors = first_operator(c, edge_masks(last_x, last_y, rows, lanes, 1), hold)
    empty = jnp.zeros((ROWS, LANES), jnp.float32)
    full = {}
    for o in range(27):
        offset = (o // 9 - 1, o // 3 % 3 - 1, o % 3 - 1)
        for z in range(2):
            full[offset, z] = operator.get((offset, z), empty)
            first_ref[o // 9, o % 9, z] = full[offset, z][0:4, 0:64]
    results, own = second_operator(full, chain, rows, lanes, hold)
    masks = edge_masks(last_x, last_y, rows, lanes, 2)
    second_ref[...] = jnp.zeros(second_ref.shape, jnp.float32)
    for (ox, oy), values in results.items():
        compact = pick_lanes(dropped(values, ox, oy, masks), (2 * lanes) % LANES)
        second_ref[9 + (ox + 1) * 3 + oy + 1, 0, 0:1, :] = compact[0:1, 0:32]
        second_ref[9 + (ox + 1) * 3 + oy + 1, 0, 1:2, :] = compact[2:3, 0:32]
    return operator, factors, own


fix_entries = [((oz, 1, oy), z) for z in (0, 1) for oz in (-z, 1 - z) for oy in (-1, 0, 1)]
fix_factors = [
    (zc, qz, qy, (tz, 0, ty))
    for zc in (0, 1)
    for qz in (0, 1)
    for qy in (0, 1)
    if qz or qy
    for tz in range(1 + (qz if zc == 0 else 0))
    for ty in range(1 + qy)
]
fix_sides = [(z, 1, my) for z in (0, 1) for my in (-1, 0, 1)]
fix_count = len(fix_entries) + len(fix_factors) + len(fix_sides)


def early_kernel(
    own_ref, first_columns_ref, second_columns_ref, third_columns_ref, far_ref,
    first_ref, second_ref, kept_ref, block,
):
    tiles = [own_ref[r] for r in range(12)] + beside((first_columns_ref, second_columns_ref, third_columns_ref))
    for r, values in enumerate(tiles):
        block[r, 0:8, :] = values
        block[r, 8:12, :] = jnp.zeros((4, LANES), jnp.float32)
        block[r, 12:16, :] = far_ref[r]
    operator, factors, own = operators(block, first_ref, second_ref, ROWS // 2 - 1)
    kept = [operator[e] for e in fix_entries] + [factors[e] for e in fix_factors]
    kept += [own[e] for e in fix_sides]
    for i, values in enumerate(kept):
        kept_ref[i] = values


def add_row_above(near_ref, early_second_ref, kept_ref, first_ref, second_ref, send_first):
    rows, lanes, last_x, last_y = places()
    kept = {e: kept_ref[i] for i, e in enumerate(fix_entries + fix_factors + fix_sides)}

    def row(r):
        return jnp.broadcast_to(near_ref[r, 0:1, :], (ROWS, LANES))

    _, even_lanes, at_even, at_odd = lane_picks(lanes)
    left, right = row(12), row(13)
    in_left = 2 * (lanes % 2)
    c = {}
    for d in (0, 2):
        for z in range(4):
            r = d * 4 + z
            values = row(r)
            below = [pick_lanes(left, in_left + (4 * r + py)) for py in range(2)]
            above = pick_lanes(right, jnp.full((ROWS, LANES), 4 * r + 4, jnp.int32))
            even = jnp.where(at_even, jnp.where(at_odd, below[0], above), pick_lanes(values, even_lanes))
            c[d, z] = (even, jnp.where(at_odd, below[1], pick_lanes(values, even_lanes + 1)))
    line_y = {z: line_terms(*c[2, z]) for z in range(4)}
    line_z = {(zc, py): line_terms(c[0, 2 * zc][py], c[0, 2 * zc + 1][py]) for zc in range(2) for py in range(2)}

    near_y = {(far, j): shifted(line_y[2 * far][2], 0, j) for far in range(2) for j in (-2, -1, 0, 1)}
    near_z = {(z, j): shifted(line_z[z, 0][2], 0, j) for z in range(2) for j in (-1, 0, 1)}
    odd = lanes % 2 == 1
    weights = {}
    for far in range(2):
        for oy in (-1, 0, 1):
            f, g = line_terms(near_y[far, oy - 1], near_y[far, oy])[:2]
            there = odd if oy == 0 else ~odd
            pair = jnp.where(there, f, 1.0), jnp.where(there, g, 1.0)
            if far == 1:
                depth = line_terms(near_z[0, oy], near_z[1, oy])[0]
                pair = pair[0] * depth, pair[1] * depth
            for jy, o in reaches:
                if o == oy:
                    weights[far, jy, oy] = reaching(jy, oy, pair[0 if from_below(jy, oy) else 1], odd)

    sums = {}
    for zc, qz, qy, t in fix_factors:
        pair_z = line_z[zc, qy][:2] if qz else (None,)
        pair_y = line_y[2 * zc + qz][:2] if qy else (None,)
        for uz in range(1 + (qz if zc == 0 else 0)):
            for uy in range(1 + qy):
                key = ((uz - t[0], 1, uy - t[2]), zc + t[0], t[2])
                term = kept[zc, qz, qy, t] * times(pair_z[uz], pair_y[uy])
                sums[key] = sums[key] + term if key in sums else term
    masks = edge_masks(last_x, last_y, rows, lanes, 1)
    entries = {}
    for offset, z in fix_entries:
        total = kept[offset, z]
        if (offset, z, 0) in sums:
            total = total - sums[offset, z, 0]
        if (offset, z, 1) in sums:
            total = total - shifted(sums[offset, z, 1], 0, -1)
        entries[offset, z] = dropped(total, *offset[1:], masks)
        whole = jnp.where(rows == ROWS // 2 - 1, entries[offset, z], kept[offset, z])
        first_ref[offset[0] + 1, offset[2] + 1, z] = whole[0:4, 0:64]
    for oz, z in ((0, 0), (2, 1)):
        for oy in range(3):
            first_ref[oz, oy, z] = jnp.zeros((4, 64), jnp.float32)
    send_first()

    spread = {}
    for far in range(2):
        for jy, oy in reaches:
            for z in range(2):
                term = entries[(far - z, 1, oy), z] * weights[far, jy, oy]
                spread[z, jy] = spread[z, jy] + term if (z, jy) in spread else term
    for oy in (-1, 0, 1):
        total = None
        for my, jy in taken(oy):
            part = kept[0, 1, my] * spread[0, jy] + kept[1, 1, my] * spread[1, jy]
            part = pick_lanes(part, (2 * lanes + my) % LANES)
            total = part if total is None else total + part
        total = jnp.where(last_x, 0.0, total)
        if oy == 1:
            total = jnp.where((lanes == LANES // 4 - 1) & last_y, 0.0, total)
        second_ref[oy + 1, 0, 0:1, :] = early_second_ref[16 + oy, 0, 0:1, :]
        row_two = early_second_ref[16 + oy, 0, 1:2, :]
        second_ref[oy + 1, 0, 1:2, :] = row_two + total[ROWS // 2 - 1:ROWS // 2, 0:32]


def last_kernel(
    own_ref, first_columns_ref, second_columns_ref, third_columns_ref, far_ref,
    early_first_ref, early_second_ref, kept_ref, near_ref,
    first_hbm, second_hbm, block, first_ref, second_ref, first_fix, second_fix, sems,
):
    odd_x = lax.axis_index("gx") % 2 == 1

    def send(parts):
        copies = [pltpu.make_async_copy(source, target, sems.at[i]) for i, source, target in parts]
        for copy in copies:
            copy.start()
        return copies

    @pl.when(odd_x)
    def _():
        tiles = [own_ref[r] for r in range(12)] + beside((first_columns_ref, second_columns_ref, third_columns_ref))
        for r, values in enumerate(tiles):
            block[r, 0:8, :] = values
            block[r, 8:12, :] = far_ref[r]
            block[r, 12:16, :] = near_ref[r]
        operators(block, first_ref, second_ref)
        for copy in send([(0, first_ref, first_hbm), (1, second_ref, second_hbm)]):
            copy.wait()

    @pl.when(jnp.logical_not(odd_x))
    def _():
        copies = []

        def send_first():
            copies.extend(send([
                (0, first_fix, first_hbm.at[:, pl.ds(6, 3)]),
                (1, early_first_ref.at[:, pl.ds(0, 6)], first_hbm.at[:, pl.ds(0, 6)]),
                (2, early_second_ref.at[pl.ds(0, 15)], second_hbm.at[pl.ds(0, 15)]),
                (3, early_second_ref.at[pl.ds(18, 9)], second_hbm.at[pl.ds(18, 9)]),
            ]))

        add_row_above(near_ref, early_second_ref, kept_ref, first_fix, second_fix, send_first)
        for copy in copies + send([(4, second_fix, second_hbm.at[pl.ds(15, 3)])]):
            copy.wait()


def swapped(values, axis, first):
    pairs = [(i, i + 1) for i in range(first, lax.axis_size(axis) - 1, 2)]
    return lax.ppermute(values, axis, pairs + [(b, a) for a, b in pairs])


def swapped_columns(values, which):
    count_x, count_y = lax.axis_size("gx"), lax.axis_size("gy")
    pairs = [
        (row * count_y + edge, row * count_y + edge + 1)
        for row in range(count_x)
        for edge in range(count_y - 1)
        if swap_order(row, edge, count_y // 2, np.where) == which
    ]
    return lax.ppermute(values, ("gx", "gy"), pairs + [(b, a) for a, b in pairs])


def body(material, face_open):
    whole = pl.BlockSpec(memory_space=pltpu.VMEM)
    page = jax.ShapeDtypeStruct((ROWS, LANES), jnp.float32)
    edge = jax.ShapeDtypeStruct((14, 4, LANES), jnp.float32)
    small = pltpu.CompilerParams(vmem_limit_bytes=1 << 20)
    own, *messages = pl.pallas_call(
        couplings_kernel,
        out_shape=(jax.ShapeDtypeStruct((12, ROWS, LANES), jnp.float32),) + (page,) * 3,
        in_specs=[whole],
        out_specs=(whole,) * 4,
        compiler_params=small,
        name="couplings",
    )(face_open * 4 + material[None])
    columns = [swapped_columns(message, k) for k, message in enumerate(messages)]
    far, near = pl.pallas_call(
        edges_kernel,
        out_shape=(edge, edge),
        in_specs=[whole] * 4,
        out_specs=(whole,) * 2,
        compiler_params=small,
        name="edges",
    )(own, *columns)
    far_rows = swapped(far, "gx", 1)
    near_rows = swapped(near, "gx", 0)
    first = jax.ShapeDtypeStruct((3, 9, 2, 4, 64), jnp.float32)
    second = jax.ShapeDtypeStruct((27, 1, 2, 32), jnp.float32)
    large = pltpu.CompilerParams(vmem_limit_bytes=3 << 20)
    block = pltpu.VMEM((14, 24, LANES), jnp.float32)
    early = pl.pallas_call(
        early_kernel,
        out_shape=(first, second, jax.ShapeDtypeStruct((fix_count, ROWS, LANES), jnp.float32)),
        in_specs=[whole] * 5,
        out_specs=(whole,) * 3,
        scratch_shapes=[block],
        compiler_params=large,
        cost_estimate=pl.CostEstimate(flops=3 << 20, bytes_accessed=1 << 20, transcendentals=0),
        name="early",
    )(own, *columns, far_rows)
    first_level, second_level = pl.pallas_call(
        last_kernel,
        out_shape=(first, second),
        in_specs=[whole] * 9,
        out_specs=(pl.BlockSpec(memory_space=pltpu.HBM),) * 2,
        scratch_shapes=[
            block,
            pltpu.VMEM(first.shape, jnp.float32),
            pltpu.VMEM(second.shape, jnp.float32),
            pltpu.VMEM((3, 3, 2, 4, 64), jnp.float32),
            pltpu.VMEM((3, 1, 2, 32), jnp.float32),
            pltpu.SemaphoreType.DMA((5,)),
        ],
        compiler_params=large,
        name="last",
    )(own, *columns, far_rows, *early, near_rows)
    return first_level.reshape(27, 2, 4, 64), second_level


def solution(mesh):
    placed = (P(None, "gx", "gy"), P(None, None, "gx", "gy"))
    return jax.shard_map(
        body,
        mesh=mesh,
        in_specs=placed,
        out_specs=(P(None, None, "gx", "gy"), P(None, None, "gx", "gy")),
        check_vma=False,
    )
```

```python
import functools

import jax
import jax.numpy as jnp
import numpy as np
from jax import lax
from jax.experimental import pallas as pl
from jax.experimental.pallas import tpu as pltpu
from jax.sharding import PartitionSpec as P

permit_levels = (1.0 / 80.0 / 64.0, 4.0 / 80.0 / 64.0, 20.0 / 80.0 / 64.0, 1.0 / 64.0)

ROWS, LANES = 8, 128


def permittivity(material):
    values = jnp.full(material.shape, permit_levels[3], jnp.float32)
    for material_id in range(3):
        values = jnp.where(material == material_id, permit_levels[material_id], values)
    return values


def shifted(values, by_x, by_y):
    if by_x:
        values = pltpu.roll(values, (-by_x) % ROWS, 0)
    if by_y:
        values = pltpu.roll(values, (-by_y) % LANES, 1)
    return values


def pick_lanes(values, index):
    return jnp.take_along_axis(values, index, axis=1)


def times(a, b):
    if a is None:
        return b
    if b is None:
        return a
    return a * b


def minus(a, b):
    return (1.0 if a is None else a) - (1.0 if b is None else b)


def line_terms(lower, upper):
    total = lower + upper
    inverse = 1.0 / jnp.where(total > 0.0, total, 1.0)
    f = lower * inverse
    g = upper * inverse
    return f, g, lower * g, lower * f, upper * g


def edge_masks(last_x, last_y, rows, lanes, step):
    return (rows == ROWS // 2 - step) & last_x, (lanes == LANES // 2 - step) & last_y


def dropped(values, offset_x, offset_y, masks):
    if offset_x == 1:
        values = jnp.where(masks[0], 0.0, values)
    if offset_y == 1:
        values = jnp.where(masks[1], 0.0, values)
    return values


def first_operator(c, masks, hold=None):
    factors = {}
    lines = {}
    for z in range(4):
        for p in range(2):
            lines[1, z, p] = line_terms(c[1][z][0][p], c[1][z][1][p])
            lines[2, z, p] = line_terms(c[2][z][p][0], c[2][z][p][1])
    for zc in range(2):
        for px in range(2):
            for py in range(2):
                lines[0, zc, px, py] = line_terms(c[0][2 * zc][px][py], c[0][2 * zc + 1][px][py])

    rolled = {}

    def fraction(dim, zc, node, raised):
        pz, px, py = node
        if raised == 0:
            zc, raised = zc + 1, None
        if dim == 0:
            key = (0, zc, px, py)
        elif dim == 1:
            key = (1, 2 * zc + pz, py)
        else:
            key = (2, 2 * zc + pz, px)
        if raised is None:
            return lines[key][:2]
        if (key, raised) not in rolled:
            f = shifted(lines[key][0], int(raised == 1), int(raised == 2))
            rolled[key, raised] = (f, 1.0 - f)
        return rolled[key, raised]

    def transverse(d, zc, node, raised):
        dims = [dim for dim in range(3) if dim != d]
        entries = {(0, 0, 0): None}
        for dim in dims:
            if not node[dim]:
                continue
            pair = fraction(dim, zc, node, raised)
            fresh = {}
            for corner, weight in entries.items():
                for side in range(2):
                    moved = list(corner)
                    moved[dim] = side
                    if dim == 0 and side == 1 and zc == 1:
                        continue
                    fresh[tuple(moved)] = times(weight, pair[side])
            entries = fresh
        return entries

    sums = {}

    def put(zc, low, high, value):
        offset = tuple(b - a for a, b in zip(low, high))
        if offset < (0, 0, 0):
            low, high = high, low
            offset = tuple(-o for o in offset)
        if zc + low[0] > 1 or zc + high[0] > 1:
            return
        key = (offset, zc + low[0], low[1], low[2])
        sums[key] = sums[key] + value if key in sums else value

    for d in range(3):
        dims = [dim for dim in range(3) if dim != d]
        for zc in range(2):
            top = d == 0 and zc == 1
            for q1 in range(2):
                for q2 in range(2):
                    node = [0, 0, 0]
                    node[dims[0]], node[dims[1]] = q1, q2
                    odd = list(node)
                    odd[d] = 1
                    if d == 0:
                        key = (0, zc, node[1], node[2])
                    elif d == 1:
                        key = (1, 2 * zc + node[0], node[2])
                    else:
                        key = (2, 2 * zc + node[0], node[1])
                    _, _, s, h, k = lines[key]

                    def raised_corner(corner):
                        moved = list(corner)
                        moved[d] = 1
                        return tuple(moved)

                    zero = (0, 0, 0)
                    if not (q1 or q2):
                        put(zc, zero, zero, s)
                        if not top:
                            up = raised_corner(zero)
                            put(zc, up, up, s)
                            put(zc, zero, up, -s)
                        continue
                    alpha = transverse(d, zc, node, None)
                    beta = transverse(d, zc, odd, None)
                    corners = list(alpha)
                    delta = {t: minus(alpha[t], beta[t]) for t in corners}
                    for i, t in enumerate(corners):
                        s_alpha, h_delta = s * alpha[t], h * delta[t]
                        for u in corners[i:]:
                            put(zc, t, u, s_alpha * alpha[u] + h_delta * delta[u])
                    if top:
                        continue
                    gamma = transverse(d, zc, node, d)
                    epsilon = {t: minus(gamma[t], beta[t]) for t in corners}
                    for i, t in enumerate(corners):
                        s_gamma, k_epsilon = s * gamma[t], k * epsilon[t]
                        for u in corners[i:]:
                            put(zc, raised_corner(t), raised_corner(u), s_gamma * gamma[u] + k_epsilon * epsilon[u])
                    waiting = hold is not None and d == 1
                    for t in corners:
                        s_delta, s_beta = s * delta[t], s * beta[t]
                        if waiting:
                            factors[zc, q1, q2, t] = s_beta
                            s_beta = jnp.where(hold, 0.0, s_beta)
                        for u in corners:
                            put(zc, t, raised_corner(u), -(s_delta * beta[u] + s_beta * gamma[u]))

    operator = {}
    keys = sorted({(offset, z) for offset, z, _, _ in sums})
    for offset, z in keys:
        total = None
        for ax in range(2):
            part = sums.get((offset, z, ax, 0))
            side = sums.get((offset, z, ax, 1))
            if side is not None:
                side = shifted(side, 0, -1)
                part = side if part is None else part + side
            if part is None:
                continue
            part = shifted(part, -ax, 0)
            total = part if total is None else total + part
        operator[offset, z] = dropped(total, *offset[1:], masks)
        if offset != (0, 0, 0):
            mirror = tuple(-o for o in offset)
            operator[mirror, z + offset[0]] = dropped(shifted(total, -offset[1], -offset[2]), *mirror[1:], masks)

    chain = [
        [lines[0, z, 0, 0][2] for z in range(2)],
        [lines[1, 2 * z, 0][2] for z in range(2)],
        [lines[2, 2 * z, 0][2] for z in range(2)],
    ]
    return operator, chain, factors


reaches = ((-1, -1), (0, -1), (0, 0), (0, 1), (1, 0), (1, 1))


def taken(offset):
    return [(m, offset + 1 if m == -1 else offset) for m in (-1, 0, 1) if m * offset != -1]


def from_below(j, o):
    return (j, o) in ((-1, -1), (0, 0), (0, 1))


def reaching(j, o, source, odd):
    if (j, o) == (0, 1):
        return jnp.where(odd, 0.0, source)
    if (j, o) == (1, 0):
        return jnp.where(odd, source, 0.0)
    return source


def second_operator(operator, chain, rows, lanes, hold=None):
    odd = {1: rows % 2 == 1, 2: lanes % 2 == 1}
    depth = line_terms(chain[0][0], chain[0][1])[0]
    down, up = {}, {}
    for d in (1, 2):
        for z in range(2):
            here = chain[d][z]
            before = shifted(here, -int(d == 1), -int(d == 2))
            f, g = line_terms(before, here)[:2]
            down[d, z] = jnp.where(odd[d], f, 1.0)
            up[d, z] = jnp.where(odd[d], g, 1.0)
    down_z = {0: down[1, 0], 1: down[1, 1] * depth}
    up_z = {0: up[1, 0], 1: up[1, 1] * depth}

    def factors(d, lower, upper):
        base = {}
        for j, o in reaches:
            source = lower if from_below(j, o) else upper
            source = reaching(j, o, shifted(source, o if d == 1 else 0, o if d == 2 else 0), odd[d])
            if hold is not None and d == 1 and (j, o) == (1, 1):
                source = jnp.where(hold, 0.0, source)
            base[j, o] = source
        return {
            (j, o, across): shifted(base[j, o], 0 if d == 1 else across, across if d == 1 else 0)
            for j, o in reaches
            for across in (-1, 0, 1)
        }

    spread = {}
    for far in range(2):
        along_x = factors(1, down_z[far], up_z[far])
        along_y = factors(2, down[2, far], up[2, far])
        for jx, ox in reaches:
            for jy, oy in reaches:
                weight = along_x[jx, ox, oy] * along_y[jy, oy, ox]
                for z in range(2):
                    term = operator[(far - z, ox, oy), z] * weight
                    key = (z, jx, jy)
                    spread[key] = spread[key] + term if key in spread else term

    sides = {
        (z, d): {-1: up_z[z] if d == 1 else up[2, z], 0: depth if (d == 1 and z == 1) else None, 1: down_z[z] if d == 1 else down[2, z]}
        for z in range(2)
        for d in (1, 2)
    }
    own = {(z, mx, my): times(sides[z, 1][mx], sides[z, 2][my]) for z in range(2) for mx in (-1, 0, 1) for my in (-1, 0, 1)}

    results = {}
    for ox in (-1, 0, 1):
        for oy in (-1, 0, 1):
            total = None
            for my, jy in taken(oy):
                part = None
                for mx, jx in taken(ox):
                    term = times(own[0, mx, my], spread[0, jx, jy]) + times(own[1, mx, my], spread[1, jx, jy])
                    term = shifted(term, mx, 0)
                    part = term if part is None else part + term
                part = shifted(part, 0, my)
                total = part if total is None else total + part
            results[ox, oy] = total
    return results, own


def swap_order(row, edge, half, where):
    below_half, inner, at_half = (where(test, 1, 0) for test in (edge < half, row > 0, edge == half))
    cores_first, border = inner * below_half, inner * at_half
    order = cores_first * (edge % 2) + (1 - cores_first) * (1 - edge % 2)
    return border * 2 + (1 - border) * order


def own_swaps():
    row, column, size = lax.axis_index("gx"), lax.axis_index("gy"), lax.axis_size("gy")

    def order(edge):
        return swap_order(row, edge, size // 2, jnp.where)

    return jnp.where(column > 0, order(column - 1 + (column == 0)), -1), jnp.where(column < size - 1, order(column), -1)


def couplings_kernel(inputs_ref, own_ref, *page_refs):
    lanes = lax.broadcasted_iota(jnp.int32, (ROWS, LANES), 1)
    page = jnp.zeros((ROWS, LANES), jnp.float32)
    eps = [permittivity(inputs_ref[0, z] & 3) for z in range(4)]
    for r in range(12):
        values = (inputs_ref[r // 4, r % 4] >> 2).astype(jnp.float32) * eps[r % 4]
        own_ref[r] = values
        page = jnp.where(lanes >= 5 * r + 1, pltpu.roll(values, 5 * r + 5, 1), page)
    for page_ref in page_refs:
        page_ref[...] = page


def beside(column_refs):
    sides = []
    for swap in own_swaps():
        values = jnp.zeros((ROWS, LANES), jnp.float32)
        for k, ref in enumerate(column_refs):
            values = jnp.where(swap == k, ref[...], values)
        sides.append(values)
    lanes = lax.broadcasted_iota(jnp.int32, (ROWS, LANES), 1)
    return [jnp.where(lanes % 5 == 0, sides[1], sides[0])]


def edges_kernel(own_ref, first_columns_ref, second_columns_ref, third_columns_ref, far_ref, near_ref):
    odd_x = lax.axis_index("gx") % 2 == 1
    tiles = [own_ref[r] for r in range(12)] + beside((first_columns_ref, second_columns_ref, third_columns_ref))
    for r, values in enumerate(tiles):
        far_ref[r] = jnp.where(odd_x, values[4:8, :], values[0:4, :])
        near_ref[r] = jnp.where(odd_x, values[0:4, :], values[4:8, :])


def lane_picks(lanes):
    return (2 * lanes) % LANES, (lanes >= 126) | (lanes == 64), lanes >= 126


def columns_beside(tile, lanes):
    first = (lanes + 2) % LANES // 2 * 5 + 1 + 2 * (lanes % 2)
    above = (lanes - 64) // 2 * 5 + 5
    even = jnp.where((lanes >= 64) & (lanes < 112), above, first) % LANES
    return pick_lanes(tile, even), pick_lanes(tile, (first + 1) % LANES)


def split_lanes(values, r, edges, picks):
    even_lanes, at_even, at_odd = picks
    even = jnp.where(at_even, shifted(edges[0], 0, 2 * r), pick_lanes(values, even_lanes))
    odd = jnp.where(at_odd, shifted(edges[1], 0, 2 * r), pick_lanes(values, even_lanes + 1))
    return even, odd


def split_couplings(block, lanes):
    picks = lane_picks(lanes)
    c = [[[[None, None], [None, None]] for _ in range(4)] for _ in range(3)]
    for px in range(2):
        edges = columns_beside(block[12, pl.ds(px, 8, stride=2), :], lanes)
        for r in range(12):
            values = block[r, pl.ds(px, 8, stride=2), :]
            c[r // 4][r % 4][px][:] = split_lanes(values, r, edges, picks)
    return c


def places():
    rows = lax.broadcasted_iota(jnp.int32, (ROWS, LANES), 0)
    lanes = lax.broadcasted_iota(jnp.int32, (ROWS, LANES), 1)
    last_x = lax.axis_index("gx") == lax.axis_size("gx") - 1
    last_y = lax.axis_index("gy") == lax.axis_size("gy") - 1
    return rows, lanes, last_x, last_y


def operators(block, first_ref, second_ref, hold_row=None):
    rows, lanes, last_x, last_y = places()
    hold = None if hold_row is None else rows == hold_row
    c = split_couplings(block, lanes)
    operator, chain, factors = first_operator(c, edge_masks(last_x, last_y, rows, lanes, 1), hold)
    empty = jnp.zeros((ROWS, LANES), jnp.float32)
    full = {}
    for o in range(27):
        offset = (o // 9 - 1, o // 3 % 3 - 1, o % 3 - 1)
        for z in range(2):
            full[offset, z] = operator.get((offset, z), empty)
            first_ref[o // 9, o % 9, z] = full[offset, z][0:4, 0:64]
    results, own = second_operator(full, chain, rows, lanes, hold)
    masks = edge_masks(last_x, last_y, rows, lanes, 2)
    second_ref[...] = jnp.zeros(second_ref.shape, jnp.float32)
    for (ox, oy), values in results.items():
        compact = pick_lanes(dropped(values, ox, oy, masks), (2 * lanes) % LANES)
        second_ref[9 + (ox + 1) * 3 + oy + 1, 0, 0:1, :] = compact[0:1, 0:32]
        second_ref[9 + (ox + 1) * 3 + oy + 1, 0, 1:2, :] = compact[2:3, 0:32]
    return operator, factors, own


fix_entries = [((oz, 1, oy), z) for z in (0, 1) for oz in (-z, 1 - z) for oy in (-1, 0, 1)]
fix_factors = [
    (zc, qz, qy, (tz, 0, ty))
    for zc in (0, 1)
    for qz in (0, 1)
    for qy in (0, 1)
    if qz or qy
    for tz in range(1 + (qz if zc == 0 else 0))
    for ty in range(1 + qy)
]
fix_sides = [(z, 1, my) for z in (0, 1) for my in (-1, 0, 1)]
fix_count = len(fix_entries) + len(fix_factors) + len(fix_sides)


def early_kernel(
    own_ref, first_columns_ref, second_columns_ref, third_columns_ref, far_ref,
    first_ref, second_ref, kept_ref, block,
):
    tiles = [own_ref[r] for r in range(12)] + beside((first_columns_ref, second_columns_ref, third_columns_ref))
    for r, values in enumerate(tiles):
        block[r, 0:8, :] = values
        block[r, 8:12, :] = jnp.zeros((4, LANES), jnp.float32)
        block[r, 12:16, :] = far_ref[r]
    operator, factors, own = operators(block, first_ref, second_ref, ROWS // 2 - 1)
    kept = [operator[e] for e in fix_entries] + [factors[e] for e in fix_factors]
    kept += [own[e] for e in fix_sides]
    for i, values in enumerate(kept):
        kept_ref[i] = values


def add_row_above(near_ref, early_second_ref, kept_ref, first_ref, second_ref, send_first):
    rows, lanes, last_x, last_y = places()
    kept = {e: kept_ref[i] for i, e in enumerate(fix_entries + fix_factors + fix_sides)}

    def row(r):
        return jnp.broadcast_to(near_ref[r, 0:1, :], (ROWS, LANES))

    even_lanes, at_even, at_odd = lane_picks(lanes)
    tile = row(12)
    first = 1 + 2 * (lanes % 2)
    c = {}
    for d in (0, 2):
        for z in range(4):
            r = d * 4 + z
            values = row(r)
            even = pick_lanes(tile, jnp.where(at_odd, first, 5) + 5 * r)
            odd = pick_lanes(tile, first + (5 * r + 1))
            even = jnp.where(at_even, even, pick_lanes(values, even_lanes))
            c[d, z] = (even, jnp.where(at_odd, odd, pick_lanes(values, even_lanes + 1)))
    line_y = {z: line_terms(*c[2, z]) for z in range(4)}
    line_z = {(zc, py): line_terms(c[0, 2 * zc][py], c[0, 2 * zc + 1][py]) for zc in range(2) for py in range(2)}

    near_y = {(far, j): shifted(line_y[2 * far][2], 0, j) for far in range(2) for j in (-2, -1, 0, 1)}
    near_z = {(z, j): shifted(line_z[z, 0][2], 0, j) for z in range(2) for j in (-1, 0, 1)}
    odd = lanes % 2 == 1
    weights = {}
    for far in range(2):
        for oy in (-1, 0, 1):
            f, g = line_terms(near_y[far, oy - 1], near_y[far, oy])[:2]
            there = odd if oy == 0 else ~odd
            pair = jnp.where(there, f, 1.0), jnp.where(there, g, 1.0)
            if far == 1:
                depth = line_terms(near_z[0, oy], near_z[1, oy])[0]
                pair = pair[0] * depth, pair[1] * depth
            for jy, o in reaches:
                if o == oy:
                    weights[far, jy, oy] = reaching(jy, oy, pair[0 if from_below(jy, oy) else 1], odd)

    sums = {}
    for zc, qz, qy, t in fix_factors:
        pair_z = line_z[zc, qy][:2] if qz else (None,)
        pair_y = line_y[2 * zc + qz][:2] if qy else (None,)
        for uz in range(1 + (qz if zc == 0 else 0)):
            for uy in range(1 + qy):
                key = ((uz - t[0], 1, uy - t[2]), zc + t[0], t[2])
                term = kept[zc, qz, qy, t] * times(pair_z[uz], pair_y[uy])
                sums[key] = sums[key] + term if key in sums else term
    masks = edge_masks(last_x, last_y, rows, lanes, 1)
    entries = {}
    for offset, z in fix_entries:
        total = kept[offset, z]
        if (offset, z, 0) in sums:
            total = total - sums[offset, z, 0]
        if (offset, z, 1) in sums:
            total = total - shifted(sums[offset, z, 1], 0, -1)
        entries[offset, z] = dropped(total, *offset[1:], masks)
        whole = jnp.where(rows == ROWS // 2 - 1, entries[offset, z], kept[offset, z])
        first_ref[offset[0] + 1, offset[2] + 1, z] = whole[0:4, 0:64]
    for oz, z in ((0, 0), (2, 1)):
        for oy in range(3):
            first_ref[oz, oy, z] = jnp.zeros((4, 64), jnp.float32)
    send_first()

    spread = {}
    for far in range(2):
        for jy, oy in reaches:
            for z in range(2):
                term = entries[(far - z, 1, oy), z] * weights[far, jy, oy]
                spread[z, jy] = spread[z, jy] + term if (z, jy) in spread else term
    for oy in (-1, 0, 1):
        total = None
        for my, jy in taken(oy):
            part = kept[0, 1, my] * spread[0, jy] + kept[1, 1, my] * spread[1, jy]
            part = pick_lanes(part, (2 * lanes + my) % LANES)
            total = part if total is None else total + part
        total = jnp.where(last_x, 0.0, total)
        if oy == 1:
            total = jnp.where((lanes == LANES // 4 - 1) & last_y, 0.0, total)
        second_ref[oy + 1, 0, 0:1, :] = early_second_ref[16 + oy, 0, 0:1, :]
        row_two = early_second_ref[16 + oy, 0, 1:2, :]
        second_ref[oy + 1, 0, 1:2, :] = row_two + total[ROWS // 2 - 1:ROWS // 2, 0:32]


def last_kernel(
    own_ref, first_columns_ref, second_columns_ref, third_columns_ref, far_ref,
    early_first_ref, early_second_ref, kept_ref, near_ref,
    first_hbm, second_hbm, block, first_ref, second_ref, first_fix, second_fix, sems,
):
    odd_x = lax.axis_index("gx") % 2 == 1

    def send(parts):
        copies = [pltpu.make_async_copy(source, target, sems.at[i]) for i, source, target in parts]
        for copy in copies:
            copy.start()
        return copies

    @pl.when(odd_x)
    def _():
        tiles = [own_ref[r] for r in range(12)] + beside((first_columns_ref, second_columns_ref, third_columns_ref))
        for r, values in enumerate(tiles):
            block[r, 0:8, :] = values
            block[r, 8:12, :] = far_ref[r]
            block[r, 12:16, :] = near_ref[r]
        operators(block, first_ref, second_ref)
        for copy in send([(0, first_ref, first_hbm), (1, second_ref, second_hbm)]):
            copy.wait()

    @pl.when(jnp.logical_not(odd_x))
    def _():
        copies = []

        def send_first():
            copies.extend(send([
                (0, first_fix, first_hbm.at[:, pl.ds(6, 3)]),
                (1, early_first_ref.at[:, pl.ds(0, 6)], first_hbm.at[:, pl.ds(0, 6)]),
                (2, early_second_ref.at[pl.ds(0, 15)], second_hbm.at[pl.ds(0, 15)]),
                (3, early_second_ref.at[pl.ds(18, 9)], second_hbm.at[pl.ds(18, 9)]),
            ]))

        add_row_above(near_ref, early_second_ref, kept_ref, first_fix, second_fix, send_first)
        for copy in copies + send([(4, second_fix, second_hbm.at[pl.ds(15, 3)])]):
            copy.wait()


def swapped(values, axis, first):
    pairs = [(i, i + 1) for i in range(first, lax.axis_size(axis) - 1, 2)]
    return lax.ppermute(values, axis, pairs + [(b, a) for a, b in pairs])


def swapped_columns(values, which):
    count_x, count_y = lax.axis_size("gx"), lax.axis_size("gy")
    pairs = [
        (row * count_y + edge, row * count_y + edge + 1)
        for row in range(count_x)
        for edge in range(count_y - 1)
        if swap_order(row, edge, count_y // 2, np.where) == which
    ]
    return lax.ppermute(values, ("gx", "gy"), pairs + [(b, a) for a, b in pairs])


def body(material, face_open):
    whole = pl.BlockSpec(memory_space=pltpu.VMEM)
    page = jax.ShapeDtypeStruct((ROWS, LANES), jnp.float32)
    edge = jax.ShapeDtypeStruct((13, 4, LANES), jnp.float32)
    small = pltpu.CompilerParams(vmem_limit_bytes=1 << 20)
    own, *pages = pl.pallas_call(
        couplings_kernel,
        out_shape=(jax.ShapeDtypeStruct((12, ROWS, LANES), jnp.float32),) + (page,) * 3,
        in_specs=[whole],
        out_specs=(whole,) * 4,
        compiler_params=small,
        name="couplings",
    )(face_open * 4 + material[None])
    columns = [swapped_columns(values, k) for k, values in enumerate(pages)]
    far, near = pl.pallas_call(
        edges_kernel,
        out_shape=(edge, edge),
        in_specs=[whole] * 4,
        out_specs=(whole,) * 2,
        compiler_params=small,
        name="edges",
    )(own, *columns)
    far_rows = swapped(far, "gx", 1)
    near_rows = swapped(near, "gx", 0)
    first = jax.ShapeDtypeStruct((3, 9, 2, 4, 64), jnp.float32)
    second = jax.ShapeDtypeStruct((27, 1, 2, 32), jnp.float32)
    large = pltpu.CompilerParams(vmem_limit_bytes=3 << 20)
    block = pltpu.VMEM((13, 24, LANES), jnp.float32)
    early = pl.pallas_call(
        early_kernel,
        out_shape=(first, second, jax.ShapeDtypeStruct((fix_count, ROWS, LANES), jnp.float32)),
        in_specs=[whole] * 5,
        out_specs=(whole,) * 3,
        scratch_shapes=[block],
        compiler_params=large,
        cost_estimate=pl.CostEstimate(flops=3 << 20, bytes_accessed=1 << 20, transcendentals=0),
        name="early",
    )(own, *columns, far_rows)
    first_level, second_level = pl.pallas_call(
        last_kernel,
        out_shape=(first, second),
        in_specs=[whole] * 9,
        out_specs=(pl.BlockSpec(memory_space=pltpu.HBM),) * 2,
        scratch_shapes=[
            block,
            pltpu.VMEM(first.shape, jnp.float32),
            pltpu.VMEM(second.shape, jnp.float32),
            pltpu.VMEM((3, 3, 2, 4, 64), jnp.float32),
            pltpu.VMEM((3, 1, 2, 32), jnp.float32),
            pltpu.SemaphoreType.DMA((5,)),
        ],
        compiler_params=large,
        name="last",
    )(own, *columns, far_rows, *early, near_rows)
    return first_level.reshape(27, 2, 4, 64), second_level


def solution(mesh):
    placed = (P(None, "gx", "gy"), P(None, None, "gx", "gy"))
    return jax.shard_map(
        body,
        mesh=mesh,
        in_specs=placed,
        out_specs=(P(None, None, "gx", "gy"), P(None, None, "gx", "gy")),
        check_vma=False,
    )
```
